32 devices in a mesh: fsdp: 8 (over y, x, core), dp: 4 (over z).
Axes of the slice: x: 2, y: 2, z: 4, core: 2. Of those that a mesh axis runs over, the one named last changes fastest.
Arguments:
- enc_input: bfloat16 [64, 512, 512], P(('fsdp', 'dp')), may hold values from -6 to 6
- segments: int32 [64, 512], P(('fsdp', 'dp')), may hold values from 0 to 3, never falling along the last dimension, each value on 1 to 256 neighbouring positions
- targets: int32 [64, 64], P(('fsdp', 'dp')), may hold values from 0 to 4095
- enc_cot: bfloat16 [64, 512, 512], P(('fsdp', 'dp')), may hold values from -6 to 6
- dec_cot: bfloat16 [64, 64, 512], P(('fsdp', 'dp')), may hold values from -6 to 6
- enc_gains: bfloat16 [2, 512], P(None, 'fsdp'), may hold values from 0.5 to 1.5
- enc_attn: bfloat16 [4, 512, 512], P(None, 'fsdp'), may hold values from -0.375 to 0.375
- enc_table: bfloat16 [256], P('fsdp'), may hold values from -4 to 4
- enc_up: bfloat16 [512, 2048], P('fsdp'), may hold values from -0.25 to 0.25
- enc_down: bfloat16 [2048, 512], P('fsdp'), may hold values from -0.125 to 0.125
- embed: bfloat16 [4096, 512], P('fsdp'), may hold values from -6 to 6
- dec_gains: bfloat16 [3, 512], P(None, 'fsdp'), may hold values from 0.5 to 1.5
- dec_self: bfloat16 [4, 512, 512], P(None, 'fsdp'), may hold values from -0.375 to 0.375
- dec_cross: bfloat16 [4, 512, 512], P(None, 'fsdp'), may hold values from -0.375 to 0.375
- dec_table: bfloat16 [256], P('fsdp'), may hold values from -4 to 4
- dec_up: bfloat16 [512, 2048], P('fsdp'), may hold values from -0.25 to 0.25
- dec_down: bfloat16 [2048, 512], P('fsdp'), may hold values from -0.125 to 0.125
Outputs:
- enc_out: bfloat16 [64, 512, 512], P(('fsdp', 'dp'))
- dec_out: bfloat16 [64, 64, 512], P(('fsdp', 'dp'))
- grad_input: float32 [64, 512, 512], P(('fsdp', 'dp'))
- grad_memory: float32 [64, 512, 512], P(('fsdp', 'dp'))
- grad_enc_gains: float32 [2, 512], P(None, 'fsdp')
- grad_enc_attn: float32 [4, 512, 512], P(None, 'fsdp')
- grad_enc_table: float32 [256], P('fsdp')
- grad_enc_up: float32 [512, 2048], P('fsdp')
- grad_enc_down: float32 [2048, 512], P('fsdp')
- grad_embed: float32 [4096, 512], P('fsdp')
- grad_dec_gains: float32 [3, 512], P(None, 'fsdp')
- grad_dec_self: float32 [4, 512, 512], P(None, 'fsdp')
- grad_dec_cross: float32 [4, 512, 512], P(None, 'fsdp')
- grad_dec_table: float32 [256], P('fsdp')
- grad_dec_up: float32 [512, 2048], P('fsdp')
- grad_dec_down: float32 [2048, 512], P('fsdp')
The draws below stay inside these ranges and needn't reach their ends.
Inputs may be any that keep to these rules, and one draw needn't show every extreme that they name: `segments`: along each row the series numbers never fall; each series holds 1 to 256 positions, and some series holds exactly 256.
All inputs are finite; a program needn't handle non-finite values.
Results may differ from the reference program's by a relative error of at most 0.028.
The reference program's roundings to bfloat16 on the way count: a program that leaves them out, or rounds other values in their place, can miss the bound.
Values may be sent and summed in bfloat16 or wider, within the bound.
No kernel may reach another device: no remote copies, remote signals or barrier semaphores. Data moves between devices by JAX's collectives and lax.ppermute only.
A program may use at most 256 MiB of HBM per device.

```python
import math
import jax
import jax.numpy as jnp
import numpy as np
from jax import lax

D = 512
HEADS = 8
HEAD_DIM = 64
FF = 2048
VOCAB = 4096
BUCKETS = 32
LEN = 512
STEPS = 64
SERIES = 4
SERIES_MOST = 256
MICRO = 2
ROWS_MB = 1
ROWS = 64


def stacked_projections(key):
    spread = jnp.array([(4.0 * D) ** (-0.5), (4.0 * D) ** (-0.5), float(D) ** (-0.5), (D / 8.0) ** (-0.5)], jnp.float32)
    samples = jax.random.truncated_normal(key, -3.0, 3.0, (4, D, D), jnp.float32)
    return jnp.clip(samples * spread[:, None, None], -0.375, 0.375).astype(jnp.bfloat16)


def draw_enc_attn(key, part):
    key = jax.random.fold_in(key, 11)
    return stacked_projections(key)


def draw_dec_self(key, part):
    key = jax.random.fold_in(key, 23)
    return stacked_projections(key)


def draw_dec_cross(key, part):
    key = jax.random.fold_in(key, 37)
    return stacked_projections(key)


def touch_ends(values, rng, smallest, high):
    spot = [jax.random.randint(jax.random.fold_in(rng, axis), (), 0, length) for axis, length in enumerate(values.shape)]
    longest = values.shape.index(max(values.shape))
    beside = spot[:longest] + [(spot[longest] + 1) % values.shape[longest]] + spot[longest + 1:]
    return values.at[tuple(spot)].set(smallest).at[tuple(beside)].set(high)


def levels(key, extent, cuts, least, top_value):
    level = 1.0
    for dim, parts in cuts:
        draws = jax.random.uniform(jax.random.fold_in(jax.random.fold_in(key, 6), dim), (parts,), jnp.float32, least / len(cuts), top_value / len(cuts))
        level = level * jnp.repeat(jnp.exp(draws), extent[dim] // parts).reshape((-1,) + (1,) * (len(extent) - 1 - dim))
    return level


def length_profile(count, total, most, slope):
    weights = [(1 << 20) // math.isqrt(rank ** slope) + 1 for rank in range(2, count + 1)]
    surplus, counts = total - most - (count - 1), [1] * (count - 1)
    while surplus > 0:
        candidates = [i for i in range(count - 1) if counts[i] < most]
        pool, remaining = sum([weights[i] for i in candidates]), surplus
        for i in candidates:
            extra = min(most - counts[i], max(1, remaining * weights[i] // pool), surplus)
            counts[i] = counts[i] + extra
            surplus = surplus - extra
    return np.array([most] + counts)


def uneven_parts(rng, count, total, reach, lean):
    if count == 2:
        one = jax.random.randint(rng, (), max(1, total - reach), min(reach, total - 1) + 1)
        return jnp.stack([one, total - one])
    tallies = jnp.asarray(length_profile(count, total, reach, lean), jnp.int32)
    pairs = (count - 1) // 2
    giver, receiver = tallies[1:1 + 2 * pairs:2], tallies[2:2 + 2 * pairs:2]
    room = jnp.minimum(giver - 1, reach - receiver)
    moved = jax.random.randint(jax.random.fold_in(rng, 1), (pairs,), 0, 1 << 20) % (room + 1)
    tallies = tallies.at[1:1 + 2 * pairs:2].set(giver - moved).at[2:2 + 2 * pairs:2].set(receiver + moved)
    return tallies[jax.random.permutation(jax.random.fold_in(rng, 2), count)]


def noise(rng, dims, deviation, limit, pieces=(), kind=jnp.bfloat16):
    drawn = deviation * jax.random.normal(rng, dims, jnp.float32)
    if pieces:
        drawn = drawn * levels(rng, dims, pieces, -0.22, 0.18)
    return jnp.clip(drawn, -limit, limit).astype(kind)


def setup_inputs(seed: int = 0) -> dict:
    streams_of = jax.random.split(jax.random.key(seed), 18)
    return {
        "enc_input": noise(streams_of[0], (ROWS, LEN, D), 1.0, 6.0, ((0, 32),)),
        "segments": jax.vmap(lambda own: jnp.searchsorted(jnp.cumsum(uneven_parts(own, SERIES, LEN, SERIES_MOST, 0)), jnp.arange(LEN), side="right"))(jax.random.split(streams_of[1], ROWS)).reshape((ROWS, LEN)).astype(jnp.int32),
        "targets": touch_ends(jax.random.randint(streams_of[2], (ROWS, STEPS), 0, VOCAB), jax.random.fold_in(streams_of[2], 1), 0, VOCAB - 1).astype(jnp.int32),
        "enc_cot": noise(streams_of[3], (ROWS, LEN, D), 1.0, 6.0, ((0, 32),)),
        "dec_cot": noise(streams_of[4], (ROWS, STEPS, D), 1.0, 6.0, ((0, 32),)),
        "enc_gains": jnp.clip(1.0 + 0.1 * jax.random.normal(streams_of[5], (2, D), jnp.float32), 0.5, 1.5).astype(jnp.bfloat16),
        "enc_attn": draw_enc_attn(jax.random.fold_in(streams_of[17], 71), 0),
        "enc_table": noise(streams_of[7], (HEADS * BUCKETS,), 1.0, 4.0, ((0, 8),)),
        "enc_up": noise(streams_of[8], (D, FF), D ** -0.5, 0.25, ((0, 8),)),
        "enc_down": noise(streams_of[9], (FF, D), FF ** -0.5, 0.125, ((0, 8),)),
        "embed": noise(streams_of[10], (VOCAB, D), 1.0, 6.0, ((0, 8),)),
        "dec_gains": jnp.clip(1.0 + 0.1 * jax.random.normal(streams_of[11], (3, D), jnp.float32), 0.5, 1.5).astype(jnp.bfloat16),
        "dec_self": draw_dec_self(jax.random.fold_in(streams_of[17], 71), 0),
        "dec_cross": draw_dec_cross(jax.random.fold_in(streams_of[17], 71), 0),
        "dec_table": noise(streams_of[14], (HEADS * BUCKETS,), 1.0, 4.0, ((0, 8),)),
        "dec_up": noise(streams_of[15], (D, FF), D ** -0.5, 0.25, ((0, 8),)),
        "dec_down": noise(streams_of[16], (FF, D), FF ** -0.5, 0.125, ((0, 8),)),
    }


epsilon = 1e-06
highest = lax.Precision.HIGHEST

@jax.custom_vjp
def low(v):
    return lax.optimization_barrier(v.astype(jnp.bfloat16)).astype(jnp.float32)

@jax.custom_vjp
def low_back(v):
    return v

def low_keep(v):
    return (low(v), None)

def low_pass(kept, grad):
    return (grad,)

def back_keep(v):
    return (v, None)

def back_low(kept, grad):
    return (low(grad),)
low.defvjp(low_keep, low_pass)
low_back.defvjp(back_keep, back_low)

def low_both(tensor):
    return low_back(low(tensor))

def bucket_codes(length, both_ways):
    bucket_list = []
    for offset in range(-(length - 1), length):
        if both_ways:
            upper_half = 16 if offset > 0 else 0
            distance = abs(offset)
            if distance < 8:
                bucket = distance
            else:
                bucket = 8 + sum((1 for exponent in range(1, 8) if distance * distance >= 64 * 2 ** exponent))
        else:
            upper_half = 0
            distance = max(-offset, 0)
            if distance < 16:
                bucket = distance
            else:
                bucket = 16 + sum((1 for exponent in range(1, 16) if distance ** 16 >= 16 ** 16 * 2 ** (3 * exponent)))
        bucket_list.append(upper_half + bucket)
    return np.array(bucket_list, dtype=np.int32)

def position_bias(bias_table, length, both_ways):
    buckets = bucket_codes(length, both_ways)
    places = np.arange(length)
    lookup = buckets[length - 1 + places[None, :] - places[:, None]]
    return bias_table.reshape(HEADS, BUCKETS)[:, lookup]

def product(left_side, right_side):
    return jnp.matmul(left_side, right_side, precision=highest)

def normalize(tensor, scales):
    return tensor * lax.rsqrt(lax.optimization_barrier(jnp.mean(tensor * tensor, axis=-1, keepdims=True)) + epsilon) * scales

def split_heads(tensor):
    return tensor.reshape(tensor.shape[0], tensor.shape[1], HEADS, HEAD_DIM)

def attention(queries, keyset, values, position, allowed):
    scores = jnp.einsum('bqhd,bkhd->bhqk', split_heads(queries), split_heads(keyset), precision=highest) + position
    scores = low_back(jnp.where(allowed[:, None], scores, -1000000000.0))
    weights = low(jax.nn.softmax(scores, axis=-1))
    blended = jnp.einsum('bhqk,bkhd->bqhd', weights, split_heads(values), precision=highest)
    return low_both(blended.reshape(queries.shape))

def feed_forward(hidden, scales, up_weights, down_weights):
    normalized_state = low(normalize(hidden, scales))
    active = low(jax.nn.gelu(low_back(product(normalized_state, up_weights))))
    return hidden + low_back(product(active, down_weights))

def encoder(inputs, segment, gain_rows, projection_weights, bias_table, up_weights, down_weights):
    position = position_bias(bias_table, LEN, True)[None]
    normalized_state = low(normalize(inputs, gain_rows[0]))
    queries = low_both(product(normalized_state, projection_weights[0]))
    keyset = low_both(product(normalized_state, projection_weights[1]))
    values = low_both(product(normalized_state, projection_weights[2]))
    allowed = segment[:, :, None] == segment[:, None, :]
    hidden = inputs + low_back(product(attention(queries, keyset, values, position, allowed), projection_weights[3]))
    return feed_forward(hidden, gain_rows[1], up_weights, down_weights)

def decoder(embedded, encoder_memory, segment, gain_rows, self_projection_weight, cross_projection_weight, bias_table, up_weights, down_weights):
    row_count = embedded.shape[0]
    position = position_bias(bias_table, STEPS, False)[None]
    places = jnp.arange(STEPS)
    causal = jnp.broadcast_to(places[None, :, None] >= places[None, None, :], (row_count, STEPS, STEPS))
    normalized_state = low(normalize(embedded, gain_rows[0]))
    queries = low_both(product(normalized_state, self_projection_weight[0]))
    keyset = low_both(product(normalized_state, self_projection_weight[1]))
    values = low_both(product(normalized_state, self_projection_weight[2]))
    hidden = embedded + low_back(product(attention(queries, keyset, values, position, causal), self_projection_weight[3]))
    normalized_state = low(normalize(hidden, gain_rows[1]))
    queries = low_both(product(normalized_state, cross_projection_weight[0]))
    source = low(encoder_memory)
    keyset = low_both(product(source, cross_projection_weight[1]))
    values = low_both(product(source, cross_projection_weight[2]))
    allowed = jnp.broadcast_to((segment == segment[:, -1:])[:, None, :], (row_count, STEPS, LEN))
    hidden = hidden + low_back(product(attention(queries, keyset, values, 0.0, allowed), cross_projection_weight[3]))
    return feed_forward(hidden, gain_rows[2], up_weights, down_weights)

def reference(enc_input, segments, targets, enc_cot, dec_cot, enc_gains, enc_attn, enc_table, enc_up, enc_down, embed, dec_gains, dec_self, dec_cross, dec_table, dec_up, dec_down):
    per_step = MICRO * ROWS_MB
    step_count = ROWS // per_step

    def grouped(tensor):
        return tensor.reshape((step_count, per_step) + tensor.shape[1:])
    inputs = grouped(enc_input.astype(jnp.float32))
    no_shift = jnp.zeros_like(inputs)
    segment_groups = grouped(segments)
    target_groups = grouped(targets)
    weights = tuple((matrix.astype(jnp.float32) for matrix in (enc_gains, enc_attn, enc_table, enc_up, enc_down, embed, dec_gains, dec_self, dec_cross, dec_table, dec_up, dec_down)))

    def forward(inputs, no_shift, enc_gains, enc_attn, enc_table, enc_up, enc_down, embed, dec_gains, dec_self, dec_cross, dec_table, dec_up, dec_down):

        def one_step(unused, row_group):
            enc_rows, memory_shift, segment, target = row_group
            encoder_memory = encoder(enc_rows, segment, enc_gains, enc_attn, enc_table, enc_up, enc_down)
            shifted = jnp.concatenate([jnp.zeros((per_step, 1), jnp.int32), target[:, :-1].astype(jnp.int32)], axis=1)
            embedded = low_back(embed[shifted])
            result = decoder(embedded, encoder_memory + memory_shift, segment, dec_gains, dec_self, dec_cross, dec_table, dec_up, dec_down)
            return (unused, (encoder_memory, result))
        _, (memories, results) = lax.scan(jax.checkpoint(one_step), None, (inputs, no_shift, segment_groups, target_groups))
        return (memories, results)
    outputs, pullback = jax.vjp(forward, inputs, no_shift, *weights)
    gradients = pullback((grouped(enc_cot.astype(jnp.float32)), grouped(dec_cot.astype(jnp.float32))))
    enc_out = outputs[0].reshape(ROWS, LEN, D).astype(jnp.bfloat16)
    dec_out = outputs[1].reshape(ROWS, STEPS, D).astype(jnp.bfloat16)
    grad_input = gradients[0].reshape(ROWS, LEN, D)
    grad_memory = enc_cot.astype(jnp.float32) + gradients[1].reshape(ROWS, LEN, D)
    return (enc_out, dec_out, grad_input, grad_memory, gradients[2], gradients[3], gradients[4], gradients[5], gradients[6], gradients[7], gradients[8], gradients[9], gradients[10], gradients[11], gradients[12], gradients[13])
```

```python
import functools

import jax
import jax.numpy as jnp
import numpy as np
from jax import lax
from jax.experimental import pallas as pl
from jax.experimental.pallas import tpu as pltpu
from jax.sharding import PartitionSpec as P

HEADS = 8
HEAD_DIM = 64
BUCKETS = 32
SERIES_MOST = 256
TILE = 128
MASKED = -1000000000.0

epsilon = 1e-06
f32 = jnp.float32
bf16 = jnp.bfloat16
PARAMS = pltpu.CompilerParams(vmem_limit_bytes=56 * 2**20)


def bucket_codes(length, both_ways):
    bucket_list = []
    for offset in range(-(length - 1), length):
        if both_ways:
            upper_half = 16 if offset > 0 else 0
            distance = abs(offset)
            if distance < 8:
                bucket = distance
            else:
                bucket = 8 + sum(
                    (1 for exponent in range(1, 8) if distance * distance >= 64 * 2**exponent)
                )
        else:
            upper_half = 0
            distance = max(-offset, 0)
            if distance < 16:
                bucket = distance
            else:
                bucket = 16 + sum(
                    (1 for exponent in range(1, 16) if distance**16 >= 16**16 * 2 ** (3 * exponent))
                )
        bucket_list.append(upper_half + bucket)
    return np.array(bucket_list, dtype=np.int32)


def offset_hot(length, both_ways, reverse):
    codes = np.concatenate([bucket_codes(length, both_ways), [-1]])
    if reverse:
        codes = codes[::-1]
    return jnp.asarray(codes[None, :] == np.arange(BUCKETS)[:, None], bf16)


def nn(a, b):
    return lax.dot_general(a, b, (((1,), (0,)), ((), ())), preferred_element_type=f32)


def nt(a, b):
    return lax.dot_general(a, b, (((1,), (1,)), ((), ())), preferred_element_type=f32)


def tn(a, b):
    return lax.dot_general(a, b, (((0,), (0,)), ((), ())), preferred_element_type=f32)


def rho_of(h):
    return lax.rsqrt(jnp.mean(h * h, axis=-1, keepdims=True) + epsilon)


def normed(h, gain):
    return (h * rho_of(h) * gain.astype(f32)).astype(bf16)


def norm_back(h, gain, dn):
    rho = rho_of(h)
    xh = h * rho
    gu = dn * gain.astype(f32)
    dh = rho * (gu - xh * jnp.mean(gu * xh, axis=-1, keepdims=True))
    return dh, jnp.sum(dn * xh, axis=0, keepdims=True)


def gelu(u):
    t = jnp.tanh(np.float32(np.sqrt(2 / np.pi)) * (u + 0.044715 * (u * u * u)))
    return 0.5 * u * (1.0 + t)


def gelu_both(u):
    c = np.float32(np.sqrt(2 / np.pi))
    u2 = u * u
    t = jnp.tanh(c * (u + 0.044715 * (u2 * u)))
    cdf = 0.5 * (1.0 + t)
    return u * cdf, cdf + 0.5 * u * (1.0 - t * t) * (c + (3 * 0.044715 * c) * u2)


def matrix(ref, w):
    part = ref[:, w]
    return part.reshape(part.shape[0] * part.shape[1], part.shape[2])


def packed(value, shards):
    return value.reshape(shards, value.shape[0] // shards, value.shape[1]).astype(bf16)


def half(lane, value, which):
    return jnp.where((lane // HEAD_DIM) == which, value, jnp.zeros_like(value))


def fill_strip(strip_ref, table, hot, shift):
    vec = nn(table, hot)
    width = hot.shape[1]
    rows = strip_ref.shape[1]
    for h in range(HEADS):
        row = jnp.broadcast_to(vec[h : h + 1], (rows, width))
        strip_ref[h] = pltpu.roll(row, (width + shift) % width, 1, stride=1, stride_axis=0)


def strip_sums(acc, hot):
    rows, width = acc.shape[1], acc.shape[2]
    total = jnp.zeros((HEADS, 8, width), f32)
    for g in range(rows // 8):
        part = acc[:, g * 8 : g * 8 + 8, :].reshape(HEADS * 8, width)
        if g:
            part = pltpu.roll(part, width - 8 * g, 1)
        total = total + part.reshape(HEADS, 8, width)
    flat = total.reshape(HEADS * 8, width)
    sub = lax.broadcasted_iota(jnp.int32, flat.shape, 0) % 8
    for b in range(3):
        flat = jnp.where((sub >> b) & 1 == 1, pltpu.roll(flat, width - (1 << b), 1), flat)
    diag = pltpu.roll(jnp.sum(flat.reshape(HEADS, 8, width), axis=1), rows, 1)
    return lax.dot_general(
        diag,
        hot.astype(f32),
        (((1,), (1,)), ((), ())),
        precision=lax.Precision.HIGHEST,
        preferred_element_type=f32,
    )


def soft_rows(s):
    e = jnp.exp(s - jnp.max(s, axis=-1, keepdims=True))
    return e * (1.0 / jnp.sum(e, axis=-1, keepdims=True))


def soft_columns(s):
    e = jnp.exp(s - jnp.max(s, axis=0, keepdims=True))
    return e * (1.0 / jnp.sum(e, axis=0, keepdims=True))


def enc_attn_fwd_kernel(
    x_ref, segc_ref, segr_ref, g_ref, w_ref, table_ref, hot_ref, hid_ref, q_ref, k_ref, v_ref, mix_ref, strip_ref
):
    length = x_ref.shape[1]
    blocks = length // TILE

    @pl.when(pl.program_id(0) == 0)
    def _():
        fill_strip(strip_ref, table_ref[...], hot_ref[...], 1 - TILE)

    x = x_ref[0].astype(f32)
    n = normed(x, g_ref[...])
    q_ref[0] = nn(n, matrix(w_ref, 0)).astype(bf16)
    k_ref[0] = nn(n, matrix(w_ref, 1)).astype(bf16)
    v_ref[0] = nn(n, matrix(w_ref, 2)).astype(bf16)
    lane = lax.broadcasted_iota(jnp.int32, (length, 2 * HEAD_DIM), 1)
    same = segc_ref[0] == segr_ref[0]
    for hp in range(HEADS // 2):
        ls = slice(hp * 2 * HEAD_DIM, (hp + 1) * 2 * HEAD_DIM)
        qp, kp, vp = q_ref[0, :, ls], k_ref[0, :, ls], v_ref[0, :, ls]
        outs = []
        for sub in range(2):
            s = nt(half(lane, qp, sub), kp)
            starts = [(blocks - 1 - b) * TILE for b in range(blocks)]
            bias = [strip_ref[hp * 2 + sub, :, c : c + length] for c in starts]
            s = jnp.where(same, s + jnp.concatenate(bias, axis=0), MASKED)
            outs.append(nn(soft_rows(s).astype(bf16), vp))
        mix_ref[0, :, ls] = jnp.where(lane < HEAD_DIM, outs[0], outs[1]).astype(bf16)
    hid_ref[0] = x + nn(mix_ref[0], matrix(w_ref, 3))


def enc_attn_fwd(x, segments, gain, weights, table):
    rows, length, width = x.shape
    hot = offset_hot(length, True, False)
    row = lambda r: (r, 0, 0)
    full = lambda r: (0, 0)
    sds = jax.ShapeDtypeStruct
    return pl.pallas_call(
        enc_attn_fwd_kernel,
        grid=(rows,),
        in_specs=[
            pl.BlockSpec((1, length, width), row),
            pl.BlockSpec((1, length, 1), row),
            pl.BlockSpec((1, 1, length), row),
            pl.BlockSpec((1, width), full),
            pl.BlockSpec(weights.shape, lambda r: (0, 0, 0, 0)),
            pl.BlockSpec(table.shape, full),
            pl.BlockSpec(hot.shape, full),
        ],
        out_specs=[pl.BlockSpec((1, length, width), row)] * 5,
        out_shape=[sds(x.shape, f32)] + [sds(x.shape, bf16)] * 4,
        scratch_shapes=[pltpu.VMEM((HEADS, TILE, 2 * length), f32)],
        compiler_params=PARAMS,
        name="enc_attn_fwd",
    )(x, segments[:, :, None], segments[:, None, :], gain, weights, table, hot)


def ffn_fwd_kernel(h_ref, g_ref, w_ref, o_ref, *, cols):
    h = h_ref[...]
    n = normed(h, g_ref[...])
    out = h
    per = w_ref.shape[0] // cols
    for b in range(cols):
        a = gelu(nn(n, matrix(w_ref, b))).astype(bf16)
        down = w_ref[b * per : (b + 1) * per, cols:]
        out = out + nn(a, down.reshape(-1, down.shape[-1]))
    o_ref[...] = out.astype(bf16)


def ffn_fwd(h, gain, weights, tokens=512):
    total, width = h.shape
    return pl.pallas_call(
        functools.partial(ffn_fwd_kernel, cols=weights.shape[1] // 2),
        grid=(total // tokens,),
        in_specs=[
            pl.BlockSpec((tokens, width), lambda t: (t, 0)),
            pl.BlockSpec((1, width), lambda t: (0, 0)),
            pl.BlockSpec(weights.shape, lambda t: (0, 0, 0, 0)),
        ],
        out_specs=pl.BlockSpec((tokens, width), lambda t: (t, 0)),
        out_shape=jax.ShapeDtypeStruct((total, width), bf16),
        compiler_params=PARAMS,
        name="enc_ffn_fwd",
    )(h, gain, weights)


def ffn_step(n, gb, wu_ref, wd_ref, dwu_ref, dwd_ref):
    wu = matrix(wu_ref, 0)
    wd = wd_ref[...].reshape(-1, wd_ref.shape[-1])
    a, slope = gelu_both(nn(n, wu))
    a = a.astype(bf16)
    dwd_ref[...] = tn(a, gb).astype(bf16).reshape(dwd_ref.shape)
    du = (slope * nt(gb, wd)).astype(bf16)
    dwu_ref[:, 0] = packed(tn(n, du), dwu_ref.shape[0])
    return a, wd, nt(du, wu)


def enc_ffn_bwd_kernel(
    h_ref, g_ref, wu_ref, wd_ref, cot_ref, gm_ref, gmem_ref, gh_ref, dwu_ref, dwd_ref, dg_ref, n_s, gb_s, dn_s
):
    i = pl.program_id(0)
    rows, length, width = cot_ref.shape
    late = gm_ref.shape[1]

    @pl.when(i == 0)
    def _():
        n_s[...] = normed(h_ref[...], g_ref[...])
        for r in range(rows):
            gmem_ref[r, : length - late] = cot_ref[r, : length - late].astype(f32)
            gmem_ref[r, length - late :] = cot_ref[r, length - late :].astype(f32) + gm_ref[r]
            gb_s[r * length : (r + 1) * length] = gmem_ref[r].astype(bf16)
        dn_s[...] = jnp.zeros_like(dn_s)

    _, _, dn = ffn_step(n_s[...], gb_s[...], wu_ref, wd_ref, dwu_ref, dwd_ref)
    dn_s[...] += dn

    @pl.when(i == pl.num_programs(0) - 1)
    def _():
        dh, dg = norm_back(h_ref[...], g_ref[...], dn_s[...])
        dg_ref[...] = dg
        gh_ref[...] = gmem_ref[...].reshape(rows * length, width) + dh


def ffn_specs(weights):
    shards, both, blk, width = weights.shape
    cols = both // 2
    up = pl.BlockSpec((shards, 1, blk, width), lambda i: (0, i, 0, 0))
    down_in = pl.BlockSpec((shards // cols, cols, blk, width), lambda i: (i, 1, 0, 0))
    down_out = pl.BlockSpec((shards // cols, cols, blk, width), lambda i: (i, 0, 0, 0))
    grads = jax.ShapeDtypeStruct((shards, cols, blk, width), bf16)
    return cols, up, down_in, down_out, grads


def enc_ffn_bwd(h, gain, weights, cot, late_grad):
    rows, length, width = cot.shape
    tokens = rows * length
    cols, up, down_in, down_out, grads = ffn_specs(weights)
    full = lambda i: (0, 0)
    full3 = lambda i: (0, 0, 0)
    sds = jax.ShapeDtypeStruct
    return pl.pallas_call(
        enc_ffn_bwd_kernel,
        grid=(cols,),
        in_specs=[
            pl.BlockSpec((tokens, width), full),
            pl.BlockSpec((1, width), full),
            up,
            down_in,
            pl.BlockSpec(cot.shape, full3),
            pl.BlockSpec(late_grad.shape, full3),
        ],
        out_specs=[
            pl.BlockSpec(cot.shape, full3),
            pl.BlockSpec((tokens, width), full),
            up,
            down_out,
            pl.BlockSpec((1, width), full),
        ],
        out_shape=[sds(cot.shape, f32), sds((tokens, width), f32), grads, grads, sds((1, width), f32)],
        scratch_shapes=[
            pltpu.VMEM((tokens, width), bf16),
            pltpu.VMEM((tokens, width), bf16),
            pltpu.VMEM((tokens, width), f32),
        ],
        compiler_params=PARAMS,
        name="enc_ffn_bwd",
    )(h, gain, weights, weights, cot, late_grad)


def enc_attn_bwd_kernel(
    gh_ref, q_ref, k_ref, v_ref, segc_ref, segr_ref, w_ref, table_ref, hot_ref,
    dq_ref, dk_ref, dv_ref, dt_ref, strip_ref, acc_ref, do_s,
):
    r = pl.program_id(0)
    length = q_ref.shape[1]
    blocks = length // TILE

    @pl.when(r == 0)
    def _():
        fill_strip(strip_ref, table_ref[...], hot_ref[...], -TILE)
        acc_ref[...] = jnp.zeros_like(acc_ref)

    do_s[...] = nt(gh_ref[0].astype(bf16), matrix(w_ref, 0)).astype(bf16)
    lane = lax.broadcasted_iota(jnp.int32, (length, 2 * HEAD_DIM), 1)
    same = segc_ref[0] == segr_ref[0]
    for hp in range(HEADS // 2):
        ls = slice(hp * 2 * HEAD_DIM, (hp + 1) * 2 * HEAD_DIM)
        qp, kp, vp, dop = q_ref[0, :, ls], k_ref[0, :, ls], v_ref[0, :, ls], do_s[:, ls]
        dq = dk = dv = None
        for sub in range(2):
            h = hp * 2 + sub
            qm, km, dom = half(lane, qp, sub), half(lane, kp, sub), half(lane, dop, sub)
            s = nt(kp, qm)
            starts = [(blocks - 1 - b) * TILE for b in range(blocks)]
            bias = [strip_ref[h, :, c : c + length] for c in starts]
            p = soft_columns(jnp.where(same, s + jnp.concatenate(bias, axis=0), MASKED))
            dp = nt(vp, dom)
            ds = (p * (dp - jnp.sum(dp * p, axis=0, keepdims=True))).astype(bf16)
            new = (tn(ds, km), nn(ds, qm), nn(p.astype(bf16), dom))
            dq, dk, dv = new if dq is None else (dq + new[0], dk + new[1], dv + new[2])
            wide = ds.astype(f32)
            for b, c in enumerate(starts):
                acc_ref[h, :, c : c + length] += wide[b * TILE : (b + 1) * TILE]
        dq_ref[0, :, ls] = dq.astype(bf16)
        dk_ref[0, :, ls] = dk.astype(bf16)
        dv_ref[0, :, ls] = dv.astype(bf16)

    @pl.when(r == pl.num_programs(0) - 1)
    def _():
        dt_ref[...] = strip_sums(acc_ref[...], hot_ref[...])


def enc_attn_bwd(grad_hidden, q, k, v, segments, weights, table):
    rows, length, width = q.shape
    shards, _, blk, _ = weights.shape
    hot = offset_hot(length, True, True)
    row = lambda r: (r, 0, 0)
    full = lambda r: (0, 0)
    sds = jax.ShapeDtypeStruct
    strip = pltpu.VMEM((HEADS, TILE, 2 * length), f32)
    return pl.pallas_call(
        enc_attn_bwd_kernel,
        grid=(rows,),
        in_specs=[pl.BlockSpec((1, length, width), row)] * 4
        + [
            pl.BlockSpec((1, length, 1), row),
            pl.BlockSpec((1, 1, length), row),
            pl.BlockSpec((shards, 1, blk, width), lambda r: (0, 3, 0, 0)),
            pl.BlockSpec(table.shape, full),
            pl.BlockSpec(hot.shape, full),
        ],
        out_specs=[pl.BlockSpec((1, length, width), row)] * 3 + [pl.BlockSpec(table.shape, full)],
        out_shape=[sds(q.shape, bf16)] * 3 + [sds(table.shape, f32)],
        scratch_shapes=[strip, strip, pltpu.VMEM((length, width), bf16)],
        compiler_params=PARAMS,
        name="enc_attn_bwd",
    )(grad_hidden, q, k, v, segments[:, :, None], segments[:, None, :], weights, table, hot)


def enc_weight_grads_kernel(x_ref, g_ref, dq_ref, dk_ref, dv_ref, mix_ref, gh_ref, dw_ref):
    shards = dw_ref.shape[0]
    n = normed(x_ref[...].astype(f32), g_ref[...])
    for w, d_ref in enumerate((dq_ref, dk_ref, dv_ref)):
        dw_ref[:, w] = packed(tn(n, d_ref[...]), shards)
    dw_ref[:, 3] = packed(tn(mix_ref[...], gh_ref[...].astype(bf16)), shards)


def enc_weight_grads(x, gain, dq, dk, dv, mix, grad_hidden, shape):
    return pl.pallas_call(
        enc_weight_grads_kernel,
        out_shape=jax.ShapeDtypeStruct(shape, bf16),
        compiler_params=PARAMS,
        name="enc_weight_grads",
    )(x, gain, dq, dk, dv, mix, grad_hidden)


def enc_input_grad_kernel(x_ref, g_ref, dq_ref, dk_ref, dv_ref, gh_ref, w_ref, gi_ref, dg_ref):
    dn = nt(dq_ref[...], matrix(w_ref, 0)) + nt(dk_ref[...], matrix(w_ref, 1)) + nt(dv_ref[...], matrix(w_ref, 2))
    dh, dg = norm_back(x_ref[...].astype(f32), g_ref[...], dn)
    gi_ref[...] = gh_ref[...] + dh

    @pl.when(pl.program_id(0) == 0)
    def _():
        dg_ref[...] = jnp.zeros_like(dg_ref)

    dg_ref[...] += dg


def enc_input_grad(x, gain, dq, dk, dv, grad_hidden, weights, tokens=512):
    total, width = x.shape
    tile = pl.BlockSpec((tokens, width), lambda t: (t, 0))
    full = pl.BlockSpec((1, width), lambda t: (0, 0))
    sds = jax.ShapeDtypeStruct
    return pl.pallas_call(
        enc_input_grad_kernel,
        grid=(total // tokens,),
        in_specs=[tile, full, tile, tile, tile, tile, pl.BlockSpec(weights.shape, lambda t: (0, 0, 0, 0))],
        out_specs=[tile, full],
        out_shape=[sds((total, width), f32), sds((1, width), f32)],
        compiler_params=PARAMS,
        name="enc_input_grad",
    )(x, gain, dq, dk, dv, grad_hidden, weights)


def dec_masks(rows, steps, late, last_ref, key_major):
    tokens, keys = rows * steps, rows * late
    shape = (tokens, tokens)
    i = lax.broadcasted_iota(jnp.int32, shape, 1 if key_major else 0)
    j = lax.broadcasted_iota(jnp.int32, shape, 0 if key_major else 1)
    causal = (i // steps == j // steps) & (j <= i)
    shape = (keys, tokens) if key_major else (tokens, keys)
    i = lax.broadcasted_iota(jnp.int32, shape, 1 if key_major else 0)
    j = lax.broadcasted_iota(jnp.int32, shape, 0 if key_major else 1)
    return causal, (i // steps == j // late) & (last_ref[...] == 1)


def dec_attn_fwd_kernel(
    emb_ref, enc_ref, last_ref, g_ref, w_ref, table_ref, hot_ref,
    na_ref, qkv_ref, mixa_ref, hida_ref, nb_ref, cq_ref, ckv_ref, mixb_ref, hidb_ref, strip_ref, *, rows,
):
    tokens = emb_ref.shape[0]
    keys = enc_ref.shape[0]
    causal, allowed = dec_masks(rows, tokens // rows, keys // rows, last_ref, False)
    fill_strip(strip_ref, table_ref[...], hot_ref[...], 1 - tokens)
    lane = lax.broadcasted_iota(jnp.int32, (tokens, 2 * HEAD_DIM), 1)

    def attend(q_at, k_at, v_at, bias_at, mask, mix_ref):
        for hp in range(HEADS // 2):
            ls = slice(hp * 2 * HEAD_DIM, (hp + 1) * 2 * HEAD_DIM)
            qp, kp, vp = q_at(ls), k_at(ls), v_at(ls)
            outs = []
            for sub in range(2):
                s = nt(half(lane, qp, sub), kp)
                if bias_at is not None:
                    s = s + bias_at(hp * 2 + sub)
                outs.append(nn(soft_rows(jnp.where(mask, s, MASKED)).astype(bf16), vp))
            mix_ref[:, ls] = jnp.where(lane < HEAD_DIM, outs[0], outs[1]).astype(bf16)

    emb = emb_ref[...].astype(f32)
    na_ref[...] = normed(emb, g_ref[0:1])
    for w in range(3):
        qkv_ref[w] = nn(na_ref[...], matrix(w_ref, w)).astype(bf16)
    attend(
        lambda ls: qkv_ref[0, :, ls],
        lambda ls: qkv_ref[1, :, ls],
        lambda ls: qkv_ref[2, :, ls],
        lambda h: strip_ref[h, :, :tokens],
        causal,
        mixa_ref,
    )
    hida_ref[...] = emb + nn(mixa_ref[...], matrix(w_ref, 3))
    nb_ref[...] = normed(hida_ref[...], g_ref[1:2])
    cq_ref[...] = nn(nb_ref[...], matrix(w_ref, 4)).astype(bf16)
    for w in range(2):
        ckv_ref[w] = nn(enc_ref[...], matrix(w_ref, 5 + w)).astype(bf16)
    attend(
        lambda ls: cq_ref[:, ls],
        lambda ls: ckv_ref[0, :, ls],
        lambda ls: ckv_ref[1, :, ls],
        None,
        allowed,
        mixb_ref,
    )
    hidb_ref[...] = hida_ref[...] + nn(mixb_ref[...], matrix(w_ref, 7))


def whole_spec(a):
    zeros = (0,) * len(a.shape)
    return pl.BlockSpec(a.shape, lambda i: zeros)


def dec_attn_fwd(emb, enc_late, last, gains, weights, table, rows):
    tokens, width = emb.shape
    keys = enc_late.shape[0]
    shards, _, blk, _ = weights.shape
    hot = dec_hot(tokens, tokens // rows, False)
    sds = jax.ShapeDtypeStruct
    one = sds((tokens, width), bf16)
    wide = sds((tokens, width), f32)
    outs = [one, sds((3, tokens, width), bf16), one, wide, one, one, sds((2, keys, width), bf16), one, wide]
    args = (emb, enc_late, last, gains, weights, table, hot)
    specs = [whole_spec(a) for a in args]
    specs[4] = pl.BlockSpec((shards, 8, blk, width), lambda i: (0, 0, 0, 0))
    return pl.pallas_call(
        functools.partial(dec_attn_fwd_kernel, rows=rows),
        grid=(1,),
        in_specs=specs,
        out_specs=[whole_spec(o) for o in outs],
        out_shape=outs,
        scratch_shapes=[pltpu.VMEM((HEADS, tokens, 2 * tokens), f32)],
        compiler_params=PARAMS,
        name="dec_attn_fwd",
    )(*args)


def dec_hot(tokens, steps, reverse):
    codes = np.full(2 * tokens, -1, np.int32)
    own = bucket_codes(steps, False)
    codes[tokens - steps : tokens - steps + len(own)] = own
    if reverse:
        codes = codes[::-1]
    return jnp.asarray(codes[None, :] == np.arange(BUCKETS)[:, None], bf16)


def dec_ffn_kernel(
    h_ref, g_ref, wu_ref, wd_ref, cot_ref, out_ref, gh_ref, dwu_ref, dwd_ref, dg_ref, n_s, gb_s, dn_s, o_s
):
    i = pl.program_id(0)

    @pl.when(i == 0)
    def _():
        n_s[...] = normed(h_ref[...], g_ref[...])
        gb_s[...] = cot_ref[...]
        dn_s[...] = jnp.zeros_like(dn_s)
        o_s[...] = h_ref[...]

    a, wd, dn = ffn_step(n_s[...], gb_s[...], wu_ref, wd_ref, dwu_ref, dwd_ref)
    o_s[...] += nn(a, wd)
    dn_s[...] += dn

    @pl.when(i == pl.num_programs(0) - 1)
    def _():
        out_ref[...] = o_s[...].astype(bf16)
        dh, dg = norm_back(h_ref[...], g_ref[...], dn_s[...])
        dg_ref[...] = dg
        gh_ref[...] = cot_ref[...].astype(f32) + dh


def dec_ffn(h, gain, weights, cot):
    tokens, width = h.shape
    cols, up, down_in, down_out, grads = ffn_specs(weights)
    sds = jax.ShapeDtypeStruct
    tile = pl.BlockSpec((tokens, width), lambda i: (0, 0))
    one = pl.BlockSpec((1, width), lambda i: (0, 0))
    return pl.pallas_call(
        dec_ffn_kernel,
        grid=(cols,),
        in_specs=[tile, one, up, down_in, tile],
        out_specs=[tile, tile, up, down_out, one],
        out_shape=[sds(h.shape, bf16), sds(h.shape, f32), grads, grads, sds((1, width), f32)],
        scratch_shapes=[
            pltpu.VMEM(h.shape, bf16),
            pltpu.VMEM(h.shape, bf16),
            pltpu.VMEM(h.shape, f32),
            pltpu.VMEM(h.shape, f32),
        ],
        compiler_params=PARAMS,
        name="dec_ffn",
    )(h, gain, weights, weights, cot)


def dec_attn_bwd_kernel(
    gb_ref, emb_ref, enc_ref, last_ref, g_ref, w_ref, table_ref, hot_ref,
    na_ref, qkv_ref, mixa_ref, hida_ref, nb_ref, cq_ref, ckv_ref, mixb_ref,
    gm_ref, gr_ref, dw_ref, dg_ref, dt_ref, strip_ref, acc_ref, dq_s, dk_s, dv_s, *, rows,
):
    tokens = emb_ref.shape[0]
    keys = enc_ref.shape[0]
    shards = dw_ref.shape[0]
    causal, allowed = dec_masks(rows, tokens // rows, keys // rows, last_ref, True)
    fill_strip(strip_ref, table_ref[...], hot_ref[...], -tokens)
    lane = lax.broadcasted_iota(jnp.int32, (tokens, 2 * HEAD_DIM), 1)

    def attend_back(q_at, k_at, v_at, do, bias_at, mask, take_score):
        for hp in range(HEADS // 2):
            ls = slice(hp * 2 * HEAD_DIM, (hp + 1) * 2 * HEAD_DIM)
            qp, kp, vp, dop = q_at(ls), k_at(ls), v_at(ls), do[:, ls]
            lanek = lax.broadcasted_iota(jnp.int32, kp.shape, 1)
            dq = dk = dv = None
            for sub in range(2):
                qm, km, dom = half(lane, qp, sub), half(lanek, kp, sub), half(lane, dop, sub)
                s = nt(kp, qm)
                if bias_at is not None:
                    s = s + bias_at(hp * 2 + sub)
                p = soft_columns(jnp.where(mask, s, MASKED))
                dp = nt(vp, dom)
                ds = (p * (dp - jnp.sum(dp * p, axis=0, keepdims=True))).astype(bf16)
                new = (tn(ds, km), nn(ds, qm), nn(p.astype(bf16), dom))
                dq, dk, dv = new if dq is None else (dq + new[0], dk + new[1], dv + new[2])
                if take_score is not None:
                    take_score(hp * 2 + sub, ds)
            dq_s[:, ls] = dq.astype(bf16)
            dk_s[: dk.shape[0], ls] = dk.astype(bf16)
            dv_s[: dv.shape[0], ls] = dv.astype(bf16)

    grad_b = gb_ref[...]
    branch = grad_b.astype(bf16)
    dw_ref[:, 7] = packed(tn(mixb_ref[...], branch), shards)
    do = nt(branch, matrix(w_ref, 7)).astype(bf16)
    attend_back(
        lambda ls: cq_ref[:, ls],
        lambda ls: ckv_ref[0, :, ls],
        lambda ls: ckv_ref[1, :, ls],
        do,
        None,
        allowed,
        None,
    )
    gm_ref[...] = nt(dk_s[...], matrix(w_ref, 5)) + nt(dv_s[...], matrix(w_ref, 6))
    dw_ref[:, 4] = packed(tn(nb_ref[...], dq_s[...]), shards)
    dw_ref[:, 5] = packed(tn(enc_ref[...], dk_s[...]), shards)
    dw_ref[:, 6] = packed(tn(enc_ref[...], dv_s[...]), shards)
    dh, dg = norm_back(hida_ref[...], g_ref[1:2], nt(dq_s[...], matrix(w_ref, 4)))
    dg_ref[1:2] = dg
    grad_a = grad_b + dh

    branch = grad_a.astype(bf16)
    dw_ref[:, 3] = packed(tn(mixa_ref[...], branch), shards)
    do = nt(branch, matrix(w_ref, 3)).astype(bf16)
    acc_ref[...] = jnp.zeros_like(acc_ref)

    def take_score(h, ds):
        acc_ref[h, :, :tokens] = ds.astype(f32)

    attend_back(
        lambda ls: qkv_ref[0, :, ls],
        lambda ls: qkv_ref[1, :, ls],
        lambda ls: qkv_ref[2, :, ls],
        do,
        lambda h: strip_ref[h, :, :tokens],
        causal,
        take_score,
    )
    parts = (dq_s[...], dk_s[:tokens], dv_s[:tokens])
    dn = nt(parts[0], matrix(w_ref, 0)) + nt(parts[1], matrix(w_ref, 1)) + nt(parts[2], matrix(w_ref, 2))
    for w in range(3):
        dw_ref[:, w] = packed(tn(na_ref[...], parts[w]), shards)
    dh, dg = norm_back(emb_ref[...].astype(f32), g_ref[0:1], dn)
    dg_ref[0:1] = dg
    gr_ref[...] = (grad_a + dh).astype(bf16)
    dt_ref[...] = strip_sums(acc_ref[...], hot_ref[...])


def dec_attn_bwd(grad_b, emb, enc_late, last, gains, weights, table, kept, rows):
    tokens, width = emb.shape
    keys = enc_late.shape[0]
    shards, _, blk, _ = weights.shape
    hot = dec_hot(tokens, tokens // rows, True)
    sds = jax.ShapeDtypeStruct
    outs = [
        sds((keys, width), f32),
        sds((tokens, width), bf16),
        sds((shards, 8, blk, width), bf16),
        sds((2, width), f32),
        sds(table.shape, f32),
    ]
    args = (grad_b, emb, enc_late, last, gains, weights, table, hot) + kept
    specs = [whole_spec(a) for a in args]
    specs[5] = pl.BlockSpec((shards, 8, blk, width), lambda i: (0, 0, 0, 0))
    strip = pltpu.VMEM((HEADS, tokens, 2 * tokens), f32)
    return pl.pallas_call(
        functools.partial(dec_attn_bwd_kernel, rows=rows),
        grid=(1,),
        in_specs=specs,
        out_specs=[whole_spec(o) for o in outs],
        out_shape=outs,
        scratch_shapes=[
            strip,
            strip,
            pltpu.VMEM((tokens, width), bf16),
            pltpu.VMEM((keys, width), bf16),
            pltpu.VMEM((keys, width), bf16),
        ],
        compiler_params=PARAMS,
        name="dec_attn_bwd",
    )(*args)


def pack_up(up, width):
    return up.reshape(up.shape[0], -1, width).transpose(1, 0, 2)


def unpack_up(blocks):
    return blocks.transpose(1, 0, 2).reshape(blocks.shape[1], -1)


def on_device(
    enc_input,
    segments,
    targets,
    enc_cot,
    dec_cot,
    enc_gains,
    enc_attn,
    enc_table,
    enc_up,
    enc_down,
    embed,
    dec_gains,
    dec_self,
    dec_cross,
    dec_table,
    dec_up,
    dec_down,
):
    rows, length, width = enc_input.shape
    steps = targets.shape[1]
    shards = lax.axis_size("fsdp")
    blk = enc_attn.shape[1]
    own = embed.shape[0]
    me = lax.axis_index("fsdp")
    late = min(length, SERIES_MOST)

    shifted = jnp.concatenate([jnp.zeros((rows, 1), jnp.int32), targets[:, :-1]], axis=1).reshape(-1)
    small = jnp.concatenate(
        [
            enc_gains.reshape(-1),
            dec_gains.reshape(-1),
            enc_table,
            dec_table,
            (shifted // 64).astype(bf16),
            (shifted % 64).astype(bf16),
        ]
    )
    small = lax.all_gather(small, "fsdp", axis=0, tiled=False)
    n_e, n_d, tab, ids = enc_gains.shape[0], dec_gains.shape[0], enc_table.shape[0], shifted.shape[0]
    at = (n_e + n_d) * blk
    gains = small[:, :at].reshape(shards, n_e + n_d, blk).transpose(1, 0, 2).reshape(n_e + n_d, width)
    enc_tab = small[:, at : at + tab].reshape(HEADS, BUCKETS)
    dec_tab = small[:, at + tab : at + 2 * tab].reshape(HEADS, BUCKETS)
    at += 2 * tab
    all_ids = small[:, at : at + ids].astype(jnp.int32) * 64 + small[:, at + ids :].astype(jnp.int32)

    w_attn = lax.all_gather(enc_attn, "fsdp", axis=0, tiled=False)
    ffn_blocks = jnp.concatenate([pack_up(enc_up, width), enc_down.reshape(-1, blk, width)], axis=0)
    w_ffn = lax.all_gather(ffn_blocks, "fsdp", axis=0, tiled=False)
    dec_blocks = jnp.concatenate([dec_self, dec_cross], axis=0)
    w_dec = lax.all_gather(dec_blocks, "fsdp", axis=0, tiled=False)
    dffn_blocks = jnp.concatenate([pack_up(dec_up, width), dec_down.reshape(-1, blk, width)], axis=0)
    w_dffn = lax.all_gather(dffn_blocks, "fsdp", axis=0, tiled=False)

    hot = (all_ids.reshape(-1)[:, None] == me * own + jnp.arange(own)[None, :]).astype(bf16)
    found = jnp.dot(hot, embed, preferred_element_type=f32).astype(bf16)
    emb = lax.psum_scatter(found, "fsdp", scatter_dimension=0, tiled=True)

    hidden, q, k, v, mix = enc_attn_fwd(enc_input, segments, gains[0:1], w_attn, enc_tab)
    hidden = hidden.reshape(-1, width)
    enc_out = ffn_fwd(hidden, gains[1:2], w_ffn).reshape(rows, length, width)
    enc_late = enc_out[:, length - late :].reshape(-1, width)
    last = (segments == segments[:, -1:])[:, length - late :].astype(jnp.int32).reshape(1, -1)
    dec_gain = gains[n_e:]
    kept = dec_attn_fwd(emb, enc_late, last, dec_gain, w_dec, dec_tab, rows)
    cot = dec_cot.reshape(-1, width)
    dec_out, grad_b, d_dup, d_ddown, dg_c = dec_ffn(kept[-1], dec_gain[2:3], w_dffn, cot)

    grad_late, grad_rows, d_dec, dg_ab, d_dtab = dec_attn_bwd(
        grad_b, emb, enc_late, last.reshape(-1, 1), dec_gain, w_dec, dec_tab, tuple(kept[:-1]), rows
    )
    grad_memory, grad_hidden, d_up, d_down, dg_1 = enc_ffn_bwd(
        hidden, gains[1:2], w_ffn, enc_cot, grad_late.reshape(rows, late, width)
    )
    dq, dk, dv, d_etab = enc_attn_bwd(
        grad_hidden.reshape(rows, length, width), q, k, v, segments, w_attn, enc_tab
    )
    flat = lambda a: a.reshape(-1, width)
    d_attn = enc_weight_grads(
        flat(enc_input), gains[0:1], flat(dq), flat(dk), flat(dv), flat(mix), grad_hidden, w_attn.shape
    )
    grad_input, dg_0 = enc_input_grad(
        flat(enc_input), gains[0:1], flat(dq), flat(dk), flat(dv), grad_hidden, w_attn
    )

    def owned(a):
        return lax.psum_scatter(a, "fsdp", scatter_dimension=0, tiled=False)

    s_dec = owned(jnp.concatenate([d_dec, d_dup, d_ddown], axis=1))
    all_rows = lax.all_gather(grad_rows, "fsdp", axis=0, tiled=True)
    g_embed = lax.dot_general(hot, all_rows, (((0,), (0,)), ((), ())), preferred_element_type=f32)
    s_enc = owned(jnp.concatenate([d_up, d_down, d_attn], axis=1))

    g_small = jnp.concatenate([dg_0, dg_1, dg_ab, dg_c], axis=0)
    g_small = jnp.concatenate(
        [
            g_small.reshape(n_e + n_d, shards, blk).transpose(1, 0, 2).reshape(shards, -1),
            d_etab.reshape(shards, tab),
            d_dtab.reshape(shards, tab),
        ],
        axis=1,
    )
    g_small = lax.psum(g_small, ("fsdp", "dp"))
    g_small = lax.dynamic_index_in_dim(g_small, me, 0, keepdims=False)
    at = (n_e + n_d) * blk
    g_gains = g_small[:at].reshape(n_e + n_d, blk)

    summed = jnp.concatenate(
        [s_dec.reshape(-1, width), s_enc.reshape(-1, width), g_embed.astype(bf16)], axis=0
    )
    summed = lax.psum(summed, "dp").astype(f32)
    counts = np.cumsum([0, 4, 4, dffn_blocks.shape[0] // 2, dffn_blocks.shape[0] // 2, ffn_blocks.shape[0] // 2, ffn_blocks.shape[0] // 2, 4])
    pieces = [summed[a * blk : b * blk].reshape(-1, blk, width) for a, b in zip(counts[:-1], counts[1:])]
    return (
        enc_out,
        dec_out.reshape(rows, steps, width),
        grad_input.reshape(rows, length, width),
        grad_memory,
        g_gains[:n_e],
        pieces[6],
        g_small[at : at + tab],
        unpack_up(pieces[4]),
        pieces[5].reshape(-1, width),
        summed[counts[-1] * blk :],
        g_gains[n_e:],
        pieces[0],
        pieces[1],
        g_small[at + tab :],
        unpack_up(pieces[2]),
        pieces[3].reshape(-1, width),
    )


def solution(mesh):
    placed = (
        P(("fsdp", "dp"), None, None),
        P(("fsdp", "dp"), None),
        P(("fsdp", "dp"), None),
        P(("fsdp", "dp"), None, None),
        P(("fsdp", "dp"), None, None),
        P(None, "fsdp"),
        P(None, "fsdp", None),
        P("fsdp"),
        P("fsdp", None),
        P("fsdp", None),
        P("fsdp", None),
        P(None, "fsdp"),
        P(None, "fsdp", None),
        P(None, "fsdp", None),
        P("fsdp"),
        P("fsdp", None),
        P("fsdp", None),
    )
    return jax.shard_map(
        on_device,
        mesh=mesh,
        in_specs=placed,
        out_specs=(
            P(("fsdp", "dp"), None, None),
            P(("fsdp", "dp"), None, None),
            P(("fsdp", "dp"), None, None),
            P(("fsdp", "dp"), None, None),
            P(None, "fsdp"),
            P(None, "fsdp", None),
            P("fsdp"),
            P("fsdp", None),
            P("fsdp", None),
            P("fsdp", None),
            P(None, "fsdp"),
            P(None, "fsdp", None),
            P(None, "fsdp", None),
            P("fsdp"),
            P("fsdp", None),
            P("fsdp", None),
        ),
        check_vma=False,
    )
```

```python
import functools

import jax
import jax.numpy as jnp
import numpy as np
from jax import lax
from jax.experimental import pallas as pl
from jax.experimental.pallas import tpu as pltpu
from jax.sharding import PartitionSpec as P

HEADS = 8
HEAD_DIM = 64
BUCKETS = 32
SERIES_MOST = 256
TILE = 128
MASKED = -1000000000.0

epsilon = 1e-06
f32 = jnp.float32
bf16 = jnp.bfloat16
PEAK = 1.15e9

TABLE_ROW = 0
GAIN_ROW = 8
ID_ROW = 13
SMALL_ROWS = 16
DEC_LANE = 128


def bucket_codes(length, both_ways):
    bucket_list = []
    for offset in range(-(length - 1), length):
        if both_ways:
            upper_half = 16 if offset > 0 else 0
            distance = abs(offset)
            if distance < 8:
                bucket = distance
            else:
                bucket = 8 + sum(
                    (1 for exponent in range(1, 8) if distance * distance >= 64 * 2**exponent)
                )
        else:
            upper_half = 0
            distance = max(-offset, 0)
            if distance < 16:
                bucket = distance
            else:
                bucket = 16 + sum(
                    (1 for exponent in range(1, 16) if distance**16 >= 16**16 * 2 ** (3 * exponent))
                )
        bucket_list.append(upper_half + bucket)
    return np.array(bucket_list, dtype=np.int32)


def offset_hot(length, both_ways, reverse):
    codes = np.concatenate([bucket_codes(length, both_ways), [-1]])
    if reverse:
        codes = codes[::-1]
    return jnp.asarray(codes[None, :] == np.arange(BUCKETS)[:, None], bf16)


def nn(a, b):
    return lax.dot_general(a, b, (((1,), (0,)), ((), ())), preferred_element_type=f32)


def nt(a, b):
    return lax.dot_general(a, b, (((1,), (1,)), ((), ())), preferred_element_type=f32)


def tn(a, b):
    return lax.dot_general(a, b, (((0,), (0,)), ((), ())), preferred_element_type=f32)


def rho_of(h):
    return lax.rsqrt(jnp.mean(h * h, axis=-1, keepdims=True) + epsilon)


def normed(h, gain):
    return (h * rho_of(h) * gain.astype(f32)).astype(bf16)


def norm_back(h, gain, dn):
    rho = rho_of(h)
    xh = h * rho
    gu = dn * gain.astype(f32)
    return rho * (gu - xh * jnp.mean(gu * xh, axis=-1, keepdims=True))


def gelu(u):
    t = jnp.tanh(np.float32(np.sqrt(2 / np.pi)) * (u + 0.044715 * (u * u * u)))
    return 0.5 * u * (1.0 + t)


def gelu_both(u):
    c = np.float32(np.sqrt(2 / np.pi))
    u2 = u * u
    t = jnp.tanh(c * (u + 0.044715 * (u2 * u)))
    cdf = 0.5 * (1.0 + t)
    return u * cdf, cdf + 0.5 * u * (1.0 - t * t) * (c + (3 * 0.044715 * c) * u2)


def matrix(ref, w):
    part = ref[:, w]
    return part.reshape(part.shape[0] * part.shape[1], part.shape[2])


def packed(value, shards):
    return value.reshape(shards, value.shape[0] // shards, value.shape[1]).astype(bf16)


def place(shard, me, shards):
    upper = shards.bit_length() - 2
    diff = shard ^ me
    spot = 0
    for j in range(upper):
        even = (diff >> (1 + j)) & 1
        odd = (diff >> (upper - j)) & 1
        spot = spot | (jnp.where((shard & 1) == 0, even, odd) << (upper - 1 - j))
    return spot


def shard_at(spot, me, shards):
    upper = shards.bit_length() - 2
    diff_even = diff_odd = 0
    for j in range(upper):
        bit = (spot >> (upper - 1 - j)) & 1
        diff_even = diff_even | (bit << (1 + j))
        diff_odd = diff_odd | (bit << (upper - j))
    return me ^ jnp.where((me & 1) == 0, diff_even, diff_odd)


def spread(refs):
    return [(ref, i) for ref in refs for i in range(ref.shape[0])]


def collect(out_ref, refs, me, rows=None):
    shards = out_ref.shape[0]
    count = len(refs) // 2
    for core, part in ((me, refs[:count]), (me ^ 1, refs[count:])):
        for p, (ref, i) in enumerate(spread(part)):
            piece = ref[i] if rows is None else ref[i, :rows]
            out_ref[shard_at(p, core, shards)] = piece.reshape(out_ref.shape[1:])


SCALAR = pl.BlockSpec(memory_space=pltpu.SMEM)
ANYWHERE = pl.BlockSpec(memory_space=pl.ANY)
sds = jax.ShapeDtypeStruct


def whole_spec(a):
    zeros = (0,) * len(a.shape)
    return pl.BlockSpec(a.shape, lambda i: zeros)


def call(kernel, name, us, args, in_specs, outs, out_specs, scratch=(), grid=1, after=(), vmem=24):
    waits = len(after)

    def body(*refs):
        kernel(*refs[waits:])

    return pl.pallas_call(
        body,
        grid=(grid,),
        in_specs=[ANYWHERE] * waits + list(in_specs),
        out_specs=list(out_specs),
        out_shape=[sds(o.shape, o.dtype) for o in outs],
        scratch_shapes=list(scratch),
        compiler_params=pltpu.CompilerParams(vmem_limit_bytes=int(vmem * 2**20)),
        cost_estimate=pl.CostEstimate(flops=int(us * PEAK), bytes_accessed=1024, transcendentals=0),
        name=name,
    )(*after, *args)


def simple(kernel, name, us, args, outs, after=(), scratch=(), vmem=None):
    if vmem is None:
        vmem = 1 + sum(2 * np.prod(a.shape) * a.dtype.itemsize for a in (*args, *outs)) / 2**20
    return call(
        kernel, name, us, args, [whole_spec(a) for a in args], outs, [whole_spec(o) for o in outs], scratch,
        after=after, vmem=vmem,
    )


def half(lane, value, which):
    return jnp.where((lane // HEAD_DIM) == which, value, jnp.zeros_like(value))


def fill_strip(strip_ref, table, hot, shift):
    vec = nn(table, hot)
    width = hot.shape[1]
    rows = strip_ref.shape[1]
    for h in range(HEADS):
        row = jnp.broadcast_to(vec[h : h + 1], (rows, width))
        strip_ref[h] = pltpu.roll(row, (width + shift) % width, 1, stride=1, stride_axis=0)


def strip_sums(acc, hot):
    rows, width = acc.shape[1], acc.shape[2]
    total = jnp.zeros((HEADS, 8, width), f32)
    for g in range(rows // 8):
        part = acc[:, g * 8 : g * 8 + 8, :].reshape(HEADS * 8, width)
        if g:
            part = pltpu.roll(part, width - 8 * g, 1)
        total = total + part.reshape(HEADS, 8, width)
    flat = total.reshape(HEADS * 8, width)
    sub = lax.broadcasted_iota(jnp.int32, flat.shape, 0) % 8
    for b in range(3):
        flat = jnp.where((sub >> b) & 1 == 1, pltpu.roll(flat, width - (1 << b), 1), flat)
    diag = pltpu.roll(jnp.sum(flat.reshape(HEADS, 8, width), axis=1), rows, 1)
    return lax.dot_general(
        diag,
        hot.astype(f32),
        (((1,), (1,)), ((), ())),
        precision=lax.Precision.HIGHEST,
        preferred_element_type=f32,
    )


def soft_rows(s):
    e = jnp.exp(s - jnp.max(s, axis=-1, keepdims=True))
    return e * (1.0 / jnp.sum(e, axis=-1, keepdims=True))


def soft_columns(s):
    e = jnp.exp(s - jnp.max(s, axis=0, keepdims=True))
    return e * (1.0 / jnp.sum(e, axis=0, keepdims=True))


def pack_first_kernel(me_ref, attn_ref, eg_ref, dg_ref, et_ref, dt_ref, tok_ref, out_ref, *, shards):
    count, blk, width = attn_ref.shape
    me = me_ref[0]
    out_ref[: count * blk] = attn_ref[...].reshape(count * blk, width)
    base = count * blk
    lane = lax.broadcasted_iota(jnp.int32, (1, width), 1)
    here = (lane // blk) == me
    per = et_ref.shape[1]
    row8 = lax.broadcasted_iota(jnp.int32, (HEADS, BUCKETS), 0)
    lane8 = lax.broadcasted_iota(jnp.int32, (HEADS, BUCKETS), 1)
    held = (row8 * BUCKETS + lane8) // per == me
    small = jnp.zeros((SMALL_ROWS, width), f32)
    rows = lax.broadcasted_iota(jnp.int32, (SMALL_ROWS, width), 0)
    gains = [eg_ref[i : i + 1] for i in range(eg_ref.shape[0])] + [dg_ref[i : i + 1] for i in range(dg_ref.shape[0])]
    for i, g in enumerate(gains):
        wide = jnp.where(here, jnp.concatenate([g.astype(f32)] * shards, axis=1), 0.0)
        small = jnp.where(rows == GAIN_ROW + i, jnp.broadcast_to(wide, small.shape), small)
    tok = tok_ref[...]
    steps = tok.shape[1]
    first = lax.broadcasted_iota(jnp.int32, tok.shape, 1) == 0
    shifted = jnp.where(first, 0, pltpu.roll(tok, 1, 1) if steps % 128 == 0 else jnp.concatenate([tok[:, -1:], tok[:, :-1]], axis=1))
    parts = [(shifted[r : r + 1] >> 6).astype(f32) for r in range(tok.shape[0])]
    parts += [(shifted[r : r + 1] & 63).astype(f32) for r in range(tok.shape[0])]
    ids = jnp.concatenate(parts, axis=1)
    ids = jnp.concatenate([ids, jnp.zeros((1, width - ids.shape[1]), f32)], axis=1)
    small = jnp.where(rows == ID_ROW, jnp.broadcast_to(ids, small.shape), small)
    out_ref[base:] = small.astype(bf16)
    for t_ref, at in ((et_ref, 0), (dt_ref, DEC_LANE)):
        table = jnp.concatenate([t_ref[...].astype(f32)] * (BUCKETS // per), axis=1)
        table = jnp.where(held, jnp.broadcast_to(table, held.shape), 0.0)
        out_ref[base : base + HEADS, at : at + BUCKETS] = table.astype(bf16)


def pack_first(me, attn, enc_gains, dec_gains, enc_table, dec_table, targets, shards):
    count, blk, width = attn.shape
    out = sds((1, count * blk + SMALL_ROWS, width), bf16)
    args = (attn, enc_gains, dec_gains, enc_table.reshape(1, -1), dec_table.reshape(1, -1), targets)

    def body(me_ref, *refs):
        pack_first_kernel(me_ref, *refs[:-1], refs[-1].at[0], shards=shards)

    return call(
        body, "pack_first", 2, (me,) + args, [SCALAR] + [whole_spec(a) for a in args], [out], [whole_spec(out)], vmem=4
    )[0]


def pack_ffn_kernel(up_ref, down_ref, out_ref, *, shards):
    blocks = out_ref.shape[0] // 2
    blk = up_ref.shape[0]
    for b in range(blocks):
        parts = [up_ref[:, (c * blocks + b) * blk : (c * blocks + b + 1) * blk] for c in range(shards)]
        out_ref[2 * b] = jnp.concatenate(parts, axis=1)
        out_ref[2 * b + 1] = down_ref[b * blk : (b + 1) * blk]


def pack_ffn(up, down, shards, after):
    blk, width = up.shape[0], down.shape[1]
    out = sds((1, 2 * up.shape[1] // width, blk, width), bf16)

    def body(up_ref, down_ref, out_ref):
        pack_ffn_kernel(up_ref, down_ref, out_ref.at[0], shards=shards)

    return simple(body, "pack_ffn", 1, (up, down), [out], after)[0]


def pack_attn_kernel(a_ref, b_ref, out_ref):
    count = a_ref.shape[0]
    out_ref[0, :count] = a_ref[...]
    out_ref[0, count:] = b_ref[...]


def pack_attn(a, b, after):
    out = sds((1, 2 * a.shape[0]) + a.shape[1:], bf16)
    return simple(pack_attn_kernel, "pack_attn", 1, (a, b), [out], after)[0]


def gate_kernel(a_ref, o_ref):
    o_ref[...] = a_ref[...]


def gate(a, after):
    return simple(gate_kernel, "gate", 0.5, (a,), [a], after)[0]


def join_kernel(a_ref, b_ref, o_ref):
    size = a_ref.shape[0]
    o_ref[:size] = a_ref[...]
    o_ref[size:] = b_ref[...]


def join(a, b, after):
    return simple(join_kernel, "join", 1, (a, b), [sds((2 * a.shape[0],) + a.shape[1:], a.dtype)], after)[0]


def add_first_kernel(me_ref, *refs):
    parts = len(refs[:-2]) // 4
    keep_ref, send_ref = refs[-2:]
    for out_ref, far in ((keep_ref, 0), (send_ref, 1)):
        at = 0
        for i in range(parts):
            a_ref, b_ref = refs[4 * i + 2 * far], refs[4 * i + 2 * far + 1]
            size = a_ref.shape[1]
            out_ref[0, at : at + size] = (a_ref[0].astype(f32) + b_ref[0].astype(f32)).astype(bf16)
            at += size


def add_first(me, pairs, after):
    shards = pairs[0][0].shape[0]
    quarter = shards // 4
    rest = (0,) * (len(pairs[0][0].shape) - 1)
    waits = len(after)

    def body(*refs):
        add_first_kernel(refs[0], *refs[1 + waits :])

    args, specs, size, total = [], [], 0, 0
    for grads, other in pairs:
        block = (1,) + grads.shape[1:]
        near = pl.BlockSpec(block, lambda p, me_ref: (shard_at(p, me_ref[0], shards),) + rest)
        far = pl.BlockSpec(block, lambda p, me_ref: (shard_at(p + quarter, me_ref[0], shards),) + rest)
        args += [grads, other, grads, other]
        specs += [near, near, far, far]
        size += grads.shape[1]
        total += np.prod(block) * 2
    out = (quarter, size) + pairs[0][0].shape[2:]
    out_spec = pl.BlockSpec((1,) + out[1:], lambda p, me_ref: (p,) + rest)
    return pl.pallas_call(
        body,
        grid_spec=pltpu.PrefetchScalarGridSpec(
            num_scalar_prefetch=1,
            grid=(quarter,),
            in_specs=[ANYWHERE] * waits + specs,
            out_specs=[out_spec, out_spec],
        ),
        out_shape=[sds(out, bf16)] * 2,
        compiler_params=pltpu.CompilerParams(vmem_limit_bytes=int(2 * 6 * total + 2**20)),
        cost_estimate=pl.CostEstimate(flops=int(2 * PEAK), bytes_accessed=1024, transcendentals=0),
        name="add_first",
    )(me, *after, *args)


def add_halves_kernel(a_ref, b_ref, keep_ref, send_ref):
    mid = keep_ref.shape[0]
    keep_ref[...] = (a_ref[:mid].astype(f32) + b_ref[:mid].astype(f32)).astype(bf16)
    send_ref[...] = (a_ref[mid:].astype(f32) + b_ref[mid:].astype(f32)).astype(bf16)


def add_halves(a, b, after):
    out = sds((a.shape[0] // 2,) + a.shape[1:], bf16)
    return simple(add_halves_kernel, "add_halves", 1, (a, b), [out] * 2, after)


def add_kernel(a_ref, b_ref, o_ref):
    o_ref[...] = (a_ref[...].astype(f32) + b_ref[...].astype(f32)).astype(o_ref.dtype)


def add(a, b, after, dtype=bf16):
    return simple(add_kernel, "add", 0.7, (a, b), [sds(a.shape, dtype)], after)[0]


def enc_attn_fwd_body(x_ref, segc_ref, segr_ref, small, w_ref, hot_ref, hid_ref, q_ref, k_ref, v_ref, mix_ref, strip_ref):
    length = x_ref.shape[1]
    blocks = length // TILE
    table = small[TABLE_ROW : TABLE_ROW + HEADS, :BUCKETS].astype(bf16)
    fill_strip(strip_ref, table, hot_ref[...], 1 - TILE)
    x = x_ref[0].astype(f32)
    n = normed(x, small[GAIN_ROW : GAIN_ROW + 1])
    q_ref[0] = nn(n, matrix(w_ref, 0)).astype(bf16)
    k_ref[0] = nn(n, matrix(w_ref, 1)).astype(bf16)
    v_ref[0] = nn(n, matrix(w_ref, 2)).astype(bf16)
    lane = lax.broadcasted_iota(jnp.int32, (length, 2 * HEAD_DIM), 1)
    same = segc_ref[0] == segr_ref[0]
    for hp in range(HEADS // 2):
        ls = slice(hp * 2 * HEAD_DIM, (hp + 1) * 2 * HEAD_DIM)
        qp, kp, vp = q_ref[0, :, ls], k_ref[0, :, ls], v_ref[0, :, ls]
        outs = []
        for sub in range(2):
            s = nt(half(lane, qp, sub), kp)
            starts = [(blocks - 1 - b) * TILE for b in range(blocks)]
            bias = [strip_ref[hp * 2 + sub, :, c : c + length] for c in starts]
            s = jnp.where(same, s + jnp.concatenate(bias, axis=0), MASKED)
            outs.append(nn(soft_rows(s).astype(bf16), vp))
        mix_ref[0, :, ls] = jnp.where(lane < HEAD_DIM, outs[0], outs[1]).astype(bf16)
    hid_ref[0] = x + nn(mix_ref[0], matrix(w_ref, 3))


def enc_attn_fwd_kernel(me_ref, x_ref, segc_ref, segr_ref, hot_ref, *refs):
    pieces, outs, (w_ref, small_ref, strip_ref) = refs[:-8], refs[-8:-3], refs[-3:]

    @pl.when(pl.program_id(0) == 0)
    def _():
        rows = pieces[0].shape[1] - SMALL_ROWS
        collect(w_ref, pieces, me_ref[0], rows)
        small = jnp.zeros(small_ref.shape, f32)
        for ref, i in spread(pieces):
            small = small + ref[i, rows:].astype(f32)
        small_ref[...] = small

    enc_attn_fwd_body(x_ref, segc_ref, segr_ref, small_ref, w_ref, hot_ref, *outs, strip_ref)


def enc_attn_fwd(me, x, segc, segr, pieces, after):
    rows, length, width = x.shape
    shards = sum(p.shape[0] for p in pieces)
    hot = offset_hot(length, True, False)
    row = lambda a: pl.BlockSpec((1,) + tuple(a.shape[1:]), lambda r: (r, 0, 0))
    outs = [sds(x.shape, f32)] + [sds(x.shape, bf16)] * 4
    full = sds((shards, 4, width // shards, width), bf16)
    small = sds((SMALL_ROWS, width), f32)
    args = [me, x, segc, segr, hot] + list(pieces)
    return call(
        enc_attn_fwd_kernel, "enc_attn_fwd", 14, args,
        [SCALAR, row(x), row(segc), row(segr)] + [whole_spec(a) for a in args[4:]],
        outs + [full, small], [row(o) for o in outs] + [whole_spec(full), whole_spec(small)],
        [pltpu.VMEM((HEADS, TILE, 2 * length), f32)], grid=rows, after=after, vmem=24,
    )


def enc_ffn_fwd_kernel(me_ref, h_ref, small_ref, *refs):
    pieces, (o_ref, w_ref, n_s, acc_s) = refs[:-4], refs[-4:]
    i = pl.program_id(0)

    @pl.when(i == 0)
    def _():
        n_s[...] = normed(h_ref[...], small_ref[GAIN_ROW + 1 : GAIN_ROW + 2])
        acc_s[...] = h_ref[...]

    collect(w_ref, pieces, me_ref[0])
    a = gelu(nn(n_s[...], matrix(w_ref, 0))).astype(bf16)
    acc_s[...] += nn(a, matrix(w_ref, 1))

    @pl.when(i == pl.num_programs(0) - 1)
    def _():
        o_ref[...] = acc_s[...].astype(bf16)


def pair_spec(a, start=0):
    return pl.BlockSpec((a.shape[0], 2) + tuple(a.shape[2:]), lambda i: (0, start + i, 0, 0))


def enc_ffn_fwd(me, h, small, pieces, after):
    tokens, width = h.shape
    full = sds((sum(p.shape[0] for p in pieces),) + pieces[0].shape[1:], bf16)
    out = sds(h.shape, bf16)
    return call(
        enc_ffn_fwd_kernel, "enc_ffn_fwd", 9, (me, h, small, *pieces),
        [SCALAR, whole_spec(h), whole_spec(small)] + [pair_spec(p) for p in pieces],
        [out, full], [whole_spec(out), pair_spec(full)],
        [pltpu.VMEM(h.shape, bf16), pltpu.VMEM(h.shape, f32)],
        grid=full.shape[1] // 2, after=after, vmem=24,
    )


def ffn_step(n, gb, w_ref, dw_ref):
    shards = w_ref.shape[0]
    wu, wd = matrix(w_ref, 0), matrix(w_ref, 1)
    a, slope = gelu_both(nn(n, wu))
    a = a.astype(bf16)
    dw_ref[:, 1] = packed(tn(a, gb), shards)
    du = (slope * nt(gb, wd)).astype(bf16)
    dw_ref[:, 0] = packed(tn(n, du), shards)
    return a, wd, nt(du, wu)


def enc_ffn_bwd_first_kernel(h_ref, small_ref, w_ref, cot_ref, gm_ref, gmem_ref, dn_ref, dw_ref, n_s, gb_s):
    rows, length, width = cot_ref.shape
    late = gm_ref.shape[1]

    @pl.when(pl.program_id(0) == 0)
    def _():
        n_s[...] = normed(h_ref[...], small_ref[GAIN_ROW + 1 : GAIN_ROW + 2])
        for r in range(rows):
            gmem_ref[r, : length - late] = cot_ref[r, : length - late].astype(f32)
            gmem_ref[r, length - late :] = cot_ref[r, length - late :].astype(f32) + gm_ref[r]
            gb_s[r * length : (r + 1) * length] = gmem_ref[r].astype(bf16)
        dn_ref[...] = jnp.zeros_like(dn_ref)

    dn_ref[...] += ffn_step(n_s[...], gb_s[...], w_ref, dw_ref)[2]


def enc_ffn_bwd_next_kernel(h_ref, small_ref, w_ref, gmem_ref, dn_ref, gh_ref, dw_ref, n_s, gb_s, dn_s):
    rows, length, width = gmem_ref.shape
    gain = small_ref[GAIN_ROW + 1 : GAIN_ROW + 2]

    @pl.when(pl.program_id(0) == 0)
    def _():
        n_s[...] = normed(h_ref[...], gain)
        gb_s[...] = gmem_ref[...].reshape(rows * length, width).astype(bf16)
        dn_s[...] = dn_ref[...]

    dn_s[...] += ffn_step(n_s[...], gb_s[...], w_ref, dw_ref)[2]

    @pl.when(pl.program_id(0) == pl.num_programs(0) - 1)
    def _():
        gh_ref[...] = gmem_ref[...].reshape(rows * length, width) + norm_back(h_ref[...], gain, dn_s[...])


def enc_ffn_bwd_first(h, small, weights, cot, late_grad, after):
    blocks = weights.shape[1] // 4
    grads = sds((weights.shape[0], 2 * blocks) + weights.shape[2:], bf16)
    gmem, dn = sds(cot.shape, f32), sds(h.shape, f32)
    args = (h, small, weights, cot, late_grad)
    specs = [whole_spec(h), whole_spec(small), pair_spec(weights), whole_spec(cot), whole_spec(late_grad)]
    return call(
        enc_ffn_bwd_first_kernel, "enc_ffn_bwd", 10, args, specs, [gmem, dn, grads],
        [whole_spec(gmem), whole_spec(dn), pair_spec(grads)],
        [pltpu.VMEM(h.shape, bf16)] * 2, grid=blocks, after=after, vmem=24,
    )


def enc_ffn_bwd_next(h, small, weights, gmem, dn, after):
    blocks = weights.shape[1] // 4
    grads = sds((weights.shape[0], 2 * blocks) + weights.shape[2:], bf16)
    gh = sds(h.shape, f32)
    args = (h, small, weights, gmem, dn)
    specs = [whole_spec(h), whole_spec(small), pair_spec(weights, blocks), whole_spec(gmem), whole_spec(dn)]
    return call(
        enc_ffn_bwd_next_kernel, "enc_ffn_bwd", 10, args, specs, [gh, grads],
        [whole_spec(gh), pair_spec(grads)],
        [pltpu.VMEM(h.shape, bf16)] * 2 + [pltpu.VMEM(h.shape, f32)], grid=blocks, after=after, vmem=24,
    )


def enc_attn_bwd_kernel(
    gh_ref, q_ref, k_ref, v_ref, segc_ref, segr_ref, w_ref, small_ref, hot_ref,
    dq_ref, dk_ref, dv_ref, dt_ref, strip_ref, acc_ref, do_s,
):
    length = q_ref.shape[1]
    blocks = length // TILE
    table = small_ref[TABLE_ROW : TABLE_ROW + HEADS, :BUCKETS].astype(bf16)
    fill_strip(strip_ref, table, hot_ref[...], -TILE)
    acc_ref[...] = jnp.zeros_like(acc_ref)
    do_s[...] = nt(gh_ref[0].astype(bf16), matrix(w_ref, 0)).astype(bf16)
    lane = lax.broadcasted_iota(jnp.int32, (length, 2 * HEAD_DIM), 1)
    same = segc_ref[0] == segr_ref[0]
    for hp in range(HEADS // 2):
        ls = slice(hp * 2 * HEAD_DIM, (hp + 1) * 2 * HEAD_DIM)
        qp, kp, vp, dop = q_ref[0, :, ls], k_ref[0, :, ls], v_ref[0, :, ls], do_s[:, ls]
        dq = dk = dv = None
        for sub in range(2):
            h = hp * 2 + sub
            qm, km, dom = half(lane, qp, sub), half(lane, kp, sub), half(lane, dop, sub)
            s = nt(kp, qm)
            starts = [(blocks - 1 - b) * TILE for b in range(blocks)]
            bias = [strip_ref[h, :, c : c + length] for c in starts]
            p = soft_columns(jnp.where(same, s + jnp.concatenate(bias, axis=0), MASKED))
            dp = nt(vp, dom)
            ds = (p * (dp - jnp.sum(dp * p, axis=0, keepdims=True))).astype(bf16)
            new = (tn(ds, km), nn(ds, qm), nn(p.astype(bf16), dom))
            dq, dk, dv = new if dq is None else (dq + new[0], dk + new[1], dv + new[2])
            wide = ds.astype(f32)
            for b, c in enumerate(starts):
                acc_ref[h, :, c : c + length] += wide[b * TILE : (b + 1) * TILE]
        dq_ref[0, :, ls] = dq.astype(bf16)
        dk_ref[0, :, ls] = dk.astype(bf16)
        dv_ref[0, :, ls] = dv.astype(bf16)
    dt_ref[...] = strip_sums(acc_ref[...], hot_ref[...])


def enc_attn_bwd(r, grad_hidden, q, k, v, segc, segr, weights, small, after):
    rows, length, width = q.shape
    shards, _, blk, _ = weights.shape
    hot = offset_hot(length, True, True)
    strip = pltpu.VMEM((HEADS, TILE, 2 * length), f32)
    args = [grad_hidden, q, k, v, segc, segr]
    specs = [pl.BlockSpec((1,) + tuple(a.shape[1:]), lambda i: (r, 0, 0)) for a in args]
    specs += [pl.BlockSpec((shards, 1, blk, width), lambda i: (0, 3, 0, 0)), whole_spec(small), whole_spec(hot)]
    args += [weights, small, hot]
    outs = [sds((1, length, width), bf16)] * 3 + [sds((HEADS, BUCKETS), f32)]
    return call(
        enc_attn_bwd_kernel, "enc_attn_bwd", 10, args, specs, outs, [whole_spec(o) for o in outs],
        [strip, strip, pltpu.VMEM((length, width), bf16)], after=after, vmem=24,
    )


def enc_weight_grads_kernel(x_ref, small_ref, mix_ref, gh_ref, td_ref, *refs):
    *parts, dw_ref = refs
    rows, length, width = x_ref.shape
    shards = dw_ref.shape[0]
    blk = width // shards
    gain = small_ref[GAIN_ROW : GAIN_ROW + 1]
    n = normed(x_ref[...].astype(f32).reshape(rows * length, width), gain)
    for w in range(3):
        total = None
        for r in range(rows):
            new = tn(n[r * length : (r + 1) * length], parts[4 * r + w][0])
            total = new if total is None else total + new
        dw_ref[:, w * blk : (w + 1) * blk] = packed(total, shards)
    dw_ref[:, 3 * blk : 4 * blk] = packed(tn(mix_ref[...], gh_ref[...].astype(bf16)), shards)
    table = sum(parts[4 * r + 3][...] for r in range(rows))
    for s in range(shards):
        dw_ref[s, 4 * blk :] = jnp.zeros((SMALL_ROWS, width), bf16)
        dw_ref[s, 4 * blk : 4 * blk + HEADS, :BUCKETS] = table.astype(bf16)
        dw_ref[s, 4 * blk : 4 * blk + HEADS, DEC_LANE : DEC_LANE + BUCKETS] = td_ref[...].astype(bf16)


def enc_weight_grads(x, small, mix, grad_hidden, dec_grad, parts, shards, after):
    width = x.shape[-1]
    grads = sds((shards, 4 * width // shards + SMALL_ROWS, width), bf16)
    args = (x, small, mix, grad_hidden, dec_grad) + tuple(a for row in parts for a in row)
    return simple(enc_weight_grads_kernel, "enc_weight_grads", 3, args, [grads], after, vmem=24)[0]


def enc_input_grad_kernel(x_ref, small_ref, gh_ref, w_ref, *refs):
    *parts, gi_ref = refs
    rows, length, width = x_ref.shape
    gain = small_ref[GAIN_ROW : GAIN_ROW + 1]
    for r in range(rows):
        dn = sum(nt(parts[4 * r + w][0], matrix(w_ref, w)) for w in range(3))
        gi_ref[r] = gh_ref[r * length : (r + 1) * length] + norm_back(x_ref[r].astype(f32), gain, dn)


def enc_input_grad(x, small, grad_hidden, weights, parts, after):
    args = (x, small, grad_hidden, weights) + tuple(a for row in parts for a in row)
    return simple(enc_input_grad_kernel, "enc_input_grad", 4, args, [sds(x.shape, f32)], after, vmem=24)[0]


def embed_rows_kernel(me_ref, embed_ref, *refs):
    pieces, (found_ref, ids_ref) = refs[:-2], refs[-2:]
    shards, tokens, _ = found_ref.shape
    own = embed_ref.shape[0]
    me = me_ref[0]
    count = len(pieces) // 2
    row = pieces[0].shape[1] - SMALL_ROWS + ID_ROW
    for core, part in ((me, pieces[:count]), (me ^ 1, pieces[count:])):
        for p, (ref, i) in enumerate(spread(part)):
            code = ref[i, row : row + 1, :].astype(f32).astype(jnp.int32)
            ids = code[:, :tokens] * 64 + code[:, tokens : 2 * tokens]
            s = shard_at(p, core, shards)
            ids_ref[s] = ids
            found_ref[s] = tn(one_hot(ids, own, me), embed_ref[...]).astype(bf16)


def one_hot(ids, own, me):
    return (lax.broadcasted_iota(jnp.int32, (own, ids.shape[1]), 0) + me * own == ids).astype(f32).astype(bf16)


def embed_rows(me, embed, pieces, tokens, after):
    shards = sum(p.shape[0] for p in pieces)
    outs = [sds((shards, tokens, embed.shape[1]), bf16), sds((shards, 1, tokens), jnp.int32)]
    args = (embed, *pieces)
    return call(
        embed_rows_kernel, "embed_rows", 2, (me,) + args, [SCALAR] + [whole_spec(a) for a in args], outs,
        [whole_spec(o) for o in outs], after=after, vmem=10,
    )


def embed_grads_kernel(me_ref, ids_ref, *refs):
    pieces, out_ref = refs[:-1], refs[-1]
    shards = ids_ref.shape[0]
    me = me_ref[0]
    count = len(pieces) // 2
    total = jnp.zeros(out_ref.shape, f32)
    for core, part in ((me, pieces[:count]), (me ^ 1, pieces[count:])):
        for p, (ref, i) in enumerate(spread(part)):
            ids = ids_ref[shard_at(p, core, shards)]
            total = total + nn(one_hot(ids, out_ref.shape[0], me), ref[i])
    out_ref[...] = total.astype(bf16)


def embed_grads(me, ids, pieces, own, after):
    out = sds((own, pieces[0].shape[-1]), bf16)
    args = (ids, *pieces)
    return call(
        embed_grads_kernel, "embed_grads", 2, (me,) + args, [SCALAR] + [whole_spec(a) for a in args], [out],
        [whole_spec(out)], after=after, vmem=10,
    )[0]


def dec_masks(rows, steps, late, last_ref, key_major):
    tokens, keys = rows * steps, rows * late
    shape = (tokens, tokens)
    i = lax.broadcasted_iota(jnp.int32, shape, 1 if key_major else 0)
    j = lax.broadcasted_iota(jnp.int32, shape, 0 if key_major else 1)
    causal = (i // steps == j // steps) & (j <= i)
    shape = (keys, tokens) if key_major else (tokens, keys)
    i = lax.broadcasted_iota(jnp.int32, shape, 1 if key_major else 0)
    j = lax.broadcasted_iota(jnp.int32, shape, 0 if key_major else 1)
    return causal, (i // steps == j // late) & (last_ref[...] == 1)


def dec_table(small_ref):
    return small_ref[TABLE_ROW : TABLE_ROW + HEADS, DEC_LANE : DEC_LANE + BUCKETS].astype(bf16)


def dec_attn_fwd_kernel(
    emb_ref, enc_ref, last_ref, small_ref, w_ref, hot_ref,
    na_ref, qkv_ref, mixa_ref, hida_ref, nb_ref, cq_ref, ckv_ref, mixb_ref, hidb_ref, strip_ref, *, rows,
):
    tokens = emb_ref.shape[0]
    keys = enc_ref.shape[0]
    causal, allowed = dec_masks(rows, tokens // rows, keys // rows, last_ref, False)
    fill_strip(strip_ref, dec_table(small_ref), hot_ref[...], 1 - tokens)
    lane = lax.broadcasted_iota(jnp.int32, (tokens, 2 * HEAD_DIM), 1)

    def attend(q_at, k_at, v_at, bias_at, mask, mix_ref):
        for hp in range(HEADS // 2):
            ls = slice(hp * 2 * HEAD_DIM, (hp + 1) * 2 * HEAD_DIM)
            qp, kp, vp = q_at(ls), k_at(ls), v_at(ls)
            outs = []
            for sub in range(2):
                s = nt(half(lane, qp, sub), kp)
                if bias_at is not None:
                    s = s + bias_at(hp * 2 + sub)
                outs.append(nn(soft_rows(jnp.where(mask, s, MASKED)).astype(bf16), vp))
            mix_ref[:, ls] = jnp.where(lane < HEAD_DIM, outs[0], outs[1]).astype(bf16)

    emb = emb_ref[...].astype(f32)
    na_ref[...] = normed(emb, small_ref[GAIN_ROW + 2 : GAIN_ROW + 3])
    for w in range(3):
        qkv_ref[w] = nn(na_ref[...], matrix(w_ref, w)).astype(bf16)
    attend(
        lambda ls: qkv_ref[0, :, ls],
        lambda ls: qkv_ref[1, :, ls],
        lambda ls: qkv_ref[2, :, ls],
        lambda h: strip_ref[h, :, :tokens],
        causal,
        mixa_ref,
    )
    hida_ref[...] = emb + nn(mixa_ref[...], matrix(w_ref, 3))
    nb_ref[...] = normed(hida_ref[...], small_ref[GAIN_ROW + 3 : GAIN_ROW + 4])
    cq_ref[...] = nn(nb_ref[...], matrix(w_ref, 4)).astype(bf16)
    for w in range(2):
        ckv_ref[w] = nn(enc_ref[...], matrix(w_ref, 5 + w)).astype(bf16)
    attend(
        lambda ls: cq_ref[:, ls],
        lambda ls: ckv_ref[0, :, ls],
        lambda ls: ckv_ref[1, :, ls],
        None,
        allowed,
        mixb_ref,
    )
    hidb_ref[...] = hida_ref[...] + nn(mixb_ref[...], matrix(w_ref, 7))


def dec_attn_fwd(emb, enc_late, last, small, pieces, me, rows, after):
    tokens, width = emb.shape
    keys = enc_late.shape[0]
    hot = dec_hot(tokens, tokens // rows, False)
    one = sds((tokens, width), bf16)
    wide = sds((tokens, width), f32)
    full = sds((sum(p.shape[0] for p in pieces),) + pieces[0].shape[1:], bf16)
    outs = [one, sds((3, tokens, width), bf16), one, wide, one, one, sds((2, keys, width), bf16), one, wide, full]
    args = (emb, enc_late, last, small, hot, *pieces)

    def body(me_ref, emb_ref, enc_ref, last_ref, small_ref, hot_ref, *refs):
        parts, kept, w_ref, strip_ref = refs[: len(pieces)], refs[len(pieces) : -2], refs[-2], refs[-1]
        collect(w_ref, parts, me_ref[0])
        dec_attn_fwd_kernel(
            emb_ref, enc_ref, last_ref, small_ref, w_ref, hot_ref, *kept, strip_ref, rows=rows
        )

    return call(
        body, "dec_attn_fwd", 7, (me,) + args, [SCALAR] + [whole_spec(a) for a in args], outs,
        [whole_spec(o) for o in outs], [pltpu.VMEM((HEADS, tokens, 2 * tokens), f32)], after=after, vmem=24,
    )


def dec_hot(tokens, steps, reverse):
    codes = np.full(2 * tokens, -1, np.int32)
    own = bucket_codes(steps, False)
    codes[tokens - steps : tokens - steps + len(own)] = own
    if reverse:
        codes = codes[::-1]
    return jnp.asarray(codes[None, :] == np.arange(BUCKETS)[:, None], bf16)


def dec_ffn_kernel(me_ref, h_ref, small_ref, cot_ref, *refs):
    pieces, (out_ref, gh_ref, dw_ref, w_s, n_s, dn_s, o_s) = refs[:-7], refs[-7:]
    i = pl.program_id(0)
    gain = small_ref[GAIN_ROW + 4 : GAIN_ROW + 5]

    @pl.when(i == 0)
    def _():
        n_s[...] = normed(h_ref[...], gain)
        dn_s[...] = jnp.zeros_like(dn_s)
        o_s[...] = h_ref[...]

    collect(w_s, pieces, me_ref[0])
    a, wd, dn = ffn_step(n_s[...], cot_ref[...], w_s, dw_ref)
    o_s[...] += nn(a, wd)
    dn_s[...] += dn

    @pl.when(i == pl.num_programs(0) - 1)
    def _():
        out_ref[...] = o_s[...].astype(bf16)
        gh_ref[...] = cot_ref[...].astype(f32) + norm_back(h_ref[...], gain, dn_s[...])


def dec_ffn(me, h, small, cot, pieces, after):
    grads = sds((sum(p.shape[0] for p in pieces),) + pieces[0].shape[1:], bf16)
    outs = [sds(h.shape, bf16), sds(h.shape, f32), grads]
    return call(
        dec_ffn_kernel, "dec_ffn", 8, (me, h, small, cot, *pieces),
        [SCALAR, whole_spec(h), whole_spec(small), whole_spec(cot)] + [pair_spec(p) for p in pieces],
        outs, [whole_spec(outs[0]), whole_spec(outs[1]), pair_spec(grads)],
        [
            pltpu.VMEM((grads.shape[0], 2) + grads.shape[2:], bf16),
            pltpu.VMEM(h.shape, bf16),
            pltpu.VMEM(h.shape, f32),
            pltpu.VMEM(h.shape, f32),
        ],
        grid=grads.shape[1] // 2, after=after, vmem=16,
    )


def attend_back(q_at, k_at, v_at, do, bias_at, mask, take_score, dq_s, dk_s, dv_s):
    for hp in range(HEADS // 2):
        ls = slice(hp * 2 * HEAD_DIM, (hp + 1) * 2 * HEAD_DIM)
        qp, kp, vp, dop = q_at(ls), k_at(ls), v_at(ls), do[:, ls]
        lane = lax.broadcasted_iota(jnp.int32, qp.shape, 1)
        lanek = lax.broadcasted_iota(jnp.int32, kp.shape, 1)
        dq = dk = dv = None
        for sub in range(2):
            qm, km, dom = half(lane, qp, sub), half(lanek, kp, sub), half(lane, dop, sub)
            s = nt(kp, qm)
            if bias_at is not None:
                s = s + bias_at(hp * 2 + sub)
            p = soft_columns(jnp.where(mask, s, MASKED))
            dp = nt(vp, dom)
            ds = (p * (dp - jnp.sum(dp * p, axis=0, keepdims=True))).astype(bf16)
            new = (tn(ds, km), nn(ds, qm), nn(p.astype(bf16), dom))
            dq, dk, dv = new if dq is None else (dq + new[0], dk + new[1], dv + new[2])
            if take_score is not None:
                take_score(hp * 2 + sub, ds)
        dq_s[:, ls] = dq.astype(bf16)
        dk_s[:, ls] = dk.astype(bf16)
        dv_s[:, ls] = dv.astype(bf16)


def dec_cross_bwd_kernel(
    gb_ref, enc_ref, last_ref, small_ref, w_ref, hida_ref, nb_ref, cq_ref, ckv_ref, mixb_ref,
    gm_ref, ga_ref, dw_ref, dq_s, dk_s, dv_s, *, rows,
):
    tokens = gb_ref.shape[0]
    keys = enc_ref.shape[0]
    shards = dw_ref.shape[0]
    _, allowed = dec_masks(rows, tokens // rows, keys // rows, last_ref, True)
    grad_b = gb_ref[...]
    branch = grad_b.astype(bf16)
    dw_ref[:, 3] = packed(tn(mixb_ref[...], branch), shards)
    do = nt(branch, matrix(w_ref, 7)).astype(bf16)
    attend_back(
        lambda ls: cq_ref[:, ls],
        lambda ls: ckv_ref[0, :, ls],
        lambda ls: ckv_ref[1, :, ls],
        do,
        None,
        allowed,
        None,
        dq_s,
        dk_s,
        dv_s,
    )
    gm_ref[...] = nt(dk_s[...], matrix(w_ref, 5)) + nt(dv_s[...], matrix(w_ref, 6))
    dw_ref[:, 0] = packed(tn(nb_ref[...], dq_s[...]), shards)
    dw_ref[:, 1] = packed(tn(enc_ref[...], dk_s[...]), shards)
    dw_ref[:, 2] = packed(tn(enc_ref[...], dv_s[...]), shards)
    gain = small_ref[GAIN_ROW + 3 : GAIN_ROW + 4]
    ga_ref[...] = grad_b + norm_back(hida_ref[...], gain, nt(dq_s[...], matrix(w_ref, 4)))


def dec_cross_bwd(grad_b, enc_late, last, small, weights, kept, rows, after):
    tokens, width = grad_b.shape
    keys = enc_late.shape[0]
    _, _, _, hida, nb, cq, ckv, mixb, _ = kept
    shards, _, blk, _ = weights.shape
    outs = [sds((keys, width), f32), sds((tokens, width), f32), sds((shards, 4, blk, width), bf16)]
    args = (grad_b, enc_late, last, small, weights, hida, nb, cq, ckv, mixb)
    return simple(
        functools.partial(dec_cross_bwd_kernel, rows=rows), "dec_cross_bwd", 6, args, outs, after,
        [pltpu.VMEM((tokens, width), bf16), pltpu.VMEM((keys, width), bf16), pltpu.VMEM((keys, width), bf16)], vmem=24,
    )


def dec_self_bwd_kernel(
    ga_ref, emb_ref, small_ref, w_ref, hot_ref, na_ref, qkv_ref, mixa_ref,
    gr_ref, dt_ref, dw_ref, strip_ref, acc_ref, dq_s, dk_s, dv_s, *, rows,
):
    tokens = emb_ref.shape[0]
    shards = dw_ref.shape[0]
    steps = tokens // rows
    i = lax.broadcasted_iota(jnp.int32, (tokens, tokens), 1)
    j = lax.broadcasted_iota(jnp.int32, (tokens, tokens), 0)
    causal = (i // steps == j // steps) & (j <= i)
    fill_strip(strip_ref, dec_table(small_ref), hot_ref[...], -tokens)
    grad_a = ga_ref[...]
    branch = grad_a.astype(bf16)
    dw_ref[:, 3] = packed(tn(mixa_ref[...], branch), shards)
    do = nt(branch, matrix(w_ref, 3)).astype(bf16)
    acc_ref[...] = jnp.zeros_like(acc_ref)

    def take_score(h, ds):
        acc_ref[h, :, :tokens] = ds.astype(f32)

    attend_back(
        lambda ls: qkv_ref[0, :, ls],
        lambda ls: qkv_ref[1, :, ls],
        lambda ls: qkv_ref[2, :, ls],
        do,
        lambda h: strip_ref[h, :, :tokens],
        causal,
        take_score,
        dq_s,
        dk_s,
        dv_s,
    )
    parts = (dq_s[...], dk_s[...], dv_s[...])
    dn = nt(parts[0], matrix(w_ref, 0)) + nt(parts[1], matrix(w_ref, 1)) + nt(parts[2], matrix(w_ref, 2))
    for w in range(3):
        dw_ref[:, w] = packed(tn(na_ref[...], parts[w]), shards)
    gain = small_ref[GAIN_ROW + 2 : GAIN_ROW + 3]
    gr_ref[0] = (grad_a + norm_back(emb_ref[...].astype(f32), gain, dn)).astype(bf16)
    dt_ref[...] = strip_sums(acc_ref[...], hot_ref[...])


def dec_self_bwd(grad_a, emb, small, weights, kept, rows, after):
    tokens, width = emb.shape
    shards, _, blk, _ = weights.shape
    na, qkv, mixa = kept[:3]
    hot = dec_hot(tokens, tokens // rows, True)
    outs = [sds((1, tokens, width), bf16), sds((HEADS, BUCKETS), f32), sds((shards, 4, blk, width), bf16)]
    args = (grad_a, emb, small, weights, hot, na, qkv, mixa)
    strip = pltpu.VMEM((HEADS, tokens, 2 * tokens), f32)
    return simple(
        functools.partial(dec_self_bwd_kernel, rows=rows), "dec_self_bwd", 4, args, outs, after,
        [strip, strip] + [pltpu.VMEM((tokens, width), bf16)] * 3, vmem=24,
    )


def exchange(value, shards, even_bit, odd_bit):
    pairs = [(i, i ^ (1 << (odd_bit if i & 1 else even_bit))) for i in range(shards)]
    return lax.ppermute(value, "fsdp", pairs)


def swap_cores(value, shards):
    return exchange(value, shards, 0, 0)


def round_of(value, j, shards):
    upper = shards.bit_length() - 2
    return exchange(value, shards, 1 + j, upper - j)


class Gather:
    def __init__(self, block, shards):
        self.shards = shards
        self.upper = shards.bit_length() - 2
        self.block = block
        if self.upper == 2:
            self.one, self.two = round_of(block, 0, shards), round_of(block, 1, shards)
            self.swapped = [swap_cores(block, shards)]
        else:
            self.one = round_of(block, self.upper - 1, shards)

    def forward(self, after):
        if self.upper == 2:
            passed = gate(self.one, after)
            self.far = round_of(passed, 1, self.shards)
            self.pieces = [self.block, self.two, passed, self.far]
            self.swapped += [swap_cores(p, self.shards) for p in self.pieces[1:3]]
            return passed
        held = join(self.block, self.one, after)
        for j in reversed(range(self.upper - 1)):
            held = join(held, round_of(held, j, self.shards), ())
        self.pieces = [held]
        self.swapped = []
        return held

    def finish(self):
        return self.pieces + self.swapped + [swap_cores(self.pieces[-1], self.shards)]


class Sum:
    def __init__(self, me, groups, short=False):
        self.me, self.shards, self.short, self.line = me, groups[0].shape[0], short, None
        self.groups = [(g, swap_cores(g, self.shards)) for g in groups]
        self.upper = self.shards.bit_length() - 2
        self.size = lax.axis_size("dp")
        self.step = -1

    def include(self, group):
        self.groups.append((group, swap_cores(group, self.shards)))

    def done(self):
        return self.line is not None and self.line.done()

    def advance(self, after):
        if self.done():
            return after[0]
        if self.step < 0:
            self.keep, send = add_first(self.me, self.groups, after)
        elif self.step < self.upper - 1:
            self.keep, send = add_halves(self.keep, self.flight, after)
        else:
            if self.step == self.upper - 1:
                self.keep = add(self.keep, self.flight, after)[0]
                self.line = Line(self.keep, self.size, self.short)
            else:
                self.keep = self.line.advance(after)
            self.step += 1
            return self.keep
        self.step += 1
        self.flight = round_of(send, self.step, self.shards)
        return self.keep


class Line:
    def __init__(self, value, size, short=False):
        self.value, self.size = value, size
        self.short = short or size != 4
        self.step = 0
        self.start()

    def start(self):
        if self.short:
            pairs = [(i, i ^ (1 << self.step)) for i in range(self.size)]
        else:
            pairs = ([(0, 1), (3, 2)], [(1, 2), (2, 1)], [(1, 0), (2, 3)])[self.step]
        self.flight = lax.ppermute(self.value, "dp", pairs)

    def rounds(self):
        return self.size.bit_length() - 1 if self.short else 3

    def done(self):
        return self.step >= self.rounds()

    def advance(self, after):
        if self.done():
            return after[0]
        if self.short or self.step < 2:
            self.value = add(self.value, self.flight, after)
        else:
            inner = ((lax.axis_index("dp") + 1) // 2 % 2).astype(jnp.int32).reshape(1)
            self.value = pick(inner, self.value, self.flight, after)
        self.step += 1
        if not self.done():
            self.start()
        return self.value


def pick_kernel(inner_ref, a_ref, b_ref, o_ref):
    @pl.when(inner_ref[0] == 1)
    def _():
        o_ref[...] = a_ref[...]

    @pl.when(inner_ref[0] == 0)
    def _():
        o_ref[...] = b_ref[...]


def pick(inner, a, b, after):
    size = 1 + 6 * np.prod(a.shape) * a.dtype.itemsize / 2**20
    return call(
        pick_kernel, "pick", 0.7, (inner, a, b), [SCALAR, whole_spec(a), whole_spec(b)], [a], [whole_spec(a)],
        after=after, vmem=size,
    )[0]


def unpack_ffn_kernel(sum_ref, up_ref, down_ref, *, shards):
    blocks = sum_ref.shape[0] // 2
    blk = up_ref.shape[0]
    for b in range(blocks):
        up = sum_ref[2 * b].astype(f32)
        for c in range(shards):
            up_ref[:, (c * blocks + b) * blk : (c * blocks + b + 1) * blk] = up[:, c * blk : (c + 1) * blk]
        down_ref[b * blk : (b + 1) * blk] = sum_ref[2 * b + 1].astype(f32)


def unpack_ffn(a, shards, after=()):
    count, blk, width = a.shape
    outs = [sds((blk, count // 2 * width), f32), sds((count // 2 * blk, width), f32)]
    return simple(functools.partial(unpack_ffn_kernel, shards=shards), "unpack_ffn", 1.5, (a,), outs, after)


def on_device(
    enc_input,
    segments,
    targets,
    enc_cot,
    dec_cot,
    enc_gains,
    enc_attn,
    enc_table,
    enc_up,
    enc_down,
    embed,
    dec_gains,
    dec_self,
    dec_cross,
    dec_table,
    dec_up,
    dec_down,
):
    rows, length, width = enc_input.shape
    steps = targets.shape[1]
    tokens = rows * steps
    shards = lax.axis_size("fsdp")
    blk = enc_attn.shape[1]
    own = embed.shape[0]
    index = lax.axis_index("fsdp").astype(jnp.int32)
    me = index.reshape(1)
    late = min(length, SERIES_MOST)
    flat = lambda a: a.reshape(-1, width)
    segc, segr = segments[:, :, None], segments[:, None, :]

    first = pack_first(me, enc_attn, enc_gains, dec_gains, enc_table, dec_table, targets, shards)
    a = Gather(first, shards)
    b = Gather(pack_ffn(enc_up, enc_down, shards, (a.forward((a.two,)) if a.upper == 2 else a.forward(()),)), shards)
    a_pieces = a.finish()
    found, ids = embed_rows(me, embed, a_pieces, tokens, (b.block,))
    e = Sum(me, [found])
    mark = b.forward((found,))
    c = Gather(pack_attn(dec_self, dec_cross, (mark,)), shards)
    hidden, q, k, v, mix, w_attn, small = enc_attn_fwd(me, enc_input, segc, segr, a_pieces, (c.block,))
    hidden = flat(hidden)

    b_pieces = b.finish()
    mark = e.advance((hidden,))
    d = Gather(pack_ffn(dec_up, dec_down, shards, (mark,)), shards)
    enc_out, w_ffn = enc_ffn_fwd(me, hidden, small, b_pieces, (d.block,))
    mark = c.forward((e.advance((enc_out,)),))
    mark = d.forward((mark,))
    enc_out = enc_out.reshape(rows, length, width)
    enc_late = flat(enc_out[:, length - late :])
    last = (segments == segments[:, -1:])[:, length - late :].astype(jnp.int32).reshape(1, -1)
    while e.step < e.upper - 1:
        mark = e.advance((mark,))
    emb = add(e.keep, e.flight, (mark,))[0]
    kept = dec_attn_fwd(emb, enc_late, last, small, c.finish(), me, rows, ())
    kept, w_dec = kept[:-1], kept[-1]
    dec_out, grad_b, g_dffn = dec_ffn(me, kept[-1], small, flat(dec_cot), d.finish(), ())

    r1 = Sum(me, [g_dffn])
    grad_late, grad_a, g_cross = dec_cross_bwd(grad_b, enc_late, last.reshape(-1, 1), small, w_dec, kept, rows, ())
    r2 = Sum(me, [g_cross])
    grad_rows, d_dtab, g_self = dec_self_bwd(grad_a, emb, small, w_dec, kept, rows, ())
    mark = r1.advance((grad_rows,))
    r2.include(g_self)
    f = Gather(grad_rows, shards)
    grad_memory, dn, g_ffn = enc_ffn_bwd_first(
        hidden, small, w_ffn, enc_cot, grad_late.reshape(rows, late, width), (mark,)
    )
    mark = r2.advance((r1.advance((dn,)),))
    mark = f.forward((mark,))
    r3 = Sum(me, [g_ffn])
    grad_hidden, g_ffn = enc_ffn_bwd_next(hidden, small, w_ffn, grad_memory, dn, (mark,))
    mark = r2.advance((r1.advance((grad_hidden,)),))
    mark = r3.advance((mark,))
    r4 = Sum(me, [g_ffn])
    three = grad_hidden.reshape(rows, length, width)
    parts = [enc_attn_bwd(0, three, q, k, v, segc, segr, w_attn, small, (mark,))]
    mark = parts[0][3]
    for r in (r1, r2, r3, r4):
        mark = r.advance((mark,))
    g_embed = embed_grads(me, ids, f.finish(), own, (mark,))
    r5 = Line(g_embed, lax.axis_size("dp"))
    mark = g_embed
    for row in range(1, rows):
        parts.append(enc_attn_bwd(row, three, q, k, v, segc, segr, w_attn, small, (mark,)))
        mark = parts[-1][3]
    for r in (r1, r2, r3, r4, r5):
        mark = r.advance((mark,))
    g_attn = enc_weight_grads(enc_input, small, flat(mix), grad_hidden, d_dtab, parts, shards, (mark,))
    r6 = Sum(me, [g_attn], short=True)
    grad_input = enc_input_grad(enc_input, small, grad_hidden, w_attn, parts, (g_attn,))
    mark = r6.advance((grad_input,))
    while not r6.done():
        for r in (r4, r3, r2, r1, r5, r6):
            mark = r.advance((mark,))
    for r in (r1, r2, r3, r4, r5):
        while not r.done():
            mark = r.advance((mark,))
    s_dup, s_ddown = unpack_ffn(r1.keep, shards)
    s_up, s_down = unpack_ffn(jnp.concatenate([r3.keep, r4.keep], axis=0), shards)
    s_attn = r6.keep.astype(f32)
    tabs = s_attn[4 * blk :]
    per = enc_table.shape[0]
    entries = lambda lane: lax.dynamic_slice(
        tabs[:HEADS, lane : lane + BUCKETS].reshape(-1), (index * per,), (per,)
    )
    s_attn = s_attn[: 4 * blk].reshape(4, blk, width)
    s_dec = r2.keep.astype(f32)

    def gain_grad(weights, sums, gain):
        axes = (0, 2) if weights.ndim == 3 else 1
        return jnp.sum(weights.astype(f32) * sums, axis=axes) / gain.astype(f32)

    return (
        enc_out,
        dec_out.reshape(rows, steps, width),
        grad_input,
        grad_memory,
        jnp.stack([gain_grad(enc_attn[:3], s_attn[:3], enc_gains[0]), gain_grad(enc_up, s_up, enc_gains[1])]),
        s_attn,
        entries(0),
        s_up,
        s_down,
        r5.value.astype(f32),
        jnp.stack(
            [
                gain_grad(dec_self[:3], s_dec[4:7], dec_gains[0]),
                gain_grad(dec_cross[0], s_dec[0], dec_gains[1]),
                gain_grad(dec_up, s_dup, dec_gains[2]),
            ]
        ),
        s_dec[4:],
        s_dec[:4],
        entries(DEC_LANE),
        s_dup,
        s_ddown,
    )


def solution(mesh):
    placed = (
        P(("fsdp", "dp"), None, None),
        P(("fsdp", "dp"), None),
        P(("fsdp", "dp"), None),
        P(("fsdp", "dp"), None, None),
        P(("fsdp", "dp"), None, None),
        P(None, "fsdp"),
        P(None, "fsdp", None),
        P("fsdp"),
        P("fsdp", None),
        P("fsdp", None),
        P("fsdp", None),
        P(None, "fsdp"),
        P(None, "fsdp", None),
        P(None, "fsdp", None),
        P("fsdp"),
        P("fsdp", None),
        P("fsdp", None),
    )
    return jax.shard_map(
        on_device,
        mesh=mesh,
        in_specs=placed,
        out_specs=(
            P(("fsdp", "dp"), None, None),
            P(("fsdp", "dp"), None, None),
            P(("fsdp", "dp"), None, None),
            P(("fsdp", "dp"), None, None),
            P(None, "fsdp"),
            P(None, "fsdp", None),
            P("fsdp"),
            P("fsdp", None),
            P("fsdp", None),
            P("fsdp", None),
            P(None, "fsdp"),
            P(None, "fsdp", None),
            P(None, "fsdp", None),
            P("fsdp"),
            P("fsdp", None),
            P("fsdp", None),
        ),
        check_vma=False,
    )
```

```python
import functools

import jax
import jax.numpy as jnp
import numpy as np
from jax import lax
from jax.experimental import pallas as pl
from jax.experimental.pallas import tpu as pltpu
from jax.sharding import PartitionSpec as P

HEADS = 8
HEAD_DIM = 64
BUCKETS = 32
SERIES_MOST = 256
TILE = 128
MASKED = -1000000000.0

epsilon = 1e-06
f32 = jnp.float32
bf16 = jnp.bfloat16
PEAK = 1.15e9

WEIGHT = 1

VMEM = {
    "pack_first": 4,
    "enc_attn_fwd": 24,
    "enc_ffn_fwd": 20,
    "enc_ffn_bwd": 24,
    "enc_attn_bwd": 24,
    "enc_weight_grads": 16,
    "enc_input_grad": 20,
    "embed_rows": 8,
    "embed_grads": 8,
    "dec_attn_fwd": 20,
    "dec_ffn": 16,
    "dec_cross_bwd": 20,
    "dec_self_bwd": 16,
}

TABLE_ROW = 0
GAIN_ROW = 8
ID_ROW = 13
SMALL_ROWS = 16
DEC_LANE = 128


def bucket_codes(length, both_ways):
    bucket_list = []
    for offset in range(-(length - 1), length):
        if both_ways:
            upper_half = 16 if offset > 0 else 0
            distance = abs(offset)
            if distance < 8:
                bucket = distance
            else:
                bucket = 8 + sum(
                    (1 for exponent in range(1, 8) if distance * distance >= 64 * 2**exponent)
                )
        else:
            upper_half = 0
            distance = max(-offset, 0)
            if distance < 16:
                bucket = distance
            else:
                bucket = 16 + sum(
                    (1 for exponent in range(1, 16) if distance**16 >= 16**16 * 2 ** (3 * exponent))
                )
        bucket_list.append(upper_half + bucket)
    return np.array(bucket_list, dtype=np.int32)


def offset_hot(length, both_ways, reverse):
    codes = np.concatenate([bucket_codes(length, both_ways), [-1]])
    if reverse:
        codes = codes[::-1]
    return jnp.asarray(codes[None, :] == np.arange(BUCKETS)[:, None], bf16)


def nn(a, b):
    return lax.dot_general(a, b, (((1,), (0,)), ((), ())), preferred_element_type=f32)


def nt(a, b):
    return lax.dot_general(a, b, (((1,), (1,)), ((), ())), preferred_element_type=f32)


def tn(a, b):
    return lax.dot_general(a, b, (((0,), (0,)), ((), ())), preferred_element_type=f32)


def rho_of(h):
    return lax.rsqrt(jnp.mean(h * h, axis=-1, keepdims=True) + epsilon)


def normed(h, gain):
    return (h * rho_of(h) * gain.astype(f32)).astype(bf16)


def norm_back(h, gain, dn):
    rho = rho_of(h)
    xh = h * rho
    gu = dn * gain.astype(f32)
    return rho * (gu - xh * jnp.mean(gu * xh, axis=-1, keepdims=True))


def gelu(u):
    t = jnp.tanh(np.float32(np.sqrt(2 / np.pi)) * (u + 0.044715 * (u * u * u)))
    return 0.5 * u * (1.0 + t)


def gelu_both(u):
    c = np.float32(np.sqrt(2 / np.pi))
    u2 = u * u
    t = jnp.tanh(c * (u + 0.044715 * (u2 * u)))
    cdf = 0.5 * (1.0 + t)
    return u * cdf, cdf + 0.5 * u * (1.0 - t * t) * (c + (3 * 0.044715 * c) * u2)


def matrix(ref, w):
    part = ref[:, w]
    return part.reshape(part.shape[0] * part.shape[1], part.shape[2])


def packed(value, shards):
    return value.reshape(shards, value.shape[0] // shards, value.shape[1]).astype(bf16)


def place(shard, me, shards):
    upper = shards.bit_length() - 2
    diff = shard ^ me
    spot = 0
    for j in range(upper):
        even = (diff >> (1 + j)) & 1
        odd = (diff >> (upper - j)) & 1
        spot = spot | (jnp.where((shard & 1) == 0, even, odd) << (upper - 1 - j))
    return spot


def shard_at(spot, me, shards):
    upper = shards.bit_length() - 2
    diff_even = diff_odd = 0
    for j in range(upper):
        bit = (spot >> (upper - 1 - j)) & 1
        diff_even = diff_even | (bit << (1 + j))
        diff_odd = diff_odd | (bit << (upper - j))
    return me ^ jnp.where((me & 1) == 0, diff_even, diff_odd)


def spread(refs):
    return [(ref, i) for ref in refs for i in range(ref.shape[0])]


def collect(out_ref, refs, me, rows=None):
    shards = out_ref.shape[0]
    count = len(refs) // 2
    for core, part in ((me, refs[:count]), (me ^ 1, refs[count:])):
        for p, (ref, i) in enumerate(spread(part)):
            piece = ref[i] if rows is None else ref[i, :rows]
            out_ref[shard_at(p, core, shards)] = piece.reshape(out_ref.shape[1:])


SCALAR = pl.BlockSpec(memory_space=pltpu.SMEM)
ANYWHERE = pl.BlockSpec(memory_space=pl.ANY)
sds = jax.ShapeDtypeStruct


def far(shape, dtype):
    return pltpu.HBM(shape, dtype)


def stay(arrays):
    return [pltpu.with_memory_space_constraint(a, pltpu.HBM) for a in arrays]


def whole_spec(a):
    zeros = (0,) * len(a.shape)
    return pl.BlockSpec(a.shape, lambda i: zeros)


def call(kernel, name, us, args, in_specs, outs, out_specs, scratch=(), grid=1, after=(), vmem=None, distant=()):
    waits = len(after)

    def body(*refs):
        kernel(*refs[waits:])

    return pl.pallas_call(
        body,
        grid=(grid,),
        in_specs=[ANYWHERE] * waits + list(in_specs),
        out_specs=list(out_specs),
        out_shape=[far(o.shape, o.dtype) if i in distant else sds(o.shape, o.dtype) for i, o in enumerate(outs)],
        scratch_shapes=list(scratch),
        compiler_params=pltpu.CompilerParams(vmem_limit_bytes=int(VMEM.get(name, vmem) * 2**20)),
        cost_estimate=pl.CostEstimate(flops=int(us * PEAK * (4 if us >= 3 else 0.3)), bytes_accessed=1024, transcendentals=0),
        name=name,
    )(*after, *args)


def simple(kernel, name, us, args, outs, after=(), scratch=(), vmem=None, distant=()):
    if vmem is None:
        vmem = 1 + sum(2 * np.prod(a.shape) * a.dtype.itemsize for a in (*args, *outs)) / 2**20
    return call(
        kernel, name, us, args, [whole_spec(a) for a in args], outs, [whole_spec(o) for o in outs], scratch,
        after=after, vmem=vmem, distant=distant,
    )


def half(lane, value, which):
    return jnp.where((lane // HEAD_DIM) == which, value, jnp.zeros_like(value))


def fill_strip(strip_ref, table, hot, shift):
    vec = nn(table, hot)
    width = hot.shape[1]
    rows = strip_ref.shape[1]
    for h in range(HEADS):
        row = jnp.broadcast_to(vec[h : h + 1], (rows, width))
        strip_ref[h] = pltpu.roll(row, (width + shift) % width, 1, stride=1, stride_axis=0)


def strip_sums(acc, hot):
    rows, width = acc.shape[1], acc.shape[2]
    total = jnp.zeros((HEADS, 8, width), f32)
    for g in range(rows // 8):
        part = acc[:, g * 8 : g * 8 + 8, :].reshape(HEADS * 8, width)
        if g:
            part = pltpu.roll(part, width - 8 * g, 1)
        total = total + part.reshape(HEADS, 8, width)
    flat = total.reshape(HEADS * 8, width)
    sub = lax.broadcasted_iota(jnp.int32, flat.shape, 0) % 8
    for b in range(3):
        flat = jnp.where((sub >> b) & 1 == 1, pltpu.roll(flat, width - (1 << b), 1), flat)
    diag = pltpu.roll(jnp.sum(flat.reshape(HEADS, 8, width), axis=1), rows, 1)
    return lax.dot_general(
        diag,
        hot.astype(f32),
        (((1,), (1,)), ((), ())),
        precision=lax.Precision.HIGHEST,
        preferred_element_type=f32,
    )


def soft_rows(s):
    e = jnp.exp(s - jnp.max(s, axis=-1, keepdims=True))
    return e * (1.0 / jnp.sum(e, axis=-1, keepdims=True))


def soft_columns(s):
    e = jnp.exp(s - jnp.max(s, axis=0, keepdims=True))
    return e * (1.0 / jnp.sum(e, axis=0, keepdims=True))


def pack_first_kernel(me_ref, attn_ref, eg_ref, dg_ref, et_ref, dt_ref, tok_ref, out_ref, *, shards):
    count, blk, width = attn_ref.shape
    me = me_ref[0]
    out_ref[: count * blk] = attn_ref[...].reshape(count * blk, width)
    base = count * blk
    lane = lax.broadcasted_iota(jnp.int32, (1, width), 1)
    here = (lane // blk) == me
    per = et_ref.shape[1]
    row8 = lax.broadcasted_iota(jnp.int32, (HEADS, BUCKETS), 0)
    lane8 = lax.broadcasted_iota(jnp.int32, (HEADS, BUCKETS), 1)
    held = (row8 * BUCKETS + lane8) // per == me
    small = jnp.zeros((SMALL_ROWS, width), f32)
    rows = lax.broadcasted_iota(jnp.int32, (SMALL_ROWS, width), 0)
    gains = [eg_ref[i : i + 1] for i in range(eg_ref.shape[0])] + [dg_ref[i : i + 1] for i in range(dg_ref.shape[0])]
    for i, g in enumerate(gains):
        wide = jnp.where(here, jnp.concatenate([g.astype(f32)] * shards, axis=1), 0.0)
        small = jnp.where(rows == GAIN_ROW + i, jnp.broadcast_to(wide, small.shape), small)
    tok = tok_ref[...]
    steps = tok.shape[1]
    first = lax.broadcasted_iota(jnp.int32, tok.shape, 1) == 0
    shifted = jnp.where(first, 0, pltpu.roll(tok, 1, 1) if steps % 128 == 0 else jnp.concatenate([tok[:, -1:], tok[:, :-1]], axis=1))
    parts = [(shifted[r : r + 1] >> 6).astype(f32) for r in range(tok.shape[0])]
    parts += [(shifted[r : r + 1] & 63).astype(f32) for r in range(tok.shape[0])]
    ids = jnp.concatenate(parts, axis=1)
    ids = jnp.concatenate([ids, jnp.zeros((1, width - ids.shape[1]), f32)], axis=1)
    small = jnp.where(rows == ID_ROW, jnp.broadcast_to(ids, small.shape), small)
    out_ref[base:] = small.astype(bf16)
    for t_ref, at in ((et_ref, 0), (dt_ref, DEC_LANE)):
        table = jnp.concatenate([t_ref[...].astype(f32)] * (BUCKETS // per), axis=1)
        table = jnp.where(held, jnp.broadcast_to(table, held.shape), 0.0)
        out_ref[base : base + HEADS, at : at + BUCKETS] = table.astype(bf16)


def pack_first(me, attn, enc_gains, dec_gains, enc_table, dec_table, targets, shards):
    count, blk, width = attn.shape
    out = sds((1, count * blk + SMALL_ROWS, width), bf16)
    args = stay((attn, enc_gains, dec_gains, enc_table.reshape(1, -1), dec_table.reshape(1, -1), targets))

    def body(me_ref, *refs):
        pack_first_kernel(me_ref, *refs[:-1], refs[-1].at[0], shards=shards)

    return call(
        body, "pack_first", 2, (me, *args), [SCALAR] + [whole_spec(a) for a in args], [out], [whole_spec(out)]
    )[0]


def pack_ffn_kernel(up_ref, down_ref, out_ref, *, shards):
    blocks = out_ref.shape[0] // 2
    blk = up_ref.shape[0]
    for b in range(blocks):
        parts = [up_ref[:, (c * blocks + b) * blk : (c * blocks + b + 1) * blk] for c in range(shards)]
        out_ref[2 * b] = jnp.concatenate(parts, axis=1)
        out_ref[2 * b + 1] = down_ref[b * blk : (b + 1) * blk]


def pack_ffn(up, down, shards, after):
    blk, width = up.shape[0], down.shape[1]
    out = sds((1, 2 * up.shape[1] // width, blk, width), bf16)

    def body(up_ref, down_ref, out_ref):
        pack_ffn_kernel(up_ref, down_ref, out_ref.at[0], shards=shards)

    return simple(body, "pack_ffn", 1, stay((up, down)), [out], after)[0]


def pack_attn_kernel(a_ref, b_ref, out_ref):
    count = a_ref.shape[0]
    out_ref[0, :count] = a_ref[...]
    out_ref[0, count:] = b_ref[...]


def pack_attn(a, b, after):
    out = sds((1, 2 * a.shape[0]) + a.shape[1:], bf16)
    return simple(pack_attn_kernel, "pack_attn", 1, stay((a, b)), [out], after)[0]


def gate_kernel(a_ref, o_ref):
    o_ref[...] = a_ref[...]


def gate(a, after, us=0.5):
    return simple(gate_kernel, "gate", us, (a,), [a], after)[0]


def join_kernel(a_ref, b_ref, o_ref):
    size = a_ref.shape[0]
    o_ref[:size] = a_ref[...]
    o_ref[size:] = b_ref[...]


def join(a, b, after):
    return simple(join_kernel, "join", 1, (a, b), [sds((2 * a.shape[0],) + a.shape[1:], a.dtype)], after)[0]


def add_first_kernel(me_ref, *refs):
    *parts, keep_ref, send_ref = refs
    quarter = keep_ref.shape[0]
    shards = 4 * quarter
    at = 0
    for a_ref, b_ref in zip(parts[::2], parts[1::2]):
        size = a_ref.shape[1]
        for p in range(2 * quarter):
            s = shard_at(p, me_ref[0], shards)
            out_ref = keep_ref if p < quarter else send_ref
            total = a_ref[s].astype(f32) + b_ref[s].astype(f32)
            out_ref[p % quarter, at : at + size] = total.astype(bf16)
        at += size


def add_first(me, pairs, after, us=2):
    shards = pairs[0][0].shape[0]
    args = [a for pair in pairs for a in pair]
    size = sum(grads.shape[1] for grads, _ in pairs)
    out = sds((shards // 4, size) + pairs[0][0].shape[2:], bf16)
    limit = 1 + 2 * sum(np.prod(a.shape) * 2 for a in args) / 2**20
    return call(
        add_first_kernel, "add_first", us, (me, *args), [SCALAR] + [whole_spec(a) for a in args],
        [out] * 2, [whole_spec(out)] * 2, after=after, vmem=limit,
    )


def add_halves_kernel(a_ref, b_ref, keep_ref, send_ref):
    mid = keep_ref.shape[0]
    keep_ref[...] = (a_ref[:mid].astype(f32) + b_ref[:mid].astype(f32)).astype(bf16)
    send_ref[...] = (a_ref[mid:].astype(f32) + b_ref[mid:].astype(f32)).astype(bf16)


def add_halves(a, b, after):
    out = sds((a.shape[0] // 2,) + a.shape[1:], bf16)
    return simple(add_halves_kernel, "add_halves", 1, (a, b), [out] * 2, after)


def add_kernel(a_ref, b_ref, o_ref):
    o_ref[...] = (a_ref[...].astype(f32) + b_ref[...].astype(f32)).astype(o_ref.dtype)


def add(a, b, after, dtype=bf16):
    return simple(add_kernel, "add", 0.7, (a, b), [sds(a.shape, dtype)], after)[0]


def enc_attn_fwd_kernel(me_ref, x_ref, segc_ref, segr_ref, hot_ref, *refs):
    pieces, (hid_ref, q_ref, k_ref, v_ref, mix_ref, w_ref, small_ref, strip_ref) = refs[:-8], refs[-8:]
    rows, length, _ = x_ref.shape
    blocks = length // TILE
    own = pieces[0].shape[1] - SMALL_ROWS
    collect(w_ref, pieces, me_ref[0], own)
    small = jnp.zeros(small_ref.shape, f32)
    for ref, i in spread(pieces):
        small = small + ref[i, own:].astype(f32)
    small_ref[...] = small
    table = small[TABLE_ROW : TABLE_ROW + HEADS, :BUCKETS].astype(bf16)
    fill_strip(strip_ref, table, hot_ref[...], 1 - TILE)
    lane = lax.broadcasted_iota(jnp.int32, (length, 2 * HEAD_DIM), 1)

    @pl.loop(0, rows)
    def _(r):
        here = pl.ds(r * length, length)
        x = x_ref[r].astype(f32)
        n = normed(x, small_ref[GAIN_ROW : GAIN_ROW + 1])
        q_ref[r] = nn(n, matrix(w_ref, 0)).astype(bf16)
        k_ref[r] = nn(n, matrix(w_ref, 1)).astype(bf16)
        v_ref[r] = nn(n, matrix(w_ref, 2)).astype(bf16)
        same = segc_ref[r] == segr_ref[r]
        for hp in range(HEADS // 2):
            ls = slice(hp * 2 * HEAD_DIM, (hp + 1) * 2 * HEAD_DIM)
            qp, kp, vp = q_ref[r, :, ls], k_ref[r, :, ls], v_ref[r, :, ls]
            outs = []
            for sub in range(2):
                s = nt(half(lane, qp, sub), kp)
                starts = [(blocks - 1 - b) * TILE for b in range(blocks)]
                bias = [strip_ref[hp * 2 + sub, :, c : c + length] for c in starts]
                s = jnp.where(same, s + jnp.concatenate(bias, axis=0), MASKED)
                outs.append(nn(soft_rows(s).astype(bf16), vp))
            mix_ref[here, ls] = jnp.where(lane < HEAD_DIM, outs[0], outs[1]).astype(bf16)
        hid_ref[here] = x + nn(mix_ref[here], matrix(w_ref, 3))


def enc_attn_fwd(me, x, segc, segr, pieces, after):
    rows, length, width = x.shape
    shards = sum(p.shape[0] for p in pieces)
    hot = offset_hot(length, True, False)
    flat = (rows * length, width)
    outs = [sds(flat, f32)] + [sds(x.shape, bf16)] * 3 + [sds(flat, bf16)]
    outs += [sds((shards, 4, width // shards, width), bf16), sds((SMALL_ROWS, width), f32)]
    args = [me, x, segc, segr, hot] + list(pieces)
    return call(
        enc_attn_fwd_kernel, "enc_attn_fwd", 14, args, [SCALAR] + [whole_spec(a) for a in args[1:]],
        outs, [whole_spec(o) for o in outs], [pltpu.VMEM((HEADS, TILE, 2 * length), f32)], after=after,
    )


def enc_ffn_fwd_kernel(me_ref, h_ref, small_ref, *refs):
    pieces, (o_ref, w_ref, acc_s) = refs[:-3], refs[-3:]
    collect(w_ref, pieces, me_ref[0])
    n = normed(h_ref[...], small_ref[GAIN_ROW + 1 : GAIN_ROW + 2])
    for i in range(w_ref.shape[1] // 2):
        a = gelu(nn(n, matrix(w_ref, 2 * i))).astype(bf16)
        acc_s[...] = (h_ref[...] if i == 0 else acc_s[...]) + nn(a, matrix(w_ref, 2 * i + 1))
    o_ref[...] = acc_s[...].astype(bf16)


def enc_ffn_fwd(me, h, small, pieces, after):
    outs = [sds(h.shape, bf16), sds((sum(p.shape[0] for p in pieces),) + pieces[0].shape[1:], bf16)]
    args = (me, h, small, *pieces)
    return call(
        enc_ffn_fwd_kernel, "enc_ffn_fwd", 9, args, [SCALAR] + [whole_spec(a) for a in args[1:]],
        outs, [whole_spec(o) for o in outs], [pltpu.VMEM(h.shape, f32)], after=after,
    )


def ffn_step(n, gb, w_ref, dw_ref, at=0, to=0):
    shards = w_ref.shape[0]
    wu, wd = matrix(w_ref, at), matrix(w_ref, at + 1)
    a, slope = gelu_both(nn(n, wu))
    a = a.astype(bf16)
    dw_ref[:, to + 1] = packed(tn(a, gb), shards)
    du = (slope * nt(gb, wd)).astype(bf16)
    dw_ref[:, to] = packed(tn(n, du), shards)
    return a, wd, nt(du, wu)


def enc_ffn_bwd_first_kernel(h_ref, small_ref, w_ref, cot_ref, gm_ref, gmem_ref, dn_ref, dw_ref, gb_s):
    rows, length, width = cot_ref.shape
    late = gm_ref.shape[1]
    n = normed(h_ref[...], small_ref[GAIN_ROW + 1 : GAIN_ROW + 2])
    for r in range(rows):
        gmem_ref[r, : length - late] = cot_ref[r, : length - late].astype(f32)
        gmem_ref[r, length - late :] = cot_ref[r, length - late :].astype(f32) + gm_ref[r]
        gb_s[r * length : (r + 1) * length] = gmem_ref[r].astype(bf16)
    gb = gb_s[...]
    for i in range(dw_ref.shape[1] // 2):
        dn = ffn_step(n, gb, w_ref, dw_ref, 2 * i, 2 * i)[2]
        dn_ref[...] = dn if i == 0 else dn_ref[...] + dn


def enc_ffn_bwd_next_kernel(h_ref, small_ref, w_ref, gmem_ref, dn_ref, gh_ref, dw_ref, dn_s):
    rows, length, width = gmem_ref.shape
    gain = small_ref[GAIN_ROW + 1 : GAIN_ROW + 2]
    n = normed(h_ref[...], gain)
    gmem = gmem_ref[...].reshape(rows * length, width)
    gb = gmem.astype(bf16)
    count = dw_ref.shape[1]
    for i in range(count // 2):
        dn = ffn_step(n, gb, w_ref, dw_ref, w_ref.shape[1] - count + 2 * i, 2 * i)[2]
        dn_s[...] = (dn_ref[...] if i == 0 else dn_s[...]) + dn
    gh_ref[...] = gmem + norm_back(h_ref[...], gain, dn_s[...])


def enc_ffn_bwd_first(h, small, weights, cot, late_grad, after):
    grads = sds((weights.shape[0], weights.shape[1] // 2) + weights.shape[2:], bf16)
    args = (h, small, weights, cot, late_grad)
    outs = [sds(cot.shape, f32), sds(h.shape, f32), grads]
    return simple(enc_ffn_bwd_first_kernel, "enc_ffn_bwd", 10, args, outs, after, [pltpu.VMEM(h.shape, bf16)])


def enc_ffn_bwd_next(h, small, weights, gmem, dn, after):
    grads = sds((weights.shape[0], weights.shape[1] // 2) + weights.shape[2:], bf16)
    args = (h, small, weights, gmem, dn)
    outs = [sds(h.shape, f32), grads]
    return simple(enc_ffn_bwd_next_kernel, "enc_ffn_bwd", 10, args, outs, after, [pltpu.VMEM(h.shape, f32)])


def enc_attn_bwd_kernel(
    gh_ref, q_ref, k_ref, v_ref, segc_ref, segr_ref, w_ref, small_ref, hot_ref,
    dq_ref, dk_ref, dv_ref, dt_ref, strip_ref, acc_ref, do_s, *, r,
):
    length = q_ref.shape[1]
    blocks = length // TILE
    table = small_ref[TABLE_ROW : TABLE_ROW + HEADS, :BUCKETS].astype(bf16)
    fill_strip(strip_ref, table, hot_ref[...], -TILE)
    acc_ref[...] = jnp.zeros_like(acc_ref)
    gb = gh_ref[r * length : (r + 1) * length].astype(bf16)
    do_s[...] = nt(gb, matrix(w_ref, 3)).astype(bf16)
    lane = lax.broadcasted_iota(jnp.int32, (length, 2 * HEAD_DIM), 1)
    same = segc_ref[r] == segr_ref[r]
    for hp in range(HEADS // 2):
        ls = slice(hp * 2 * HEAD_DIM, (hp + 1) * 2 * HEAD_DIM)
        qp, kp, vp, dop = q_ref[r, :, ls], k_ref[r, :, ls], v_ref[r, :, ls], do_s[:, ls]
        dq = dk = dv = None
        for sub in range(2):
            h = hp * 2 + sub
            qm, km, dom = half(lane, qp, sub), half(lane, kp, sub), half(lane, dop, sub)
            s = nt(kp, qm)
            starts = [(blocks - 1 - b) * TILE for b in range(blocks)]
            bias = [strip_ref[h, :, c : c + length] for c in starts]
            p = soft_columns(jnp.where(same, s + jnp.concatenate(bias, axis=0), MASKED))
            dp = nt(vp, dom)
            ds = (p * (dp - jnp.sum(dp * p, axis=0, keepdims=True))).astype(bf16)
            new = (tn(ds, km), nn(ds, qm), nn(p.astype(bf16), dom))
            dq, dk, dv = new if dq is None else (dq + new[0], dk + new[1], dv + new[2])
            wide = ds.astype(f32)
            for b, c in enumerate(starts):
                acc_ref[h, :, c : c + length] += wide[b * TILE : (b + 1) * TILE]
        dq_ref[0, :, ls] = dq.astype(bf16)
        dk_ref[0, :, ls] = dk.astype(bf16)
        dv_ref[0, :, ls] = dv.astype(bf16)
    dt_ref[...] = strip_sums(acc_ref[...], hot_ref[...])


def enc_attn_bwd(r, grad_hidden, q, k, v, segc, segr, weights, small, after):
    rows, length, width = q.shape
    strip = pltpu.VMEM((HEADS, TILE, 2 * length), f32)
    args = (grad_hidden, q, k, v, segc, segr, weights, small, offset_hot(length, True, True))
    outs = [sds((1, length, width), bf16)] * 3 + [sds((HEADS, BUCKETS), f32)]
    return simple(
        functools.partial(enc_attn_bwd_kernel, r=r), "enc_attn_bwd", 10, args, outs, after,
        [strip, strip, pltpu.VMEM((length, width), bf16)],
    )


def enc_weight_grads_kernel(x_ref, small_ref, mix_ref, gh_ref, td_ref, *refs):
    *parts, dw_ref = refs
    rows, length, width = x_ref.shape
    shards = dw_ref.shape[0]
    blk = width // shards
    gain = small_ref[GAIN_ROW : GAIN_ROW + 1]
    n = normed(x_ref[...].astype(f32).reshape(rows * length, width), gain)
    for w in range(3):
        total = None
        for r in range(rows):
            new = tn(n[r * length : (r + 1) * length], parts[4 * r + w][0])
            total = new if total is None else total + new
        dw_ref[:, w * blk : (w + 1) * blk] = packed(total, shards)
    dw_ref[:, 3 * blk : 4 * blk] = packed(tn(mix_ref[...], gh_ref[...].astype(bf16)), shards)
    table = sum(parts[4 * r + 3][...] for r in range(rows))
    for s in range(shards):
        dw_ref[s, 4 * blk :] = jnp.zeros((SMALL_ROWS, width), bf16)
        dw_ref[s, 4 * blk : 4 * blk + HEADS, :BUCKETS] = table.astype(bf16)
        dw_ref[s, 4 * blk : 4 * blk + HEADS, DEC_LANE : DEC_LANE + BUCKETS] = td_ref[...].astype(bf16)


def enc_weight_grads(x, small, mix, grad_hidden, dec_grad, parts, shards, after):
    width = x.shape[-1]
    grads = sds((shards, 4 * width // shards + SMALL_ROWS, width), bf16)
    args = (x, small, mix, grad_hidden, dec_grad) + tuple(a for row in parts for a in row)
    return simple(enc_weight_grads_kernel, "enc_weight_grads", 3, args, [grads], after)[0]


def enc_input_grad_kernel(x_ref, small_ref, gh_ref, w_ref, *refs):
    *parts, gi_ref = refs
    rows, length, width = x_ref.shape
    gain = small_ref[GAIN_ROW : GAIN_ROW + 1]
    for r in range(rows):
        dn = sum(nt(parts[4 * r + w][0], matrix(w_ref, w)) for w in range(3))
        gi_ref[r] = gh_ref[r * length : (r + 1) * length] + norm_back(x_ref[r].astype(f32), gain, dn)


def enc_input_grad(x, small, grad_hidden, weights, parts, after):
    args = (x, small, grad_hidden, weights, *(a for row in parts for a in row))
    return simple(enc_input_grad_kernel, "enc_input_grad", 4, args, [sds(x.shape, f32)], after)[0]


def embed_rows_kernel(me_ref, embed_ref, *refs):
    pieces, (found_ref, ids_ref) = refs[:-2], refs[-2:]
    shards, tokens, _ = found_ref.shape
    own = embed_ref.shape[0]
    me = me_ref[0]
    count = len(pieces) // 2
    row = pieces[0].shape[1] - SMALL_ROWS + ID_ROW
    for core, part in ((me, pieces[:count]), (me ^ 1, pieces[count:])):
        for p, (ref, i) in enumerate(spread(part)):
            code = ref[i, row : row + 1, :].astype(f32).astype(jnp.int32)
            ids = code[:, :tokens] * 64 + code[:, tokens : 2 * tokens]
            s = shard_at(p, core, shards)
            ids_ref[s] = ids
            found_ref[s] = tn(one_hot(ids, own, me), embed_ref[...]).astype(bf16)


def sum_rows_kernel(a_ref, o_ref):
    total = a_ref[0].astype(f32)
    for s in range(1, a_ref.shape[0]):
        total = total + a_ref[s].astype(f32)
    o_ref[...] = total.astype(bf16)


def sum_rows(a, after):
    return simple(sum_rows_kernel, "sum_rows", 0.7, (a,), [sds(a.shape[1:], bf16)], after)[0]


def one_hot(ids, own, me):
    return (lax.broadcasted_iota(jnp.int32, (own, ids.shape[1]), 0) + me * own == ids).astype(f32).astype(bf16)


def embed_rows(me, embed, pieces, tokens, after):
    shards = sum(p.shape[0] for p in pieces)
    outs = [sds((shards, tokens, embed.shape[1]), bf16), sds((shards, 1, tokens), jnp.int32)]
    args = (embed, *pieces)
    return call(
        embed_rows_kernel, "embed_rows", 2, (me,) + args, [SCALAR] + [whole_spec(a) for a in args], outs,
        [whole_spec(o) for o in outs], after=after,
    )


def embed_grads_kernel(me_ref, ids_ref, *refs):
    pieces, out_ref = refs[:-1], refs[-1]
    shards = ids_ref.shape[0]
    me = me_ref[0]
    count = len(pieces) // 2
    total = jnp.zeros(out_ref.shape, f32)
    for core, part in ((me, pieces[:count]), (me ^ 1, pieces[count:])):
        for p, (ref, i) in enumerate(spread(part)):
            ids = ids_ref[shard_at(p, core, shards)]
            total = total + nn(one_hot(ids, out_ref.shape[0], me), ref[i])
    out_ref[...] = total.astype(bf16)


def embed_grads(me, ids, pieces, own, after):
    out = sds((own, pieces[0].shape[-1]), bf16)
    args = (ids, *pieces)
    return call(
        embed_grads_kernel, "embed_grads", 2, (me,) + args, [SCALAR] + [whole_spec(a) for a in args], [out],
        [whole_spec(out)], after=after,
    )[0]


def dec_masks(rows, steps, late, last_ref, key_major):
    tokens, keys = rows * steps, rows * late
    shape = (tokens, tokens)
    i = lax.broadcasted_iota(jnp.int32, shape, 1 if key_major else 0)
    j = lax.broadcasted_iota(jnp.int32, shape, 0 if key_major else 1)
    causal = (i // steps == j // steps) & (j <= i)
    shape = (keys, tokens) if key_major else (tokens, keys)
    i = lax.broadcasted_iota(jnp.int32, shape, 1 if key_major else 0)
    j = lax.broadcasted_iota(jnp.int32, shape, 0 if key_major else 1)
    return causal, (i // steps == j // late) & (last_ref[...] == 1)


def dec_table(small_ref):
    return small_ref[TABLE_ROW : TABLE_ROW + HEADS, DEC_LANE : DEC_LANE + BUCKETS].astype(bf16)


def dec_attn_fwd_kernel(
    emb_ref, enc_ref, last_ref, small_ref, w_ref, hot_ref,
    na_ref, qkv_ref, mixa_ref, hida_ref, nb_ref, cq_ref, ckv_ref, mixb_ref, hidb_ref, strip_ref, *, rows,
):
    tokens = emb_ref.shape[0]
    keys = enc_ref.shape[0]
    causal, allowed = dec_masks(rows, tokens // rows, keys // rows, last_ref, False)
    fill_strip(strip_ref, dec_table(small_ref), hot_ref[...], 1 - tokens)
    lane = lax.broadcasted_iota(jnp.int32, (tokens, 2 * HEAD_DIM), 1)

    def attend(q_at, k_at, v_at, bias_at, mask, mix_ref):
        for hp in range(HEADS // 2):
            ls = slice(hp * 2 * HEAD_DIM, (hp + 1) * 2 * HEAD_DIM)
            qp, kp, vp = q_at(ls), k_at(ls), v_at(ls)
            outs = []
            for sub in range(2):
                s = nt(half(lane, qp, sub), kp)
                if bias_at is not None:
                    s = s + bias_at(hp * 2 + sub)
                outs.append(nn(soft_rows(jnp.where(mask, s, MASKED)).astype(bf16), vp))
            mix_ref[:, ls] = jnp.where(lane < HEAD_DIM, outs[0], outs[1]).astype(bf16)

    emb = emb_ref[...].astype(f32)
    na_ref[...] = normed(emb, small_ref[GAIN_ROW + 2 : GAIN_ROW + 3])
    for w in range(3):
        qkv_ref[w] = nn(na_ref[...], matrix(w_ref, w)).astype(bf16)
    attend(
        lambda ls: qkv_ref[0, :, ls],
        lambda ls: qkv_ref[1, :, ls],
        lambda ls: qkv_ref[2, :, ls],
        lambda h: strip_ref[h, :, :tokens],
        causal,
        mixa_ref,
    )
    hida_ref[...] = emb + nn(mixa_ref[...], matrix(w_ref, 3))
    nb_ref[...] = normed(hida_ref[...], small_ref[GAIN_ROW + 3 : GAIN_ROW + 4])
    cq_ref[...] = nn(nb_ref[...], matrix(w_ref, 4)).astype(bf16)
    for w in range(2):
        ckv_ref[w] = nn(enc_ref[...], matrix(w_ref, 5 + w)).astype(bf16)
    attend(
        lambda ls: cq_ref[:, ls],
        lambda ls: ckv_ref[0, :, ls],
        lambda ls: ckv_ref[1, :, ls],
        None,
        allowed,
        mixb_ref,
    )
    hidb_ref[...] = hida_ref[...] + nn(mixb_ref[...], matrix(w_ref, 7))


def dec_attn_fwd(emb, enc_late, last, small, pieces, me, rows, after):
    tokens, width = emb.shape
    keys = enc_late.shape[0]
    hot = dec_hot(tokens, tokens // rows, False)
    one = sds((tokens, width), bf16)
    wide = sds((tokens, width), f32)
    full = sds((sum(p.shape[0] for p in pieces),) + pieces[0].shape[1:], bf16)
    outs = [one, sds((3, tokens, width), bf16), one, wide, one, one, sds((2, keys, width), bf16), one, wide, full]
    args = (emb, enc_late, last, small, hot, *pieces)

    def body(me_ref, emb_ref, enc_ref, last_ref, small_ref, hot_ref, *refs):
        parts, kept, w_ref, strip_ref = refs[: len(pieces)], refs[len(pieces) : -2], refs[-2], refs[-1]
        collect(w_ref, parts, me_ref[0])
        dec_attn_fwd_kernel(
            emb_ref, enc_ref, last_ref, small_ref, w_ref, hot_ref, *kept, strip_ref, rows=rows
        )

    return call(
        body, "dec_attn_fwd", 7, (me,) + args, [SCALAR] + [whole_spec(a) for a in args], outs,
        [whole_spec(o) for o in outs], [pltpu.VMEM((HEADS, tokens, 2 * tokens), f32)], after=after,
    )


def dec_hot(tokens, steps, reverse):
    codes = np.full(2 * tokens, -1, np.int32)
    own = bucket_codes(steps, False)
    codes[tokens - steps : tokens - steps + len(own)] = own
    if reverse:
        codes = codes[::-1]
    return jnp.asarray(codes[None, :] == np.arange(BUCKETS)[:, None], bf16)


def dec_ffn_kernel(me_ref, h_ref, small_ref, cot_ref, *refs):
    pieces, (out_ref, gh_ref, dw_ref, w_s, dn_s, o_s) = refs[:-6], refs[-6:]
    gain = small_ref[GAIN_ROW + 4 : GAIN_ROW + 5]
    collect(w_s, pieces, me_ref[0])
    n = normed(h_ref[...], gain)
    gb = cot_ref[...]
    for i in range(w_s.shape[1] // 2):
        a, wd, dn = ffn_step(n, gb, w_s, dw_ref, 2 * i, 2 * i)
        o_s[...] = (h_ref[...] if i == 0 else o_s[...]) + nn(a, wd)
        dn_s[...] = dn if i == 0 else dn_s[...] + dn
    out_ref[...] = o_s[...].astype(bf16)
    gh_ref[...] = gb.astype(f32) + norm_back(h_ref[...], gain, dn_s[...])


def dec_ffn(me, h, small, cot, pieces, after):
    grads = sds((sum(p.shape[0] for p in pieces),) + pieces[0].shape[1:], bf16)
    outs = [sds(h.shape, bf16), sds(h.shape, f32), grads]
    args = (me, h, small, cot, *pieces)
    return call(
        dec_ffn_kernel, "dec_ffn", 8, args, [SCALAR] + [whole_spec(a) for a in args[1:]],
        outs, [whole_spec(o) for o in outs],
        [pltpu.VMEM(grads.shape, bf16), pltpu.VMEM(h.shape, f32), pltpu.VMEM(h.shape, f32)], after=after,
    )


def attend_back(q_at, k_at, v_at, do, bias_at, mask, take_score, dq_s, dk_s, dv_s):
    for hp in range(HEADS // 2):
        ls = slice(hp * 2 * HEAD_DIM, (hp + 1) * 2 * HEAD_DIM)
        qp, kp, vp, dop = q_at(ls), k_at(ls), v_at(ls), do[:, ls]
        lane = lax.broadcasted_iota(jnp.int32, qp.shape, 1)
        lanek = lax.broadcasted_iota(jnp.int32, kp.shape, 1)
        dq = dk = dv = None
        for sub in range(2):
            qm, km, dom = half(lane, qp, sub), half(lanek, kp, sub), half(lane, dop, sub)
            s = nt(kp, qm)
            if bias_at is not None:
                s = s + bias_at(hp * 2 + sub)
            p = soft_columns(jnp.where(mask, s, MASKED))
            dp = nt(vp, dom)
            ds = (p * (dp - jnp.sum(dp * p, axis=0, keepdims=True))).astype(bf16)
            new = (tn(ds, km), nn(ds, qm), nn(p.astype(bf16), dom))
            dq, dk, dv = new if dq is None else (dq + new[0], dk + new[1], dv + new[2])
            if take_score is not None:
                take_score(hp * 2 + sub, ds)
        dq_s[:, ls] = dq.astype(bf16)
        dk_s[:, ls] = dk.astype(bf16)
        dv_s[:, ls] = dv.astype(bf16)


def dec_cross_bwd_kernel(
    gb_ref, enc_ref, last_ref, small_ref, w_ref, hida_ref, nb_ref, cq_ref, ckv_ref, mixb_ref,
    gm_ref, ga_ref, dw_ref, dq_s, dk_s, dv_s, *, rows,
):
    tokens = gb_ref.shape[0]
    keys = enc_ref.shape[0]
    shards = dw_ref.shape[0]
    _, allowed = dec_masks(rows, tokens // rows, keys // rows, last_ref, True)
    grad_b = gb_ref[...]
    branch = grad_b.astype(bf16)
    dw_ref[:, 3] = packed(tn(mixb_ref[...], branch), shards)
    do = nt(branch, matrix(w_ref, 7)).astype(bf16)
    attend_back(
        lambda ls: cq_ref[:, ls],
        lambda ls: ckv_ref[0, :, ls],
        lambda ls: ckv_ref[1, :, ls],
        do,
        None,
        allowed,
        None,
        dq_s,
        dk_s,
        dv_s,
    )
    gm_ref[...] = nt(dk_s[...], matrix(w_ref, 5)) + nt(dv_s[...], matrix(w_ref, 6))
    dw_ref[:, 0] = packed(tn(nb_ref[...], dq_s[...]), shards)
    dw_ref[:, 1] = packed(tn(enc_ref[...], dk_s[...]), shards)
    dw_ref[:, 2] = packed(tn(enc_ref[...], dv_s[...]), shards)
    gain = small_ref[GAIN_ROW + 3 : GAIN_ROW + 4]
    ga_ref[...] = grad_b + norm_back(hida_ref[...], gain, nt(dq_s[...], matrix(w_ref, 4)))


def dec_cross_bwd(grad_b, enc_late, last, small, weights, kept, rows, after):
    tokens, width = grad_b.shape
    keys = enc_late.shape[0]
    _, _, _, hida, nb, cq, ckv, mixb, _ = kept
    shards, _, blk, _ = weights.shape
    outs = [sds((keys, width), f32), sds((tokens, width), f32), sds((shards, 4, blk, width), bf16)]
    args = (grad_b, enc_late, last, small, weights, hida, nb, cq, ckv, mixb)
    return simple(
        functools.partial(dec_cross_bwd_kernel, rows=rows), "dec_cross_bwd", 6, args, outs, after,
        [pltpu.VMEM((tokens, width), bf16), pltpu.VMEM((keys, width), bf16), pltpu.VMEM((keys, width), bf16)],
    )


def dec_self_bwd_kernel(
    ga_ref, emb_ref, small_ref, w_ref, hot_ref, na_ref, qkv_ref, mixa_ref,
    gr_ref, dt_ref, dw_ref, strip_ref, acc_ref, dq_s, dk_s, dv_s, *, rows,
):
    tokens = emb_ref.shape[0]
    shards = dw_ref.shape[0]
    steps = tokens // rows
    i = lax.broadcasted_iota(jnp.int32, (tokens, tokens), 1)
    j = lax.broadcasted_iota(jnp.int32, (tokens, tokens), 0)
    causal = (i // steps == j // steps) & (j <= i)
    fill_strip(strip_ref, dec_table(small_ref), hot_ref[...], -tokens)
    grad_a = ga_ref[...]
    branch = grad_a.astype(bf16)
    dw_ref[:, 3] = packed(tn(mixa_ref[...], branch), shards)
    do = nt(branch, matrix(w_ref, 3)).astype(bf16)
    acc_ref[...] = jnp.zeros_like(acc_ref)

    def take_score(h, ds):
        acc_ref[h, :, :tokens] = ds.astype(f32)

    attend_back(
        lambda ls: qkv_ref[0, :, ls],
        lambda ls: qkv_ref[1, :, ls],
        lambda ls: qkv_ref[2, :, ls],
        do,
        lambda h: strip_ref[h, :, :tokens],
        causal,
        take_score,
        dq_s,
        dk_s,
        dv_s,
    )
    parts = (dq_s[...], dk_s[...], dv_s[...])
    dn = nt(parts[0], matrix(w_ref, 0)) + nt(parts[1], matrix(w_ref, 1)) + nt(parts[2], matrix(w_ref, 2))
    for w in range(3):
        dw_ref[:, w] = packed(tn(na_ref[...], parts[w]), shards)
    gain = small_ref[GAIN_ROW + 2 : GAIN_ROW + 3]
    gr_ref[0] = (grad_a + norm_back(emb_ref[...].astype(f32), gain, dn)).astype(bf16)
    dt_ref[...] = strip_sums(acc_ref[...], hot_ref[...])


def dec_self_bwd(grad_a, emb, small, weights, kept, rows, after):
    tokens, width = emb.shape
    shards, _, blk, _ = weights.shape
    na, qkv, mixa = kept[:3]
    hot = dec_hot(tokens, tokens // rows, True)
    outs = [sds((1, tokens, width), bf16), sds((HEADS, BUCKETS), f32), sds((shards, 4, blk, width), bf16)]
    args = (grad_a, emb, small, weights, hot, na, qkv, mixa)
    strip = pltpu.VMEM((HEADS, tokens, 2 * tokens), f32)
    return simple(
        functools.partial(dec_self_bwd_kernel, rows=rows), "dec_self_bwd", 4, args, outs, after,
        [strip, strip] + [pltpu.VMEM((tokens, width), bf16)] * 3,
    )


def exchange(value, shards, even_bit, odd_bit):
    pairs = [(i, i ^ (1 << (odd_bit if i & 1 else even_bit))) for i in range(shards)]
    return lax.ppermute(value, "fsdp", pairs)


def swap_cores(value, shards):
    return exchange(value, shards, 0, 0)


def round_of(value, j, shards):
    upper = shards.bit_length() - 2
    return exchange(value, shards, 1 + j, upper - j)


class Gather:
    def __init__(self, block, shards, apart=False):
        self.shards = shards
        self.upper = shards.bit_length() - 2
        self.held = block
        self.apart = apart and self.upper == 2
        if self.apart:
            self.one, self.two = round_of(block, 0, shards), round_of(block, 1, shards)
            self.swapped = [swap_cores(block, shards)]
        else:
            self.step = self.upper - 1
            self.flight = round_of(block, self.step, shards)

    def forward(self, after):
        if self.apart:
            passed = gate(self.one, after)
            self.far = round_of(passed, 1, self.shards)
            self.pieces = [self.held, self.two, passed, self.far]
            self.swapped += [swap_cores(p, self.shards) for p in self.pieces[1:3]]
            return passed
        self.held = join(self.held, self.flight, after)
        self.step -= 1
        self.flight = round_of(self.held, self.step, self.shards)
        if self.step == 0:
            self.pieces = [self.held, self.flight]
            self.swapped = [swap_cores(self.held, self.shards)]
        return self.held

    def done(self):
        return hasattr(self, "pieces")

    def finish(self, after=None):
        if after is not None:
            self.pieces[-1] = gate(self.pieces[-1], after)
        return self.pieces + self.swapped + [swap_cores(self.pieces[-1], self.shards)]


class Sum:
    def __init__(self, me, groups, over_dp=True, short=False):
        self.me, self.shards, self.short, self.line = me, groups[0].shape[0], short, None
        self.over_dp = over_dp
        self.groups = [(g, swap_cores(g, self.shards)) for g in groups]
        self.upper = self.shards.bit_length() - 2
        self.size = lax.axis_size("dp")
        self.step = -1

    def include(self, group):
        self.groups.append((group, swap_cores(group, self.shards)))

    def done(self):
        if not self.over_dp:
            return self.step >= self.upper
        return self.line is not None and self.line.done()

    def advance(self, after):
        if self.done():
            return after[0]
        if self.step < 0:
            self.keep, send = add_first(self.me, self.groups, after)
        elif self.step < self.upper - 1:
            self.keep, send = add_halves(self.keep, self.flight, after)
        else:
            if self.step == self.upper - 1:
                self.keep = add(self.keep, self.flight, after)[0]
                if self.over_dp:
                    self.line = Line(self.keep, self.size, self.short)
            else:
                self.keep = self.line.advance(after)
            self.step += 1
            return self.keep
        self.step += 1
        self.flight = round_of(send, self.step, self.shards)
        return self.keep


class Line:
    def __init__(self, value, size, short=False):
        self.value, self.size = value, size
        self.short = short or size != 4
        self.step = 0
        self.start()

    def start(self):
        if self.short:
            pairs = [(i, i ^ (1 << self.step)) for i in range(self.size)]
        else:
            pairs = ([(0, 1), (3, 2)], [(1, 2), (2, 1)], [(1, 0), (2, 3)])[self.step]
        self.flight = lax.ppermute(self.value, "dp", pairs)

    def rounds(self):
        return self.size.bit_length() - 1 if self.short else 3

    def done(self):
        return self.step >= self.rounds()

    def advance(self, after):
        if self.done():
            return after[0]
        if self.short or self.step < 2:
            self.value = add(self.value, self.flight, after)
        else:
            inner = ((lax.axis_index("dp") + 1) // 2 % 2).astype(jnp.int32).reshape(1)
            self.value = pick(inner, self.value, self.flight, after)
        self.step += 1
        if not self.done():
            self.start()
        return self.value


def pick_kernel(inner_ref, a_ref, b_ref, o_ref):
    @pl.when(inner_ref[0] == 1)
    def _():
        o_ref[...] = a_ref[...]

    @pl.when(inner_ref[0] == 0)
    def _():
        o_ref[...] = b_ref[...]


def pick(inner, a, b, after):
    size = 1 + 6 * np.prod(a.shape) * a.dtype.itemsize / 2**20
    return call(
        pick_kernel, "pick", 0.7, (inner, a, b), [SCALAR, whole_spec(a), whole_spec(b)], [a], [whole_spec(a)],
        after=after, vmem=size,
    )[0]


def unpack_ffn_kernel(sum_ref, up_ref, down_ref, *, shards):
    blocks = sum_ref.shape[0] // 2
    blk = up_ref.shape[0]
    for b in range(blocks):
        up = sum_ref[2 * b].astype(f32)
        for c in range(shards):
            up_ref[:, (c * blocks + b) * blk : (c * blocks + b + 1) * blk] = up[:, c * blk : (c + 1) * blk]
        down_ref[b * blk : (b + 1) * blk] = sum_ref[2 * b + 1].astype(f32)


def unpack_ffn(a, shards, after=()):
    count, blk, width = a.shape
    outs = [sds((blk, count // 2 * width), f32), sds((count // 2 * blk, width), f32)]
    return simple(functools.partial(unpack_ffn_kernel, shards=shards), "unpack_ffn", 1.5, (a,), outs, after)


def on_device(
    enc_input,
    segments,
    targets,
    enc_cot,
    dec_cot,
    enc_gains,
    enc_attn,
    enc_table,
    enc_up,
    enc_down,
    embed,
    dec_gains,
    dec_self,
    dec_cross,
    dec_table,
    dec_up,
    dec_down,
):
    rows, length, width = enc_input.shape
    steps = targets.shape[1]
    tokens = rows * steps
    shards = lax.axis_size("fsdp")
    blk = enc_attn.shape[1]
    own = embed.shape[0]
    index = lax.axis_index("fsdp").astype(jnp.int32)
    me = index.reshape(1)
    late = min(length, SERIES_MOST)
    flat = lambda a: a.reshape(-1, width)
    segc, segr = segments[:, :, None], segments[:, None, :]

    first = pack_first(me, enc_attn, enc_gains, dec_gains, enc_table, dec_table, targets, shards)
    a = Gather(first, shards, apart=True)
    b_block = pack_ffn(enc_up, enc_down, shards, (first,))
    mark = a.forward((b_block, a.two) if a.apart else (b_block,))
    while not a.done():
        mark = a.forward((mark,))
    b = Gather(gate(b_block, (mark,)), shards)
    c_block = pack_attn(dec_self, dec_cross, (b.held,))
    a_pieces = a.finish()
    found, ids = embed_rows(me, embed, a_pieces, tokens, (c_block,))
    e = Sum(me, [found], over_dp=False)
    mark = ids
    while not b.done():
        mark = b.forward((mark,))
    c = Gather(gate(c_block, (mark,)), shards)
    hidden, q, k, v, mix, w_attn, small = enc_attn_fwd(me, enc_input, segc, segr, a_pieces, (c.held,))
    b_pieces = b.finish((hidden,))
    mark = b_pieces[1]
    while not c.done():
        mark = c.forward((mark,))
    d = Gather(pack_ffn(dec_up, dec_down, shards, (mark,)), shards)
    mark = e.advance((d.held,))
    mark = gate(small, (mark,), 4)
    enc_out, w_ffn = enc_ffn_fwd(me, hidden, small, b_pieces, (mark,))
    c_pieces = c.finish((enc_out,))
    mark = c_pieces[1]
    while e.step < e.upper - 1:
        mark = e.advance((mark,))
    while not d.done():
        mark = d.forward((mark,))
    mark = gate(small, (mark,), 4)
    mark = e.advance((mark,))
    emb = e.keep
    enc_out = enc_out.reshape(rows, length, width)
    enc_late = flat(enc_out[:, length - late :])
    last = (segments == segments[:, -1:])[:, length - late :].astype(jnp.int32).reshape(1, -1)
    kept = dec_attn_fwd(emb, enc_late, last, small, c_pieces, me, rows, ())
    kept, w_dec = kept[:-1], kept[-1]
    d_pieces = d.finish((kept[-1],))
    mark = gate(small, (d_pieces[1],), 4)
    dec_out, grad_b, g_dffn = dec_ffn(me, kept[-1], small, flat(dec_cot), d_pieces, (mark,))

    def turn(mark, *sums):
        for r in sums:
            mark = r.advance((mark,))
        return mark

    r1 = Sum(me, [g_dffn])
    grad_late, grad_a, g_cross = dec_cross_bwd(grad_b, enc_late, last.reshape(-1, 1), small, w_dec, kept, rows, ())
    r2 = Sum(me, [g_cross])
    grad_rows, d_dtab, g_self = dec_self_bwd(grad_a, emb, small, w_dec, kept, rows, ())
    r2.include(g_self)
    mark = turn(grad_rows, r1)
    f = Gather(gate(grad_rows, (mark,)), shards)
    grad_memory, dn, g_half = enc_ffn_bwd_first(
        hidden, small, w_ffn, enc_cot, grad_late.reshape(rows, late, width), (f.held,)
    )
    r3 = Sum(me, [g_half])
    mark = turn(dn, r1, r2)
    while not f.done():
        mark = f.forward((mark,))
    grad_hidden, g_ffn = enc_ffn_bwd_next(hidden, small, w_ffn, grad_memory, dn, (mark,))
    r3.include(g_ffn)
    mark = turn(grad_hidden, r1, r2)
    f_pieces = f.finish((mark,))
    mark = gate(small, (f_pieces[1],), 8)
    mark = turn(mark, r3)
    parts = []
    for row in range(rows):
        parts.append(enc_attn_bwd(row, grad_hidden, q, k, v, segc, segr, w_attn, small, (mark,)))
        mark = parts[-1][3]
        if row == 0:
            mark = turn(mark, r1, r2, r3)
            g_embed = embed_grads(me, ids, f_pieces, own, (mark,))
            r5 = Line(g_embed, lax.axis_size("dp"))
            mark = g_embed
        else:
            mark = turn(mark, r1, r2, r3, r5)
    g_attn = enc_weight_grads(enc_input, small, mix, grad_hidden, d_dtab, parts, shards, (mark,))
    r6 = Sum(me, [g_attn], short=True)
    mark = turn(g_attn, r6)
    grad_input = enc_input_grad(enc_input, small, grad_hidden, w_attn, parts, (mark,))
    mark = turn(grad_input, r6, r2, r1, r5, r3, r6, r6, r2, r3, r5, r6, r3)
    for r in (r6, r1, r2, r3, r5):
        while not r.done():
            mark = r.advance((mark,))
    s_dup, s_ddown = unpack_ffn(r1.keep, shards)
    s_up, s_down = unpack_ffn(r3.keep, shards)
    s_attn = r6.keep.astype(f32)
    tabs = s_attn[4 * blk :]
    per = enc_table.shape[0]
    entries = lambda lane: lax.dynamic_slice(
        tabs[:HEADS, lane : lane + BUCKETS].reshape(-1), (index * per,), (per,)
    )
    s_attn = s_attn[: 4 * blk].reshape(4, blk, width)
    s_dec = r2.keep.astype(f32)

    def gain_grad(weights, sums, gain):
        axes = (0, 2) if weights.ndim == 3 else 1
        return jnp.sum(weights.astype(f32) * sums, axis=axes) / gain.astype(f32)

    return (
        enc_out,
        dec_out.reshape(rows, steps, width),
        grad_input,
        grad_memory,
        jnp.stack([gain_grad(enc_attn[:3], s_attn[:3], enc_gains[0]), gain_grad(enc_up, s_up, enc_gains[1])]),
        s_attn,
        entries(0),
        s_up,
        s_down,
        r5.value.astype(f32),
        jnp.stack(
            [
                gain_grad(dec_self[:3], s_dec[4:7], dec_gains[0]),
                gain_grad(dec_cross[0], s_dec[0], dec_gains[1]),
                gain_grad(dec_up, s_dup, dec_gains[2]),
            ]
        ),
        s_dec[4:],
        s_dec[:4],
        entries(DEC_LANE),
        s_dup,
        s_ddown,
    )


def solution(mesh):
    placed = (
        P(("fsdp", "dp"), None, None),
        P(("fsdp", "dp"), None),
        P(("fsdp", "dp"), None),
        P(("fsdp", "dp"), None, None),
        P(("fsdp", "dp"), None, None),
        P(None, "fsdp"),
        P(None, "fsdp", None),
        P("fsdp"),
        P("fsdp", None),
        P("fsdp", None),
        P("fsdp", None),
        P(None, "fsdp"),
        P(None, "fsdp", None),
        P(None, "fsdp", None),
        P("fsdp"),
        P("fsdp", None),
        P("fsdp", None),
    )
    return jax.shard_map(
        on_device,
        mesh=mesh,
        in_specs=placed,
        out_specs=(
            P(("fsdp", "dp"), None, None),
            P(("fsdp", "dp"), None, None),
            P(("fsdp", "dp"), None, None),
            P(("fsdp", "dp"), None, None),
            P(None, "fsdp"),
            P(None, "fsdp", None),
            P("fsdp"),
            P("fsdp", None),
            P("fsdp", None),
            P("fsdp", None),
            P(None, "fsdp"),
            P(None, "fsdp", None),
            P(None, "fsdp", None),
            P("fsdp"),
            P("fsdp", None),
            P("fsdp", None),
        ),
        check_vma=False,
    )
```

```python
import functools

import jax
import jax.numpy as jnp
import numpy as np
from jax import lax
from jax.experimental import pallas as pl
from jax.experimental.pallas import tpu as pltpu
from jax.sharding import PartitionSpec as P

HEADS = 8
HEAD_DIM = 64
BUCKETS = 32
SERIES_MOST = 256
TILE = 128
MASKED = -1000000000.0

epsilon = 1e-06
f32 = jnp.float32
bf16 = jnp.bfloat16
PEAK = 1.15e9

WEIGHT = 1

VMEM = {
    "pack_first": 4,
    "enc_attn_fwd": 24,
    "enc_ffn_fwd": 20,
    "enc_ffn_bwd": 24,
    "enc_attn_bwd": 24,
    "enc_weight_grads": 16,
    "enc_input_grad": 20,
    "embed_rows": 8,
    "embed_grads": 8,
    "dec_attn_fwd": 20,
    "dec_ffn": 16,
    "dec_cross_bwd": 20,
    "dec_self_bwd": 16,
}

TABLE_ROW = 0
GAIN_ROW = 8
ID_ROW = 13
SMALL_ROWS = 16
DEC_LANE = 128


def bucket_codes(length, both_ways):
    bucket_list = []
    for offset in range(-(length - 1), length):
        if both_ways:
            upper_half = 16 if offset > 0 else 0
            distance = abs(offset)
            if distance < 8:
                bucket = distance
            else:
                bucket = 8 + sum(
                    (1 for exponent in range(1, 8) if distance * distance >= 64 * 2**exponent)
                )
        else:
            upper_half = 0
            distance = max(-offset, 0)
            if distance < 16:
                bucket = distance
            else:
                bucket = 16 + sum(
                    (1 for exponent in range(1, 16) if distance**16 >= 16**16 * 2 ** (3 * exponent))
                )
        bucket_list.append(upper_half + bucket)
    return np.array(bucket_list, dtype=np.int32)


def offset_hot(length, both_ways, reverse):
    codes = np.concatenate([bucket_codes(length, both_ways), [-1]])
    if reverse:
        codes = codes[::-1]
    return jnp.asarray(codes[None, :] == np.arange(BUCKETS)[:, None], bf16)


def nn(a, b):
    return lax.dot_general(a, b, (((1,), (0,)), ((), ())), preferred_element_type=f32)


def nt(a, b):
    return lax.dot_general(a, b, (((1,), (1,)), ((), ())), preferred_element_type=f32)


def tn(a, b):
    return lax.dot_general(a, b, (((0,), (0,)), ((), ())), preferred_element_type=f32)


def rho_of(h):
    return lax.rsqrt(jnp.mean(h * h, axis=-1, keepdims=True) + epsilon)


def normed(h, gain):
    return (h * rho_of(h) * gain.astype(f32)).astype(bf16)


def norm_back(h, gain, dn):
    rho = rho_of(h)
    xh = h * rho
    gu = dn * gain.astype(f32)
    return rho * (gu - xh * jnp.mean(gu * xh, axis=-1, keepdims=True))


def gelu(u):
    t = jnp.tanh(np.float32(np.sqrt(2 / np.pi)) * (u + 0.044715 * (u * u * u)))
    return 0.5 * u * (1.0 + t)


def gelu_both(u):
    c = np.float32(np.sqrt(2 / np.pi))
    u2 = u * u
    t = jnp.tanh(c * (u + 0.044715 * (u2 * u)))
    cdf = 0.5 * (1.0 + t)
    return u * cdf, cdf + 0.5 * u * (1.0 - t * t) * (c + (3 * 0.044715 * c) * u2)


def matrix(ref, w):
    part = ref[:, w]
    return part.reshape(part.shape[0] * part.shape[1], part.shape[2])


def packed(value, shards):
    return value.reshape(shards, value.shape[0] // shards, value.shape[1]).astype(bf16)


def place(shard, me, shards):
    upper = shards.bit_length() - 2
    diff = shard ^ me
    spot = 0
    for j in range(upper):
        even = (diff >> (1 + j)) & 1
        odd = (diff >> (upper - j)) & 1
        spot = spot | (jnp.where((shard & 1) == 0, even, odd) << (upper - 1 - j))
    return spot


def shard_at(spot, me, shards):
    upper = shards.bit_length() - 2
    diff_even = diff_odd = 0
    for j in range(upper):
        bit = (spot >> (upper - 1 - j)) & 1
        diff_even = diff_even | (bit << (1 + j))
        diff_odd = diff_odd | (bit << (upper - j))
    return me ^ jnp.where((me & 1) == 0, diff_even, diff_odd)


def spread(refs):
    return [(ref, i) for ref in refs for i in range(ref.shape[0])]


def collect(out_ref, refs, me, rows=None):
    shards = out_ref.shape[0]
    count = len(refs) // 2
    for core, part in ((me, refs[:count]), (me ^ 1, refs[count:])):
        for p, (ref, i) in enumerate(spread(part)):
            piece = ref[i] if rows is None else ref[i, :rows]
            out_ref[shard_at(p, core, shards)] = piece.reshape(out_ref.shape[1:])


SCALAR = pl.BlockSpec(memory_space=pltpu.SMEM)
ANYWHERE = pl.BlockSpec(memory_space=pl.ANY)
sds = jax.ShapeDtypeStruct


def far(shape, dtype):
    return pltpu.HBM(shape, dtype)


def stay(arrays):
    return [pltpu.with_memory_space_constraint(a, pltpu.HBM) for a in arrays]


def whole_spec(a):
    zeros = (0,) * len(a.shape)
    return pl.BlockSpec(a.shape, lambda i: zeros)


def call(kernel, name, us, args, in_specs, outs, out_specs, scratch=(), grid=1, after=(), vmem=None, distant=()):
    waits = len(after)

    def body(*refs):
        kernel(*refs[waits:])

    return pl.pallas_call(
        body,
        grid=(grid,),
        in_specs=[ANYWHERE] * waits + list(in_specs),
        out_specs=list(out_specs),
        out_shape=[far(o.shape, o.dtype) if i in distant else sds(o.shape, o.dtype) for i, o in enumerate(outs)],
        scratch_shapes=list(scratch),
        compiler_params=pltpu.CompilerParams(vmem_limit_bytes=int(VMEM.get(name, vmem) * 2**20)),
        cost_estimate=pl.CostEstimate(flops=int(us * PEAK * (4 if us >= 3 else 0.3)), bytes_accessed=1024, transcendentals=0),
        name=name,
    )(*after, *args)


def simple(kernel, name, us, args, outs, after=(), scratch=(), vmem=None, distant=()):
    if vmem is None:
        vmem = 1 + sum(2 * np.prod(a.shape) * a.dtype.itemsize for a in (*args, *outs)) / 2**20
    return call(
        kernel, name, us, args, [whole_spec(a) for a in args], outs, [whole_spec(o) for o in outs], scratch,
        after=after, vmem=vmem, distant=distant,
    )


def half(lane, value, which):
    return jnp.where((lane // HEAD_DIM) == which, value, jnp.zeros_like(value))


def fill_strip(strip_ref, table, hot, shift):
    vec = nn(table, hot)
    width = hot.shape[1]
    rows = strip_ref.shape[1]
    for h in range(HEADS):
        row = jnp.broadcast_to(vec[h : h + 1], (rows, width))
        strip_ref[h] = pltpu.roll(row, (width + shift) % width, 1, stride=1, stride_axis=0)


def strip_sums(acc, hot):
    rows, width = acc.shape[1], acc.shape[2]
    total = jnp.zeros((HEADS, 8, width), f32)
    for g in range(rows // 8):
        part = acc[:, g * 8 : g * 8 + 8, :].reshape(HEADS * 8, width)
        if g:
            part = pltpu.roll(part, width - 8 * g, 1)
        total = total + part.reshape(HEADS, 8, width)
    flat = total.reshape(HEADS * 8, width)
    sub = lax.broadcasted_iota(jnp.int32, flat.shape, 0) % 8
    for b in range(3):
        flat = jnp.where((sub >> b) & 1 == 1, pltpu.roll(flat, width - (1 << b), 1), flat)
    diag = pltpu.roll(jnp.sum(flat.reshape(HEADS, 8, width), axis=1), rows, 1)
    return lax.dot_general(
        diag,
        hot.astype(f32),
        (((1,), (1,)), ((), ())),
        precision=lax.Precision.HIGHEST,
        preferred_element_type=f32,
    )


def soft_rows(s):
    e = jnp.exp(s - jnp.max(s, axis=-1, keepdims=True))
    return e * (1.0 / jnp.sum(e, axis=-1, keepdims=True))


def soft_columns(s):
    e = jnp.exp(s - jnp.max(s, axis=0, keepdims=True))
    return e * (1.0 / jnp.sum(e, axis=0, keepdims=True))


def pack_first_kernel(me_ref, attn_ref, eg_ref, dg_ref, et_ref, dt_ref, tok_ref, out_ref, *, shards):
    count, blk, width = attn_ref.shape
    me = me_ref[0]
    out_ref[: count * blk] = attn_ref[...].reshape(count * blk, width)
    base = count * blk
    lane = lax.broadcasted_iota(jnp.int32, (1, width), 1)
    here = (lane // blk) == me
    per = et_ref.shape[1]
    row8 = lax.broadcasted_iota(jnp.int32, (HEADS, BUCKETS), 0)
    lane8 = lax.broadcasted_iota(jnp.int32, (HEADS, BUCKETS), 1)
    held = (row8 * BUCKETS + lane8) // per == me
    small = jnp.zeros((SMALL_ROWS, width), f32)
    rows = lax.broadcasted_iota(jnp.int32, (SMALL_ROWS, width), 0)
    gains = [eg_ref[i : i + 1] for i in range(eg_ref.shape[0])] + [dg_ref[i : i + 1] for i in range(dg_ref.shape[0])]
    for i, g in enumerate(gains):
        wide = jnp.where(here, jnp.concatenate([g.astype(f32)] * shards, axis=1), 0.0)
        small = jnp.where(rows == GAIN_ROW + i, jnp.broadcast_to(wide, small.shape), small)
    tok = tok_ref[...]
    steps = tok.shape[1]
    first = lax.broadcasted_iota(jnp.int32, tok.shape, 1) == 0
    shifted = jnp.where(first, 0, pltpu.roll(tok, 1, 1) if steps % 128 == 0 else jnp.concatenate([tok[:, -1:], tok[:, :-1]], axis=1))
    parts = [(shifted[r : r + 1] >> 6).astype(f32) for r in range(tok.shape[0])]
    parts += [(shifted[r : r + 1] & 63).astype(f32) for r in range(tok.shape[0])]
    ids = jnp.concatenate(parts, axis=1)
    ids = jnp.concatenate([ids, jnp.zeros((1, width - ids.shape[1]), f32)], axis=1)
    small = jnp.where(rows == ID_ROW, jnp.broadcast_to(ids, small.shape), small)
    out_ref[base:] = small.astype(bf16)
    for t_ref, at in ((et_ref, 0), (dt_ref, DEC_LANE)):
        table = jnp.concatenate([t_ref[...].astype(f32)] * (BUCKETS // per), axis=1)
        table = jnp.where(held, jnp.broadcast_to(table, held.shape), 0.0)
        out_ref[base : base + HEADS, at : at + BUCKETS] = table.astype(bf16)


def pack_first(me, attn, enc_gains, dec_gains, enc_table, dec_table, targets, shards):
    count, blk, width = attn.shape
    out = sds((1, count * blk + SMALL_ROWS, width), bf16)
    args = stay((attn, enc_gains, dec_gains, enc_table.reshape(1, -1), dec_table.reshape(1, -1), targets))

    def body(me_ref, *refs):
        pack_first_kernel(me_ref, *refs[:-1], refs[-1].at[0], shards=shards)

    return call(
        body, "pack_first", 2, (me, *args), [SCALAR] + [whole_spec(a) for a in args], [out], [whole_spec(out)]
    )[0]


def pack_ffn_kernel(up_ref, down_ref, out_ref, *, shards):
    blocks = out_ref.shape[0] // 2
    blk = up_ref.shape[0]
    for b in range(blocks):
        parts = [up_ref[:, (c * blocks + b) * blk : (c * blocks + b + 1) * blk] for c in range(shards)]
        out_ref[2 * b] = jnp.concatenate(parts, axis=1)
        out_ref[2 * b + 1] = down_ref[b * blk : (b + 1) * blk]


def pack_ffn(up, down, shards, after):
    blk, width = up.shape[0], down.shape[1]
    out = sds((1, 2 * up.shape[1] // width, blk, width), bf16)

    def body(up_ref, down_ref, out_ref):
        pack_ffn_kernel(up_ref, down_ref, out_ref.at[0], shards=shards)

    return simple(body, "pack_ffn", 1, stay((up, down)), [out], after)[0]


def pack_attn_kernel(a_ref, b_ref, out_ref):
    count = a_ref.shape[0]
    out_ref[0, :count] = a_ref[...]
    out_ref[0, count:] = b_ref[...]


def pack_attn(a, b, after):
    out = sds((1, 2 * a.shape[0]) + a.shape[1:], bf16)
    return simple(pack_attn_kernel, "pack_attn", 1, stay((a, b)), [out], after)[0]


def gate_kernel(a_ref, o_ref):
    o_ref[...] = a_ref[...]


def gate(a, after, us=0.5):
    return simple(gate_kernel, "gate", us, (a,), [a], after)[0]


def join_kernel(a_ref, b_ref, o_ref):
    size = a_ref.shape[0]
    o_ref[:size] = a_ref[...]
    o_ref[size:] = b_ref[...]


def join(a, b, after):
    return simple(join_kernel, "join", 1, (a, b), [sds((2 * a.shape[0],) + a.shape[1:], a.dtype)], after)[0]


def add_first_kernel(me_ref, *refs):
    *parts, keep_ref, send_ref = refs
    quarter = keep_ref.shape[0]
    shards = 4 * quarter
    at = 0
    for a_ref, b_ref in zip(parts[::2], parts[1::2]):
        size = a_ref.shape[1]
        for p in range(2 * quarter):
            s = shard_at(p, me_ref[0], shards)
            out_ref = keep_ref if p < quarter else send_ref
            total = a_ref[s].astype(f32) + b_ref[s].astype(f32)
            out_ref[p % quarter, at : at + size] = total.astype(bf16)
        at += size


def add_first(me, pairs, after, us=2):
    shards = pairs[0][0].shape[0]
    args = [a for pair in pairs for a in pair]
    size = sum(grads.shape[1] for grads, _ in pairs)
    out = sds((shards // 4, size) + pairs[0][0].shape[2:], bf16)
    limit = 1 + 2 * sum(np.prod(a.shape) * 2 for a in args) / 2**20
    return call(
        add_first_kernel, "add_first", us, (me, *args), [SCALAR] + [whole_spec(a) for a in args],
        [out] * 2, [whole_spec(out)] * 2, after=after, vmem=limit,
    )


def add_halves_kernel(a_ref, b_ref, keep_ref, send_ref):
    mid = keep_ref.shape[0]
    keep_ref[...] = (a_ref[:mid].astype(f32) + b_ref[:mid].astype(f32)).astype(bf16)
    send_ref[...] = (a_ref[mid:].astype(f32) + b_ref[mid:].astype(f32)).astype(bf16)


def add_halves(a, b, after):
    out = sds((a.shape[0] // 2,) + a.shape[1:], bf16)
    return simple(add_halves_kernel, "add_halves", 1, (a, b), [out] * 2, after)


def add_kernel(a_ref, b_ref, o_ref):
    o_ref[...] = (a_ref[...].astype(f32) + b_ref[...].astype(f32)).astype(o_ref.dtype)


def add(a, b, after, dtype=bf16):
    return simple(add_kernel, "add", 0.7, (a, b), [sds(a.shape, dtype)], after)[0]


def enc_attn_fwd_kernel(me_ref, x_ref, segc_ref, segr_ref, hot_ref, *refs):
    pieces, (hid_ref, q_ref, k_ref, v_ref, mix_ref, w_ref, small_ref, strip_ref) = refs[:-8], refs[-8:]
    rows, length, _ = x_ref.shape
    blocks = length // TILE
    own = pieces[0].shape[1] - SMALL_ROWS
    collect(w_ref, pieces, me_ref[0], own)
    small = jnp.zeros(small_ref.shape, f32)
    for ref, i in spread(pieces):
        small = small + ref[i, own:].astype(f32)
    small_ref[...] = small
    table = small[TABLE_ROW : TABLE_ROW + HEADS, :BUCKETS].astype(bf16)
    fill_strip(strip_ref, table, hot_ref[...], 1 - TILE)
    lane = lax.broadcasted_iota(jnp.int32, (length, 2 * HEAD_DIM), 1)

    @pl.loop(0, rows)
    def _(r):
        here = pl.ds(r * length, length)
        x = x_ref[r].astype(f32)
        n = normed(x, small_ref[GAIN_ROW : GAIN_ROW + 1])
        q_ref[r] = nn(n, matrix(w_ref, 0)).astype(bf16)
        k_ref[r] = nn(n, matrix(w_ref, 1)).astype(bf16)
        v_ref[r] = nn(n, matrix(w_ref, 2)).astype(bf16)
        same = segc_ref[r] == segr_ref[r]
        for hp in range(HEADS // 2):
            ls = slice(hp * 2 * HEAD_DIM, (hp + 1) * 2 * HEAD_DIM)
            qp, kp, vp = q_ref[r, :, ls], k_ref[r, :, ls], v_ref[r, :, ls]
            outs = []
            for sub in range(2):
                s = nt(half(lane, qp, sub), kp)
                starts = [(blocks - 1 - b) * TILE for b in range(blocks)]
                bias = [strip_ref[hp * 2 + sub, :, c : c + length] for c in starts]
                s = jnp.where(same, s + jnp.concatenate(bias, axis=0), MASKED)
                outs.append(nn(soft_rows(s).astype(bf16), vp))
            mix_ref[here, ls] = jnp.where(lane < HEAD_DIM, outs[0], outs[1]).astype(bf16)
        hid_ref[here] = x + nn(mix_ref[here], matrix(w_ref, 3))


def enc_attn_fwd(me, x, segc, segr, pieces, after):
    rows, length, width = x.shape
    shards = sum(p.shape[0] for p in pieces)
    hot = offset_hot(length, True, False)
    flat = (rows * length, width)
    outs = [sds(flat, f32)] + [sds(x.shape, bf16)] * 3 + [sds(flat, bf16)]
    outs += [sds((shards, 4, width // shards, width), bf16), sds((SMALL_ROWS, width), f32)]
    args = [me, x, segc, segr, hot] + list(pieces)
    return call(
        enc_attn_fwd_kernel, "enc_attn_fwd", 14, args, [SCALAR] + [whole_spec(a) for a in args[1:]],
        outs, [whole_spec(o) for o in outs], [pltpu.VMEM((HEADS, TILE, 2 * length), f32)], after=after,
    )


def enc_ffn_fwd_kernel(me_ref, h_ref, small_ref, *refs):
    pieces, (o_ref, w_ref, acc_s) = refs[:-3], refs[-3:]
    collect(w_ref, pieces, me_ref[0])
    n = normed(h_ref[...], small_ref[GAIN_ROW + 1 : GAIN_ROW + 2])
    for i in range(w_ref.shape[1] // 2):
        a = gelu(nn(n, matrix(w_ref, 2 * i))).astype(bf16)
        acc_s[...] = (h_ref[...] if i == 0 else acc_s[...]) + nn(a, matrix(w_ref, 2 * i + 1))
    o_ref[...] = acc_s[...].astype(bf16)


def enc_ffn_fwd(me, h, small, pieces, after):
    outs = [sds(h.shape, bf16), sds((sum(p.shape[0] for p in pieces),) + pieces[0].shape[1:], bf16)]
    args = (me, h, small, *pieces)
    return call(
        enc_ffn_fwd_kernel, "enc_ffn_fwd", 9, args, [SCALAR] + [whole_spec(a) for a in args[1:]],
        outs, [whole_spec(o) for o in outs], [pltpu.VMEM(h.shape, f32)], after=after,
    )


def ffn_step(n, gb, w_ref, dw_ref, at=0, to=0):
    shards = w_ref.shape[0]
    wu, wd = matrix(w_ref, at), matrix(w_ref, at + 1)
    a, slope = gelu_both(nn(n, wu))
    a = a.astype(bf16)
    dw_ref[:, to + 1] = packed(tn(a, gb), shards)
    du = (slope * nt(gb, wd)).astype(bf16)
    dw_ref[:, to] = packed(tn(n, du), shards)
    return a, wd, nt(du, wu)


def enc_ffn_bwd_first_kernel(h_ref, small_ref, w_ref, cot_ref, gm_ref, gmem_ref, dn_ref, dw_ref, gb_s):
    rows, length, width = cot_ref.shape
    late = gm_ref.shape[1]
    n = normed(h_ref[...], small_ref[GAIN_ROW + 1 : GAIN_ROW + 2])
    for r in range(rows):
        gmem_ref[r, : length - late] = cot_ref[r, : length - late].astype(f32)
        gmem_ref[r, length - late :] = cot_ref[r, length - late :].astype(f32) + gm_ref[r]
        gb_s[r * length : (r + 1) * length] = gmem_ref[r].astype(bf16)
    gb = gb_s[...]
    for i in range(dw_ref.shape[1] // 2):
        dn = ffn_step(n, gb, w_ref, dw_ref, 2 * i, 2 * i)[2]
        dn_ref[...] = dn if i == 0 else dn_ref[...] + dn


def enc_ffn_bwd_next_kernel(h_ref, small_ref, w_ref, gmem_ref, dn_ref, gh_ref, dw_ref, dn_s):
    rows, length, width = gmem_ref.shape
    gain = small_ref[GAIN_ROW + 1 : GAIN_ROW + 2]
    n = normed(h_ref[...], gain)
    gmem = gmem_ref[...].reshape(rows * length, width)
    gb = gmem.astype(bf16)
    count = dw_ref.shape[1]
    for i in range(count // 2):
        dn = ffn_step(n, gb, w_ref, dw_ref, w_ref.shape[1] - count + 2 * i, 2 * i)[2]
        dn_s[...] = (dn_ref[...] if i == 0 else dn_s[...]) + dn
    gh_ref[...] = gmem + norm_back(h_ref[...], gain, dn_s[...])


def enc_ffn_bwd_first(h, small, weights, cot, late_grad, after):
    grads = sds((weights.shape[0], weights.shape[1] // 2) + weights.shape[2:], bf16)
    args = (h, small, weights, cot, late_grad)
    outs = [sds(cot.shape, f32), sds(h.shape, f32), grads]
    return simple(enc_ffn_bwd_first_kernel, "enc_ffn_bwd", 10, args, outs, after, [pltpu.VMEM(h.shape, bf16)])


def enc_ffn_bwd_next(h, small, weights, gmem, dn, after):
    grads = sds((weights.shape[0], weights.shape[1] // 2) + weights.shape[2:], bf16)
    args = (h, small, weights, gmem, dn)
    outs = [sds(h.shape, f32), grads]
    return simple(enc_ffn_bwd_next_kernel, "enc_ffn_bwd", 10, args, outs, after, [pltpu.VMEM(h.shape, f32)])


def enc_attn_bwd_kernel(
    gh_ref, q_ref, k_ref, v_ref, segc_ref, segr_ref, w_ref, small_ref, hot_ref,
    dq_ref, dk_ref, dv_ref, dt_ref, strip_ref, acc_ref, do_s, *, r,
):
    length = q_ref.shape[1]
    blocks = length // TILE
    table = small_ref[TABLE_ROW : TABLE_ROW + HEADS, :BUCKETS].astype(bf16)
    fill_strip(strip_ref, table, hot_ref[...], -TILE)
    acc_ref[...] = jnp.zeros_like(acc_ref)
    gb = gh_ref[r * length : (r + 1) * length].astype(bf16)
    do_s[...] = nt(gb, matrix(w_ref, 3)).astype(bf16)
    lane = lax.broadcasted_iota(jnp.int32, (length, 2 * HEAD_DIM), 1)
    same = segc_ref[r] == segr_ref[r]
    for hp in range(HEADS // 2):
        ls = slice(hp * 2 * HEAD_DIM, (hp + 1) * 2 * HEAD_DIM)
        qp, kp, vp, dop = q_ref[r, :, ls], k_ref[r, :, ls], v_ref[r, :, ls], do_s[:, ls]
        dq = dk = dv = None
        for sub in range(2):
            h = hp * 2 + sub
            qm, km, dom = half(lane, qp, sub), half(lane, kp, sub), half(lane, dop, sub)
            s = nt(kp, qm)
            starts = [(blocks - 1 - b) * TILE for b in range(blocks)]
            bias = [strip_ref[h, :, c : c + length] for c in starts]
            p = soft_columns(jnp.where(same, s + jnp.concatenate(bias, axis=0), MASKED))
            dp = nt(vp, dom)
            ds = (p * (dp - jnp.sum(dp * p, axis=0, keepdims=True))).astype(bf16)
            new = (tn(ds, km), nn(ds, qm), nn(p.astype(bf16), dom))
            dq, dk, dv = new if dq is None else (dq + new[0], dk + new[1], dv + new[2])
            wide = ds.astype(f32)
            for b, c in enumerate(starts):
                acc_ref[h, :, c : c + length] += wide[b * TILE : (b + 1) * TILE]
        dq_ref[0, :, ls] = dq.astype(bf16)
        dk_ref[0, :, ls] = dk.astype(bf16)
        dv_ref[0, :, ls] = dv.astype(bf16)
    dt_ref[...] = strip_sums(acc_ref[...], hot_ref[...])


def enc_attn_bwd(r, grad_hidden, q, k, v, segc, segr, weights, small, after):
    rows, length, width = q.shape
    strip = pltpu.VMEM((HEADS, TILE, 2 * length), f32)
    args = (grad_hidden, q, k, v, segc, segr, weights, small, offset_hot(length, True, True))
    outs = [sds((1, length, width), bf16)] * 3 + [sds((HEADS, BUCKETS), f32)]
    return simple(
        functools.partial(enc_attn_bwd_kernel, r=r), "enc_attn_bwd", 10, args, outs, after,
        [strip, strip, pltpu.VMEM((length, width), bf16)],
    )


def enc_weight_grads_kernel(x_ref, small_ref, mix_ref, gh_ref, td_ref, *refs):
    *parts, dw_ref = refs
    rows, length, width = x_ref.shape
    shards = dw_ref.shape[0]
    blk = width // shards
    gain = small_ref[GAIN_ROW : GAIN_ROW + 1]
    n = normed(x_ref[...].astype(f32).reshape(rows * length, width), gain)
    for w in range(3):
        total = None
        for r in range(rows):
            new = tn(n[r * length : (r + 1) * length], parts[4 * r + w][0])
            total = new if total is None else total + new
        dw_ref[:, w * blk : (w + 1) * blk] = packed(total, shards)
    dw_ref[:, 3 * blk : 4 * blk] = packed(tn(mix_ref[...], gh_ref[...].astype(bf16)), shards)
    table = sum(parts[4 * r + 3][...] for r in range(rows))
    for s in range(shards):
        dw_ref[s, 4 * blk :] = jnp.zeros((SMALL_ROWS, width), bf16)
        dw_ref[s, 4 * blk : 4 * blk + HEADS, :BUCKETS] = table.astype(bf16)
        dw_ref[s, 4 * blk : 4 * blk + HEADS, DEC_LANE : DEC_LANE + BUCKETS] = td_ref[...].astype(bf16)


def enc_weight_grads(x, small, mix, grad_hidden, dec_grad, parts, shards, after):
    width = x.shape[-1]
    grads = sds((shards, 4 * width // shards + SMALL_ROWS, width), bf16)
    args = (x, small, mix, grad_hidden, dec_grad) + tuple(a for row in parts for a in row)
    return simple(enc_weight_grads_kernel, "enc_weight_grads", 3, args, [grads], after)[0]


def enc_input_grad_kernel(x_ref, small_ref, gh_ref, w_ref, *refs):
    *parts, gi_ref = refs
    rows, length, width = x_ref.shape
    gain = small_ref[GAIN_ROW : GAIN_ROW + 1]
    for r in range(rows):
        dn = sum(nt(parts[4 * r + w][0], matrix(w_ref, w)) for w in range(3))
        gi_ref[r] = gh_ref[r * length : (r + 1) * length] + norm_back(x_ref[r].astype(f32), gain, dn)


def enc_input_grad(x, small, grad_hidden, weights, parts, after):
    args = (x, small, grad_hidden, weights, *(a for row in parts for a in row))
    return simple(enc_input_grad_kernel, "enc_input_grad", 4, args, [sds(x.shape, f32)], after)[0]


def embed_rows_kernel(me_ref, embed_ref, *refs):
    pieces, (found_ref, ids_ref) = refs[:-2], refs[-2:]
    shards, tokens, _ = found_ref.shape
    own = embed_ref.shape[0]
    me = me_ref[0]
    count = len(pieces) // 2
    row = pieces[0].shape[1] - SMALL_ROWS + ID_ROW
    for core, part in ((me, pieces[:count]), (me ^ 1, pieces[count:])):
        for p, (ref, i) in enumerate(spread(part)):
            code = ref[i, row : row + 1, :].astype(f32).astype(jnp.int32)
            ids = code[:, :tokens] * 64 + code[:, tokens : 2 * tokens]
            s = shard_at(p, core, shards)
            ids_ref[s] = ids
            found_ref[s] = tn(one_hot(ids, own, me), embed_ref[...]).astype(bf16)


def sum_rows_kernel(a_ref, o_ref):
    total = a_ref[0].astype(f32)
    for s in range(1, a_ref.shape[0]):
        total = total + a_ref[s].astype(f32)
    o_ref[...] = total.astype(bf16)


def sum_rows(a, after):
    return simple(sum_rows_kernel, "sum_rows", 0.7, (a,), [sds(a.shape[1:], bf16)], after)[0]


def one_hot(ids, own, me):
    return (lax.broadcasted_iota(jnp.int32, (own, ids.shape[1]), 0) + me * own == ids).astype(f32).astype(bf16)


def embed_rows(me, embed, pieces, tokens, after):
    shards = sum(p.shape[0] for p in pieces)
    outs = [sds((shards, tokens, embed.shape[1]), bf16), sds((shards, 1, tokens), jnp.int32)]
    args = (embed, *pieces)
    return call(
        embed_rows_kernel, "embed_rows", 2, (me,) + args, [SCALAR] + [whole_spec(a) for a in args], outs,
        [whole_spec(o) for o in outs], after=after,
    )


def embed_grads_kernel(me_ref, ids_ref, *refs):
    pieces, out_ref = refs[:-1], refs[-1]
    shards = ids_ref.shape[0]
    me = me_ref[0]
    count = len(pieces) // 2
    total = jnp.zeros(out_ref.shape, f32)
    for core, part in ((me, pieces[:count]), (me ^ 1, pieces[count:])):
        for p, (ref, i) in enumerate(spread(part)):
            ids = ids_ref[shard_at(p, core, shards)]
            total = total + nn(one_hot(ids, out_ref.shape[0], me), ref[i])
    out_ref[...] = total.astype(bf16)


def embed_grads(me, ids, pieces, own, after):
    out = sds((own, pieces[0].shape[-1]), bf16)
    args = (ids, *pieces)
    return call(
        embed_grads_kernel, "embed_grads", 2, (me,) + args, [SCALAR] + [whole_spec(a) for a in args], [out],
        [whole_spec(out)], after=after,
    )[0]


def dec_masks(rows, steps, late, last_ref, key_major):
    tokens, keys = rows * steps, rows * late
    shape = (tokens, tokens)
    i = lax.broadcasted_iota(jnp.int32, shape, 1 if key_major else 0)
    j = lax.broadcasted_iota(jnp.int32, shape, 0 if key_major else 1)
    causal = (i // steps == j // steps) & (j <= i)
    shape = (keys, tokens) if key_major else (tokens, keys)
    i = lax.broadcasted_iota(jnp.int32, shape, 1 if key_major else 0)
    j = lax.broadcasted_iota(jnp.int32, shape, 0 if key_major else 1)
    return causal, (i // steps == j // late) & (last_ref[...] == 1)


def dec_table(small_ref):
    return small_ref[TABLE_ROW : TABLE_ROW + HEADS, DEC_LANE : DEC_LANE + BUCKETS].astype(bf16)


def dec_attn_fwd_kernel(
    emb_ref, enc_ref, last_ref, small_ref, w_ref, hot_ref,
    na_ref, qkv_ref, mixa_ref, hida_ref, nb_ref, cq_ref, ckv_ref, mixb_ref, hidb_ref, strip_ref, *, rows,
):
    tokens = emb_ref.shape[0]
    keys = enc_ref.shape[0]
    causal, allowed = dec_masks(rows, tokens // rows, keys // rows, last_ref, False)
    fill_strip(strip_ref, dec_table(small_ref), hot_ref[...], 1 - tokens)
    lane = lax.broadcasted_iota(jnp.int32, (tokens, 2 * HEAD_DIM), 1)

    def attend(q_at, k_at, v_at, bias_at, mask, mix_ref):
        for hp in range(HEADS // 2):
            ls = slice(hp * 2 * HEAD_DIM, (hp + 1) * 2 * HEAD_DIM)
            qp, kp, vp = q_at(ls), k_at(ls), v_at(ls)
            outs = []
            for sub in range(2):
                s = nt(half(lane, qp, sub), kp)
                if bias_at is not None:
                    s = s + bias_at(hp * 2 + sub)
                outs.append(nn(soft_rows(jnp.where(mask, s, MASKED)).astype(bf16), vp))
            mix_ref[:, ls] = jnp.where(lane < HEAD_DIM, outs[0], outs[1]).astype(bf16)

    emb = emb_ref[...].astype(f32)
    na_ref[...] = normed(emb, small_ref[GAIN_ROW + 2 : GAIN_ROW + 3])
    for w in range(3):
        qkv_ref[w] = nn(na_ref[...], matrix(w_ref, w)).astype(bf16)
    attend(
        lambda ls: qkv_ref[0, :, ls],
        lambda ls: qkv_ref[1, :, ls],
        lambda ls: qkv_ref[2, :, ls],
        lambda h: strip_ref[h, :, :tokens],
        causal,
        mixa_ref,
    )
    hida_ref[...] = emb + nn(mixa_ref[...], matrix(w_ref, 3))
    nb_ref[...] = normed(hida_ref[...], small_ref[GAIN_ROW + 3 : GAIN_ROW + 4])
    cq_ref[...] = nn(nb_ref[...], matrix(w_ref, 4)).astype(bf16)
    for w in range(2):
        ckv_ref[w] = nn(enc_ref[...], matrix(w_ref, 5 + w)).astype(bf16)
    attend(
        lambda ls: cq_ref[:, ls],
        lambda ls: ckv_ref[0, :, ls],
        lambda ls: ckv_ref[1, :, ls],
        None,
        allowed,
        mixb_ref,
    )
    hidb_ref[...] = hida_ref[...] + nn(mixb_ref[...], matrix(w_ref, 7))


def dec_attn_fwd(emb, enc_late, last, small, pieces, me, rows, after):
    tokens, width = emb.shape
    keys = enc_late.shape[0]
    hot = dec_hot(tokens, tokens // rows, False)
    one = sds((tokens, width), bf16)
    wide = sds((tokens, width), f32)
    full = sds((sum(p.shape[0] for p in pieces),) + pieces[0].shape[1:], bf16)
    outs = [one, sds((3, tokens, width), bf16), one, wide, one, one, sds((2, keys, width), bf16), one, wide, full]
    args = (emb, enc_late, last, small, hot, *pieces)

    def body(me_ref, emb_ref, enc_ref, last_ref, small_ref, hot_ref, *refs):
        parts, kept, w_ref, strip_ref = refs[: len(pieces)], refs[len(pieces) : -2], refs[-2], refs[-1]
        collect(w_ref, parts, me_ref[0])
        dec_attn_fwd_kernel(
            emb_ref, enc_ref, last_ref, small_ref, w_ref, hot_ref, *kept, strip_ref, rows=rows
        )

    return call(
        body, "dec_attn_fwd", 7, (me,) + args, [SCALAR] + [whole_spec(a) for a in args], outs,
        [whole_spec(o) for o in outs], [pltpu.VMEM((HEADS, tokens, 2 * tokens), f32)], after=after,
    )


def dec_hot(tokens, steps, reverse):
    codes = np.full(2 * tokens, -1, np.int32)
    own = bucket_codes(steps, False)
    codes[tokens - steps : tokens - steps + len(own)] = own
    if reverse:
        codes = codes[::-1]
    return jnp.asarray(codes[None, :] == np.arange(BUCKETS)[:, None], bf16)


def dec_ffn_kernel(me_ref, h_ref, small_ref, cot_ref, *refs):
    pieces, (out_ref, gh_ref, dw_ref, w_s, dn_s, o_s) = refs[:-6], refs[-6:]
    gain = small_ref[GAIN_ROW + 4 : GAIN_ROW + 5]
    collect(w_s, pieces, me_ref[0])
    n = normed(h_ref[...], gain)
    gb = cot_ref[...]
    for i in range(w_s.shape[1] // 2):
        a, wd, dn = ffn_step(n, gb, w_s, dw_ref, 2 * i, 2 * i)
        o_s[...] = (h_ref[...] if i == 0 else o_s[...]) + nn(a, wd)
        dn_s[...] = dn if i == 0 else dn_s[...] + dn
    out_ref[...] = o_s[...].astype(bf16)
    gh_ref[...] = gb.astype(f32) + norm_back(h_ref[...], gain, dn_s[...])


def dec_ffn(me, h, small, cot, pieces, after):
    grads = sds((sum(p.shape[0] for p in pieces),) + pieces[0].shape[1:], bf16)
    outs = [sds(h.shape, bf16), sds(h.shape, f32), grads]
    args = (me, h, small, cot, *pieces)
    return call(
        dec_ffn_kernel, "dec_ffn", 8, args, [SCALAR] + [whole_spec(a) for a in args[1:]],
        outs, [whole_spec(o) for o in outs],
        [pltpu.VMEM(grads.shape, bf16), pltpu.VMEM(h.shape, f32), pltpu.VMEM(h.shape, f32)], after=after,
    )


def attend_back(q_at, k_at, v_at, do, bias_at, mask, take_score, dq_s, dk_s, dv_s):
    for hp in range(HEADS // 2):
        ls = slice(hp * 2 * HEAD_DIM, (hp + 1) * 2 * HEAD_DIM)
        qp, kp, vp, dop = q_at(ls), k_at(ls), v_at(ls), do[:, ls]
        lane = lax.broadcasted_iota(jnp.int32, qp.shape, 1)
        lanek = lax.broadcasted_iota(jnp.int32, kp.shape, 1)
        dq = dk = dv = None
        for sub in range(2):
            qm, km, dom = half(lane, qp, sub), half(lanek, kp, sub), half(lane, dop, sub)
            s = nt(kp, qm)
            if bias_at is not None:
                s = s + bias_at(hp * 2 + sub)
            p = soft_columns(jnp.where(mask, s, MASKED))
            dp = nt(vp, dom)
            ds = (p * (dp - jnp.sum(dp * p, axis=0, keepdims=True))).astype(bf16)
            new = (tn(ds, km), nn(ds, qm), nn(p.astype(bf16), dom))
            dq, dk, dv = new if dq is None else (dq + new[0], dk + new[1], dv + new[2])
            if take_score is not None:
                take_score(hp * 2 + sub, ds)
        dq_s[:, ls] = dq.astype(bf16)
        dk_s[:, ls] = dk.astype(bf16)
        dv_s[:, ls] = dv.astype(bf16)


def dec_cross_bwd_kernel(
    gb_ref, enc_ref, last_ref, small_ref, w_ref, hida_ref, nb_ref, cq_ref, ckv_ref, mixb_ref,
    gm_ref, ga_ref, dw_ref, dq_s, dk_s, dv_s, *, rows,
):
    tokens = gb_ref.shape[0]
    keys = enc_ref.shape[0]
    shards = dw_ref.shape[0]
    _, allowed = dec_masks(rows, tokens // rows, keys // rows, last_ref, True)
    grad_b = gb_ref[...]
    branch = grad_b.astype(bf16)
    dw_ref[:, 3] = packed(tn(mixb_ref[...], branch), shards)
    do = nt(branch, matrix(w_ref, 7)).astype(bf16)
    attend_back(
        lambda ls: cq_ref[:, ls],
        lambda ls: ckv_ref[0, :, ls],
        lambda ls: ckv_ref[1, :, ls],
        do,
        None,
        allowed,
        None,
        dq_s,
        dk_s,
        dv_s,
    )
    gm_ref[...] = nt(dk_s[...], matrix(w_ref, 5)) + nt(dv_s[...], matrix(w_ref, 6))
    dw_ref[:, 0] = packed(tn(nb_ref[...], dq_s[...]), shards)
    dw_ref[:, 1] = packed(tn(enc_ref[...], dk_s[...]), shards)
    dw_ref[:, 2] = packed(tn(enc_ref[...], dv_s[...]), shards)
    gain = small_ref[GAIN_ROW + 3 : GAIN_ROW + 4]
    ga_ref[...] = grad_b + norm_back(hida_ref[...], gain, nt(dq_s[...], matrix(w_ref, 4)))


def dec_cross_bwd(grad_b, enc_late, last, small, weights, kept, rows, after):
    tokens, width = grad_b.shape
    keys = enc_late.shape[0]
    _, _, _, hida, nb, cq, ckv, mixb, _ = kept
    shards, _, blk, _ = weights.shape
    outs = [sds((keys, width), f32), sds((tokens, width), f32), sds((shards, 4, blk, width), bf16)]
    args = (grad_b, enc_late, last, small, weights, hida, nb, cq, ckv, mixb)
    return simple(
        functools.partial(dec_cross_bwd_kernel, rows=rows), "dec_cross_bwd", 6, args, outs, after,
        [pltpu.VMEM((tokens, width), bf16), pltpu.VMEM((keys, width), bf16), pltpu.VMEM((keys, width), bf16)],
    )


def dec_self_bwd_kernel(
    ga_ref, emb_ref, small_ref, w_ref, hot_ref, na_ref, qkv_ref, mixa_ref,
    gr_ref, dt_ref, dw_ref, strip_ref, acc_ref, dq_s, dk_s, dv_s, *, rows,
):
    tokens = emb_ref.shape[0]
    shards = dw_ref.shape[0]
    steps = tokens // rows
    i = lax.broadcasted_iota(jnp.int32, (tokens, tokens), 1)
    j = lax.broadcasted_iota(jnp.int32, (tokens, tokens), 0)
    causal = (i // steps == j // steps) & (j <= i)
    fill_strip(strip_ref, dec_table(small_ref), hot_ref[...], -tokens)
    grad_a = ga_ref[...]
    branch = grad_a.astype(bf16)
    dw_ref[:, 3] = packed(tn(mixa_ref[...], branch), shards)
    do = nt(branch, matrix(w_ref, 3)).astype(bf16)
    acc_ref[...] = jnp.zeros_like(acc_ref)

    def take_score(h, ds):
        acc_ref[h, :, :tokens] = ds.astype(f32)

    attend_back(
        lambda ls: qkv_ref[0, :, ls],
        lambda ls: qkv_ref[1, :, ls],
        lambda ls: qkv_ref[2, :, ls],
        do,
        lambda h: strip_ref[h, :, :tokens],
        causal,
        take_score,
        dq_s,
        dk_s,
        dv_s,
    )
    parts = (dq_s[...], dk_s[...], dv_s[...])
    dn = nt(parts[0], matrix(w_ref, 0)) + nt(parts[1], matrix(w_ref, 1)) + nt(parts[2], matrix(w_ref, 2))
    for w in range(3):
        dw_ref[:, w] = packed(tn(na_ref[...], parts[w]), shards)
    gain = small_ref[GAIN_ROW + 2 : GAIN_ROW + 3]
    gr_ref[0] = (grad_a + norm_back(emb_ref[...].astype(f32), gain, dn)).astype(bf16)
    dt_ref[...] = strip_sums(acc_ref[...], hot_ref[...])


def dec_self_bwd(grad_a, emb, small, weights, kept, rows, after):
    tokens, width = emb.shape
    shards, _, blk, _ = weights.shape
    na, qkv, mixa = kept[:3]
    hot = dec_hot(tokens, tokens // rows, True)
    outs = [sds((1, tokens, width), bf16), sds((HEADS, BUCKETS), f32), sds((shards, 4, blk, width), bf16)]
    args = (grad_a, emb, small, weights, hot, na, qkv, mixa)
    strip = pltpu.VMEM((HEADS, tokens, 2 * tokens), f32)
    return simple(
        functools.partial(dec_self_bwd_kernel, rows=rows), "dec_self_bwd", 4, args, outs, after,
        [strip, strip] + [pltpu.VMEM((tokens, width), bf16)] * 3,
    )


def exchange(value, shards, even_bit, odd_bit):
    pairs = [(i, i ^ (1 << (odd_bit if i & 1 else even_bit))) for i in range(shards)]
    return lax.ppermute(value, "fsdp", pairs)


def swap_cores(value, shards):
    return exchange(value, shards, 0, 0)


def round_of(value, j, shards):
    upper = shards.bit_length() - 2
    return exchange(value, shards, 1 + j, upper - j)


class Gather:
    def __init__(self, block, shards, apart=False):
        self.shards = shards
        self.upper = shards.bit_length() - 2
        self.held = block
        self.apart = apart and self.upper == 2
        if self.apart:
            self.one, self.two = round_of(block, 0, shards), round_of(block, 1, shards)
            self.swapped = [swap_cores(block, shards)]
        else:
            self.step = self.upper - 1
            self.flight = round_of(block, self.step, shards)

    def forward(self, after):
        if self.apart:
            passed = gate(self.one, after)
            self.far = round_of(passed, 1, self.shards)
            self.pieces = [self.held, self.two, passed, self.far]
            self.swapped += [swap_cores(p, self.shards) for p in self.pieces[1:3]]
            return passed
        self.held = join(self.held, self.flight, after)
        self.step -= 1
        self.flight = round_of(self.held, self.step, self.shards)
        if self.step == 0:
            self.pieces = [self.held, self.flight]
            self.swapped = [swap_cores(self.held, self.shards)]
        return self.held

    def done(self):
        return hasattr(self, "pieces")

    def finish(self, after=None):
        if after is not None:
            self.pieces[-1] = gate(self.pieces[-1], after)
        return self.pieces + self.swapped + [swap_cores(self.pieces[-1], self.shards)]


class Sum:
    def __init__(self, me, groups, over_dp=True, short=False):
        self.me, self.shards, self.short, self.line = me, groups[0].shape[0], short, None
        self.over_dp = over_dp
        self.groups = [(g, swap_cores(g, self.shards)) for g in groups]
        self.upper = self.shards.bit_length() - 2
        self.size = lax.axis_size("dp")
        self.step = -1

    def include(self, group):
        self.groups.append((group, swap_cores(group, self.shards)))

    def done(self):
        if not self.over_dp:
            return self.step >= self.upper
        return self.line is not None and self.line.done()

    def advance(self, after, hold=False):
        if self.done():
            return after[0]
        if self.step < 0:
            self.keep, send = add_first(self.me, self.groups, after)
        elif self.step < self.upper - 1:
            self.keep, send = add_halves(self.keep, self.flight, after)
        else:
            if self.step == self.upper - 1:
                self.keep = add(self.keep, self.flight, after)[0]
                if self.over_dp:
                    self.line = Line(self.keep, self.size, self.short, hold)
            else:
                self.keep = self.line.advance(after, hold)
            self.step += 1
            return self.keep
        self.step += 1
        self.flight = round_of(send, self.step, self.shards)
        return self.keep


class Line:
    def __init__(self, value, size, short=False, hold=False):
        self.value, self.size = value, size
        self.short = short or size != 4
        self.step = 0
        self.shared = False
        self.flight = None
        if not hold:
            self.start()

    def start(self):
        if self.short:
            pairs = [(i, i ^ (1 << self.step)) for i in range(self.size)]
        else:
            pairs = ([(0, 1), (3, 2)], [(1, 2), (2, 1)], [(1, 0), (2, 3)])[self.step]
        self.flight = lax.ppermute(self.value, "dp", pairs)

    def rounds(self):
        return self.size.bit_length() - 1 if self.short else 3

    def done(self):
        return self.step >= self.rounds()

    def advance(self, after, hold=False):
        if self.done():
            return after[0]
        if self.flight is None:
            self.start()
        if self.shared and self.step == 0:
            self.value = add_inner(inner_flag(), self.value, self.flight, after)
        elif self.short or self.step < 2:
            self.value = add(self.value, self.flight, after)
        else:
            self.value = pick(inner_flag(), self.value, self.flight, after)
        self.step += 1
        self.flight = None
        if not self.done() and not hold:
            self.start()
        return self.value


def inner_flag():
    return ((lax.axis_index("dp") + 1) // 2 % 2).astype(jnp.int32).reshape(1)


def share(ending, opening, after):
    lines = (ending.line, opening.line)
    if any(x is None or x.short for x in lines) or lines[0].step != 2 or lines[1].step != 0:
        return after[0]
    value = pick(inner_flag(), lines[0].value, lines[1].value, after)
    flight = lax.ppermute(value, "dp", [(0, 1), (1, 0), (2, 3), (3, 2)])
    for x in lines:
        x.flight, x.shared = flight, True
    return value


def pick_kernel(inner_ref, a_ref, b_ref, o_ref):
    @pl.when(inner_ref[0] == 1)
    def _():
        o_ref[...] = a_ref[...]

    @pl.when(inner_ref[0] == 0)
    def _():
        o_ref[...] = b_ref[...]


def add_inner_kernel(inner_ref, a_ref, b_ref, o_ref):
    @pl.when(inner_ref[0] == 1)
    def _():
        add_kernel(a_ref, b_ref, o_ref)

    @pl.when(inner_ref[0] == 0)
    def _():
        o_ref[...] = a_ref[...]


def add_inner(inner, a, b, after):
    size = 1 + 6 * np.prod(a.shape) * a.dtype.itemsize / 2**20
    return call(
        add_inner_kernel, "add_inner", 0.7, (inner, a, b), [SCALAR, whole_spec(a), whole_spec(b)], [a], [whole_spec(a)],
        after=after, vmem=size,
    )[0]


def pick(inner, a, b, after):
    size = 1 + 6 * np.prod(a.shape) * a.dtype.itemsize / 2**20
    return call(
        pick_kernel, "pick", 0.7, (inner, a, b), [SCALAR, whole_spec(a), whole_spec(b)], [a], [whole_spec(a)],
        after=after, vmem=size,
    )[0]


def unpack_ffn_kernel(sum_ref, up_ref, down_ref, *, shards):
    blocks = sum_ref.shape[0] // 2
    blk = up_ref.shape[0]
    for b in range(blocks):
        up = sum_ref[2 * b].astype(f32)
        for c in range(shards):
            up_ref[:, (c * blocks + b) * blk : (c * blocks + b + 1) * blk] = up[:, c * blk : (c + 1) * blk]
        down_ref[b * blk : (b + 1) * blk] = sum_ref[2 * b + 1].astype(f32)


def unpack_ffn(a, shards, after=()):
    count, blk, width = a.shape
    outs = [sds((blk, count // 2 * width), f32), sds((count // 2 * blk, width), f32)]
    return simple(functools.partial(unpack_ffn_kernel, shards=shards), "unpack_ffn", 1.5, (a,), outs, after)


def on_device(
    enc_input,
    segments,
    targets,
    enc_cot,
    dec_cot,
    enc_gains,
    enc_attn,
    enc_table,
    enc_up,
    enc_down,
    embed,
    dec_gains,
    dec_self,
    dec_cross,
    dec_table,
    dec_up,
    dec_down,
):
    rows, length, width = enc_input.shape
    steps = targets.shape[1]
    tokens = rows * steps
    shards = lax.axis_size("fsdp")
    blk = enc_attn.shape[1]
    own = embed.shape[0]
    index = lax.axis_index("fsdp").astype(jnp.int32)
    me = index.reshape(1)
    late = min(length, SERIES_MOST)
    flat = lambda a: a.reshape(-1, width)
    segc, segr = segments[:, :, None], segments[:, None, :]

    first = pack_first(me, enc_attn, enc_gains, dec_gains, enc_table, dec_table, targets, shards)
    a = Gather(first, shards, apart=True)
    b_block = pack_ffn(enc_up, enc_down, shards, (first,))
    mark = a.forward((b_block, a.two) if a.apart else (b_block,))
    while not a.done():
        mark = a.forward((mark,))
    b = Gather(gate(b_block, (mark,)), shards)
    c_block = pack_attn(dec_self, dec_cross, (b.held,))
    a_pieces = a.finish()
    found, ids = embed_rows(me, embed, a_pieces, tokens, (c_block,))
    e = Sum(me, [found], over_dp=False)
    mark = ids
    while not b.done():
        mark = b.forward((mark,))
    c = Gather(gate(c_block, (mark,)), shards)
    hidden, q, k, v, mix, w_attn, small = enc_attn_fwd(me, enc_input, segc, segr, a_pieces, (c.held,))
    b_pieces = b.finish((hidden,))
    mark = b_pieces[1]
    while not c.done():
        mark = c.forward((mark,))
    d = Gather(pack_ffn(dec_up, dec_down, shards, (mark,)), shards)
    mark = e.advance((d.held,))
    mark = gate(small, (mark,), 4)
    enc_out, w_ffn = enc_ffn_fwd(me, hidden, small, b_pieces, (mark,))
    c_pieces = c.finish((enc_out,))
    mark = c_pieces[1]
    while e.step < e.upper - 1:
        mark = e.advance((mark,))
    while not d.done():
        mark = d.forward((mark,))
    mark = gate(small, (mark,), 4)
    mark = e.advance((mark,))
    emb = e.keep
    enc_out = enc_out.reshape(rows, length, width)
    enc_late = flat(enc_out[:, length - late :])
    last = (segments == segments[:, -1:])[:, length - late :].astype(jnp.int32).reshape(1, -1)
    kept = dec_attn_fwd(emb, enc_late, last, small, c_pieces, me, rows, ())
    kept, w_dec = kept[:-1], kept[-1]
    d_pieces = d.finish((kept[-1],))
    mark = gate(small, (d_pieces[1],), 4)
    dec_out, grad_b, g_dffn = dec_ffn(me, kept[-1], small, flat(dec_cot), d_pieces, (mark,))

    def turn(mark, *sums):
        for r in sums:
            mark = r.advance((mark,))
        return mark

    r1 = Sum(me, [g_dffn])
    grad_late, grad_a, g_cross = dec_cross_bwd(grad_b, enc_late, last.reshape(-1, 1), small, w_dec, kept, rows, ())
    r2 = Sum(me, [g_cross])
    grad_rows, d_dtab, g_self = dec_self_bwd(grad_a, emb, small, w_dec, kept, rows, ())
    r2.include(g_self)
    mark = turn(grad_rows, r1)
    f = Gather(gate(grad_rows, (mark,)), shards)
    grad_memory, dn, g_half = enc_ffn_bwd_first(
        hidden, small, w_ffn, enc_cot, grad_late.reshape(rows, late, width), (f.held,)
    )
    r3 = Sum(me, [g_half])
    mark = turn(dn, r1, r2)
    while not f.done():
        mark = f.forward((mark,))
    grad_hidden, g_ffn = enc_ffn_bwd_next(hidden, small, w_ffn, grad_memory, dn, (mark,))
    r3.include(g_ffn)
    mark = turn(grad_hidden, r1, r2)
    f_pieces = f.finish((mark,))
    mark = gate(small, (f_pieces[1],), 8)
    mark = turn(mark, r3)
    g_embed = embed_grads(me, ids, f_pieces, own, (mark,))
    r5 = Line(g_embed, lax.axis_size("dp"))
    mark = g_embed
    parts = []
    for row in range(rows):
        parts.append(enc_attn_bwd(row, grad_hidden, q, k, v, segc, segr, w_attn, small, (mark,)))
        mark = parts[-1][3]
        if row == 0:
            mark = turn(mark, r1, r2, r5, r3)
    mark = r1.advance((mark,), hold=True)
    mark = turn(mark, r2)
    mark = r3.advance((mark,), hold=True)
    mark = share(r1, r3, (mark,))
    mark = turn(mark, r5)
    g_attn = enc_weight_grads(enc_input, small, mix, grad_hidden, d_dtab, parts, shards, (mark,))
    r6 = Sum(me, [g_attn])
    mark = gate(small, (g_attn,), 8)
    mark = turn(mark, r6, r3, r2)
    grad_input = enc_input_grad(enc_input, small, grad_hidden, w_attn, parts, (mark,))
    mark = turn(grad_input, r6, r1, r5, r3, r6, r6, r2, r6, r3, r6)
    for r in (r6, r1, r2, r3, r5):
        while not r.done():
            mark = r.advance((mark,))
    s_dup, s_ddown = unpack_ffn(r1.keep, shards)
    s_up, s_down = unpack_ffn(r3.keep, shards)
    s_attn = r6.keep.astype(f32)
    tabs = s_attn[4 * blk :]
    per = enc_table.shape[0]
    entries = lambda lane: lax.dynamic_slice(
        tabs[:HEADS, lane : lane + BUCKETS].reshape(-1), (index * per,), (per,)
    )
    s_attn = s_attn[: 4 * blk].reshape(4, blk, width)
    s_dec = r2.keep.astype(f32)

    def gain_grad(weights, sums, gain):
        axes = (0, 2) if weights.ndim == 3 else 1
        return jnp.sum(weights.astype(f32) * sums, axis=axes) / gain.astype(f32)

    return (
        enc_out,
        dec_out.reshape(rows, steps, width),
        grad_input,
        grad_memory,
        jnp.stack([gain_grad(enc_attn[:3], s_attn[:3], enc_gains[0]), gain_grad(enc_up, s_up, enc_gains[1])]),
        s_attn,
        entries(0),
        s_up,
        s_down,
        r5.value.astype(f32),
        jnp.stack(
            [
                gain_grad(dec_self[:3], s_dec[4:7], dec_gains[0]),
                gain_grad(dec_cross[0], s_dec[0], dec_gains[1]),
                gain_grad(dec_up, s_dup, dec_gains[2]),
            ]
        ),
        s_dec[4:],
        s_dec[:4],
        entries(DEC_LANE),
        s_dup,
        s_ddown,
    )


def solution(mesh):
    placed = (
        P(("fsdp", "dp"), None, None),
        P(("fsdp", "dp"), None),
        P(("fsdp", "dp"), None),
        P(("fsdp", "dp"), None, None),
        P(("fsdp", "dp"), None, None),
        P(None, "fsdp"),
        P(None, "fsdp", None),
        P("fsdp"),
        P("fsdp", None),
        P("fsdp", None),
        P("fsdp", None),
        P(None, "fsdp"),
        P(None, "fsdp", None),
        P(None, "fsdp", None),
        P("fsdp"),
        P("fsdp", None),
        P("fsdp", None),
    )
    return jax.shard_map(
        on_device,
        mesh=mesh,
        in_specs=placed,
        out_specs=(
            P(("fsdp", "dp"), None, None),
            P(("fsdp", "dp"), None, None),
            P(("fsdp", "dp"), None, None),
            P(("fsdp", "dp"), None, None),
            P(None, "fsdp"),
            P(None, "fsdp", None),
            P("fsdp"),
            P("fsdp", None),
            P("fsdp", None),
            P("fsdp", None),
            P(None, "fsdp"),
            P(None, "fsdp", None),
            P(None, "fsdp", None),
            P("fsdp"),
            P("fsdp", None),
            P("fsdp", None),
        ),
        check_vma=False,
    )
```

```python
import functools

import jax
import jax.numpy as jnp
import numpy as np
from jax import lax
from jax.experimental import pallas as pl
from jax.experimental.pallas import tpu as pltpu
from jax.sharding import PartitionSpec as P

HEADS = 8
HEAD_DIM = 64
BUCKETS = 32
SERIES_MOST = 256
TILE = 128
MASKED = -1000000000.0

epsilon = 1e-06
f32 = jnp.float32
bf16 = jnp.bfloat16
PEAK = 1.15e9

WEIGHT = 1

VMEM = {
    "pack_first": 4,
    "enc_attn_fwd": 24,
    "enc_ffn_fwd": 20,
    "enc_ffn_bwd": 24,
    "enc_attn_bwd": 24,
    "enc_weight_grads": 16,
    "enc_input_grad": 20,
    "embed_rows": 8,
    "embed_grads": 8,
    "dec_attn_fwd": 20,
    "dec_ffn": 16,
    "dec_cross_bwd": 20,
    "dec_self_bwd": 16,
}

TABLE_ROW = 0
GAIN_ROW = 8
ID_ROW = 13
SMALL_ROWS = 16
DEC_LANE = 128


def bucket_codes(length, both_ways):
    bucket_list = []
    for offset in range(-(length - 1), length):
        if both_ways:
            upper_half = 16 if offset > 0 else 0
            distance = abs(offset)
            if distance < 8:
                bucket = distance
            else:
                bucket = 8 + sum(
                    (1 for exponent in range(1, 8) if distance * distance >= 64 * 2**exponent)
                )
        else:
            upper_half = 0
            distance = max(-offset, 0)
            if distance < 16:
                bucket = distance
            else:
                bucket = 16 + sum(
                    (1 for exponent in range(1, 16) if distance**16 >= 16**16 * 2 ** (3 * exponent))
                )
        bucket_list.append(upper_half + bucket)
    return np.array(bucket_list, dtype=np.int32)


def offset_hot(length, both_ways, reverse):
    codes = np.concatenate([bucket_codes(length, both_ways), [-1]])
    if reverse:
        codes = codes[::-1]
    return jnp.asarray(codes[None, :] == np.arange(BUCKETS)[:, None], bf16)


def nn(a, b):
    return lax.dot_general(a, b, (((1,), (0,)), ((), ())), preferred_element_type=f32)


def nt(a, b):
    return lax.dot_general(a, b, (((1,), (1,)), ((), ())), preferred_element_type=f32)


def tn(a, b):
    return lax.dot_general(a, b, (((0,), (0,)), ((), ())), preferred_element_type=f32)


def rho_of(h):
    return lax.rsqrt(jnp.mean(h * h, axis=-1, keepdims=True) + epsilon)


def normed(h, gain):
    return (h * rho_of(h) * gain.astype(f32)).astype(bf16)


def norm_back(h, gain, dn):
    rho = rho_of(h)
    xh = h * rho
    gu = dn * gain.astype(f32)
    return rho * (gu - xh * jnp.mean(gu * xh, axis=-1, keepdims=True))


def gelu(u):
    t = jnp.tanh(np.float32(np.sqrt(2 / np.pi)) * (u + 0.044715 * (u * u * u)))
    return 0.5 * u * (1.0 + t)


def gelu_both(u):
    c = np.float32(np.sqrt(2 / np.pi))
    u2 = u * u
    t = jnp.tanh(c * (u + 0.044715 * (u2 * u)))
    cdf = 0.5 * (1.0 + t)
    return u * cdf, cdf + 0.5 * u * (1.0 - t * t) * (c + (3 * 0.044715 * c) * u2)


def matrix(ref, w):
    part = ref[:, w]
    return part.reshape(part.shape[0] * part.shape[1], part.shape[2])


def packed(value, shards):
    return value.reshape(shards, value.shape[0] // shards, value.shape[1]).astype(bf16)


def place(shard, me, shards):
    upper = shards.bit_length() - 2
    diff = shard ^ me
    spot = 0
    for j in range(upper):
        even = (diff >> (1 + j)) & 1
        odd = (diff >> (upper - j)) & 1
        spot = spot | (jnp.where((shard & 1) == 0, even, odd) << (upper - 1 - j))
    return spot


def shard_at(spot, me, shards):
    upper = shards.bit_length() - 2
    diff_even = diff_odd = 0
    for j in range(upper):
        bit = (spot >> (upper - 1 - j)) & 1
        diff_even = diff_even | (bit << (1 + j))
        diff_odd = diff_odd | (bit << (upper - j))
    return me ^ jnp.where((me & 1) == 0, diff_even, diff_odd)


def spread(refs):
    return [(ref, i) for ref in refs for i in range(ref.shape[0])]


def collect(out_ref, refs, me, rows=None):
    shards = out_ref.shape[0]
    count = len(refs) // 2
    for core, part in ((me, refs[:count]), (me ^ 1, refs[count:])):
        for p, (ref, i) in enumerate(spread(part)):
            piece = ref[i] if rows is None else ref[i, :rows]
            out_ref[shard_at(p, core, shards)] = piece.reshape(out_ref.shape[1:])


SCALAR = pl.BlockSpec(memory_space=pltpu.SMEM)
ANYWHERE = pl.BlockSpec(memory_space=pl.ANY)
sds = jax.ShapeDtypeStruct


def far(shape, dtype):
    return pltpu.HBM(shape, dtype)


def stay(arrays):
    return [pltpu.with_memory_space_constraint(a, pltpu.HBM) for a in arrays]


def whole_spec(a):
    zeros = (0,) * len(a.shape)
    return pl.BlockSpec(a.shape, lambda i: zeros)


def call(kernel, name, us, args, in_specs, outs, out_specs, scratch=(), grid=1, after=(), vmem=None, distant=()):
    waits = len(after)

    def body(*refs):
        kernel(*refs[waits:])

    return pl.pallas_call(
        body,
        grid=(grid,),
        in_specs=[ANYWHERE] * waits + list(in_specs),
        out_specs=list(out_specs),
        out_shape=[far(o.shape, o.dtype) if i in distant else sds(o.shape, o.dtype) for i, o in enumerate(outs)],
        scratch_shapes=list(scratch),
        compiler_params=pltpu.CompilerParams(vmem_limit_bytes=int(VMEM.get(name, vmem) * 2**20)),
        cost_estimate=pl.CostEstimate(flops=int(us * PEAK * (4 if us >= 3 else 0.3)), bytes_accessed=1024, transcendentals=0),
        name=name,
    )(*after, *args)


def simple(kernel, name, us, args, outs, after=(), scratch=(), vmem=None, distant=()):
    if vmem is None:
        vmem = 1 + sum(2 * np.prod(a.shape) * a.dtype.itemsize for a in (*args, *outs)) / 2**20
    return call(
        kernel, name, us, args, [whole_spec(a) for a in args], outs, [whole_spec(o) for o in outs], scratch,
        after=after, vmem=vmem, distant=distant,
    )


def half(lane, value, which):
    return jnp.where((lane // HEAD_DIM) == which, value, jnp.zeros_like(value))


def fill_strip(strip_ref, table, hot, shift):
    vec = nn(table, hot)
    width = hot.shape[1]
    rows = strip_ref.shape[1]
    for h in range(HEADS):
        row = jnp.broadcast_to(vec[h : h + 1], (rows, width))
        strip_ref[h] = pltpu.roll(row, (width + shift) % width, 1, stride=1, stride_axis=0)


def strip_sums(acc, hot):
    rows, width = acc.shape[1], acc.shape[2]
    total = jnp.zeros((HEADS, 8, width), f32)
    for g in range(rows // 8):
        part = acc[:, g * 8 : g * 8 + 8, :].reshape(HEADS * 8, width)
        if g:
            part = pltpu.roll(part, width - 8 * g, 1)
        total = total + part.reshape(HEADS, 8, width)
    flat = total.reshape(HEADS * 8, width)
    sub = lax.broadcasted_iota(jnp.int32, flat.shape, 0) % 8
    for b in range(3):
        flat = jnp.where((sub >> b) & 1 == 1, pltpu.roll(flat, width - (1 << b), 1), flat)
    diag = pltpu.roll(jnp.sum(flat.reshape(HEADS, 8, width), axis=1), rows, 1)
    return lax.dot_general(
        diag,
        hot.astype(f32),
        (((1,), (1,)), ((), ())),
        precision=lax.Precision.HIGHEST,
        preferred_element_type=f32,
    )


def soft_rows(s):
    e = jnp.exp(s - jnp.max(s, axis=-1, keepdims=True))
    return e * (1.0 / jnp.sum(e, axis=-1, keepdims=True))


def soft_columns(s):
    e = jnp.exp(s - jnp.max(s, axis=0, keepdims=True))
    return e * (1.0 / jnp.sum(e, axis=0, keepdims=True))


def pack_first_kernel(me_ref, attn_ref, eg_ref, dg_ref, et_ref, dt_ref, tok_ref, out_ref, *, shards):
    count, blk, width = attn_ref.shape
    me = me_ref[0]
    out_ref[: count * blk] = attn_ref[...].reshape(count * blk, width)
    base = count * blk
    lane = lax.broadcasted_iota(jnp.int32, (1, width), 1)
    here = (lane // blk) == me
    per = et_ref.shape[1]
    row8 = lax.broadcasted_iota(jnp.int32, (HEADS, BUCKETS), 0)
    lane8 = lax.broadcasted_iota(jnp.int32, (HEADS, BUCKETS), 1)
    held = (row8 * BUCKETS + lane8) // per == me
    small = jnp.zeros((SMALL_ROWS, width), f32)
    rows = lax.broadcasted_iota(jnp.int32, (SMALL_ROWS, width), 0)
    gains = [eg_ref[i : i + 1] for i in range(eg_ref.shape[0])] + [dg_ref[i : i + 1] for i in range(dg_ref.shape[0])]
    for i, g in enumerate(gains):
        wide = jnp.where(here, jnp.concatenate([g.astype(f32)] * shards, axis=1), 0.0)
        small = jnp.where(rows == GAIN_ROW + i, jnp.broadcast_to(wide, small.shape), small)
    tok = tok_ref[...]
    steps = tok.shape[1]
    first = lax.broadcasted_iota(jnp.int32, tok.shape, 1) == 0
    shifted = jnp.where(first, 0, pltpu.roll(tok, 1, 1) if steps % 128 == 0 else jnp.concatenate([tok[:, -1:], tok[:, :-1]], axis=1))
    parts = [(shifted[r : r + 1] >> 6).astype(f32) for r in range(tok.shape[0])]
    parts += [(shifted[r : r + 1] & 63).astype(f32) for r in range(tok.shape[0])]
    ids = jnp.concatenate(parts, axis=1)
    ids = jnp.concatenate([ids, jnp.zeros((1, width - ids.shape[1]), f32)], axis=1)
    small = jnp.where(rows == ID_ROW, jnp.broadcast_to(ids, small.shape), small)
    out_ref[base:] = small.astype(bf16)
    for t_ref, at in ((et_ref, 0), (dt_ref, DEC_LANE)):
        table = jnp.concatenate([t_ref[...].astype(f32)] * (BUCKETS // per), axis=1)
        table = jnp.where(held, jnp.broadcast_to(table, held.shape), 0.0)
        out_ref[base : base + HEADS, at : at + BUCKETS] = table.astype(bf16)


def pack_first(me, attn, enc_gains, dec_gains, enc_table, dec_table, targets, shards):
    count, blk, width = attn.shape
    out = sds((1, count * blk + SMALL_ROWS, width), bf16)
    args = stay((attn, enc_gains, dec_gains, enc_table.reshape(1, -1), dec_table.reshape(1, -1), targets))

    def body(me_ref, *refs):
        pack_first_kernel(me_ref, *refs[:-1], refs[-1].at[0], shards=shards)

    return call(
        body, "pack_first", 2, (me, *args), [SCALAR] + [whole_spec(a) for a in args], [out], [whole_spec(out)]
    )[0]


def pack_ffn_kernel(up_ref, down_ref, out_ref, *, shards):
    blocks = out_ref.shape[0] // 2
    blk = up_ref.shape[0]
    for b in range(blocks):
        parts = [up_ref[:, (c * blocks + b) * blk : (c * blocks + b + 1) * blk] for c in range(shards)]
        out_ref[2 * b] = jnp.concatenate(parts, axis=1)
        out_ref[2 * b + 1] = down_ref[b * blk : (b + 1) * blk]


def pack_ffn(up, down, shards, after):
    blk, width = up.shape[0], down.shape[1]
    out = sds((1, 2 * up.shape[1] // width, blk, width), bf16)

    def body(up_ref, down_ref, out_ref):
        pack_ffn_kernel(up_ref, down_ref, out_ref.at[0], shards=shards)

    return simple(body, "pack_ffn", 1, stay((up, down)), [out], after)[0]


def pack_attn_kernel(a_ref, b_ref, out_ref):
    count = a_ref.shape[0]
    out_ref[0, :count] = a_ref[...]
    out_ref[0, count:] = b_ref[...]


def pack_attn(a, b, after):
    out = sds((1, 2 * a.shape[0]) + a.shape[1:], bf16)
    return simple(pack_attn_kernel, "pack_attn", 1, stay((a, b)), [out], after)[0]


def gate_kernel(a_ref, o_ref):
    o_ref[...] = a_ref[...]


def gate(a, after, us=0.5):
    return simple(gate_kernel, "gate", us, (a,), [a], after)[0]


def join_kernel(a_ref, b_ref, o_ref):
    size = a_ref.shape[0]
    o_ref[:size] = a_ref[...]
    o_ref[size:] = b_ref[...]


def join(a, b, after):
    return simple(join_kernel, "join", 1, (a, b), [sds((2 * a.shape[0],) + a.shape[1:], a.dtype)], after)[0]


def add_first_kernel(me_ref, *refs):
    *parts, keep_ref, send_ref = refs
    quarter = keep_ref.shape[0]
    shards = 4 * quarter
    at = 0
    for a_ref, b_ref in zip(parts[::2], parts[1::2]):
        size = a_ref.shape[1]
        for p in range(2 * quarter):
            s = shard_at(p, me_ref[0], shards)
            out_ref = keep_ref if p < quarter else send_ref
            total = a_ref[s].astype(f32) + b_ref[s].astype(f32)
            out_ref[p % quarter, at : at + size] = total.astype(bf16)
        at += size


def add_first(me, pairs, after, us=2):
    shards = pairs[0][0].shape[0]
    args = [a for pair in pairs for a in pair]
    size = sum(grads.shape[1] for grads, _ in pairs)
    out = sds((shards // 4, size) + pairs[0][0].shape[2:], bf16)
    limit = 1 + 2 * sum(np.prod(a.shape) * 2 for a in args) / 2**20
    return call(
        add_first_kernel, "add_first", us, (me, *args), [SCALAR] + [whole_spec(a) for a in args],
        [out] * 2, [whole_spec(out)] * 2, after=after, vmem=limit,
    )


def add_halves_kernel(a_ref, b_ref, keep_ref, send_ref):
    mid = keep_ref.shape[0]
    keep_ref[...] = (a_ref[:mid].astype(f32) + b_ref[:mid].astype(f32)).astype(bf16)
    send_ref[...] = (a_ref[mid:].astype(f32) + b_ref[mid:].astype(f32)).astype(bf16)


def add_halves(a, b, after):
    out = sds((a.shape[0] // 2,) + a.shape[1:], bf16)
    return simple(add_halves_kernel, "add_halves", 1, (a, b), [out] * 2, after)


def add_kernel(a_ref, b_ref, o_ref):
    o_ref[...] = (a_ref[...].astype(f32) + b_ref[...].astype(f32)).astype(o_ref.dtype)


def add(a, b, after, dtype=bf16):
    return simple(add_kernel, "add", 0.7, (a, b), [sds(a.shape, dtype)], after)[0]


def enc_attn_fwd_kernel(me_ref, x_ref, segc_ref, segr_ref, hot_ref, *refs):
    pieces, (hid_ref, q_ref, k_ref, v_ref, mix_ref, w_ref, small_ref, strip_ref) = refs[:-8], refs[-8:]
    rows, length, _ = x_ref.shape
    blocks = length // TILE
    own = pieces[0].shape[1] - SMALL_ROWS
    collect(w_ref, pieces, me_ref[0], own)
    small = jnp.zeros(small_ref.shape, f32)
    for ref, i in spread(pieces):
        small = small + ref[i, own:].astype(f32)
    small_ref[...] = small
    table = small[TABLE_ROW : TABLE_ROW + HEADS, :BUCKETS].astype(bf16)
    fill_strip(strip_ref, table, hot_ref[...], 1 - TILE)
    lane = lax.broadcasted_iota(jnp.int32, (length, 2 * HEAD_DIM), 1)

    @pl.loop(0, rows)
    def _(r):
        here = pl.ds(r * length, length)
        x = x_ref[r].astype(f32)
        n = normed(x, small_ref[GAIN_ROW : GAIN_ROW + 1])
        q_ref[r] = nn(n, matrix(w_ref, 0)).astype(bf16)
        k_ref[r] = nn(n, matrix(w_ref, 1)).astype(bf16)
        v_ref[r] = nn(n, matrix(w_ref, 2)).astype(bf16)
        same = segc_ref[r] == segr_ref[r]
        for hp in range(HEADS // 2):
            ls = slice(hp * 2 * HEAD_DIM, (hp + 1) * 2 * HEAD_DIM)
            qp, kp, vp = q_ref[r, :, ls], k_ref[r, :, ls], v_ref[r, :, ls]
            outs = []
            for sub in range(2):
                s = nt(half(lane, qp, sub), kp)
                starts = [(blocks - 1 - b) * TILE for b in range(blocks)]
                bias = [strip_ref[hp * 2 + sub, :, c : c + length] for c in starts]
                s = jnp.where(same, s + jnp.concatenate(bias, axis=0), MASKED)
                outs.append(nn(soft_rows(s).astype(bf16), vp))
            mix_ref[here, ls] = jnp.where(lane < HEAD_DIM, outs[0], outs[1]).astype(bf16)
        hid_ref[here] = x + nn(mix_ref[here], matrix(w_ref, 3))


def enc_attn_fwd(me, x, segc, segr, pieces, after):
    rows, length, width = x.shape
    shards = sum(p.shape[0] for p in pieces)
    hot = offset_hot(length, True, False)
    flat = (rows * length, width)
    outs = [sds(flat, f32)] + [sds(x.shape, bf16)] * 3 + [sds(flat, bf16)]
    outs += [sds((shards, 4, width // shards, width), bf16), sds((SMALL_ROWS, width), f32)]
    args = [me, x, segc, segr, hot] + list(pieces)
    return call(
        enc_attn_fwd_kernel, "enc_attn_fwd", 14, args, [SCALAR] + [whole_spec(a) for a in args[1:]],
        outs, [whole_spec(o) for o in outs], [pltpu.VMEM((HEADS, TILE, 2 * length), f32)], after=after,
    )


def enc_ffn_fwd_kernel(me_ref, h_ref, small_ref, *refs):
    pieces, (o_ref, w_ref, acc_s) = refs[:-3], refs[-3:]
    collect(w_ref, pieces, me_ref[0])
    n = normed(h_ref[...], small_ref[GAIN_ROW + 1 : GAIN_ROW + 2])
    for i in range(w_ref.shape[1] // 2):
        a = gelu(nn(n, matrix(w_ref, 2 * i))).astype(bf16)
        acc_s[...] = (h_ref[...] if i == 0 else acc_s[...]) + nn(a, matrix(w_ref, 2 * i + 1))
    o_ref[...] = acc_s[...].astype(bf16)


def enc_ffn_fwd(me, h, small, pieces, after):
    outs = [sds(h.shape, bf16), sds((sum(p.shape[0] for p in pieces),) + pieces[0].shape[1:], bf16)]
    args = (me, h, small, *pieces)
    return call(
        enc_ffn_fwd_kernel, "enc_ffn_fwd", 9, args, [SCALAR] + [whole_spec(a) for a in args[1:]],
        outs, [whole_spec(o) for o in outs], [pltpu.VMEM(h.shape, f32)], after=after,
    )


def ffn_step(n, gb, w_ref, dw_ref, at=0, to=0):
    shards = w_ref.shape[0]
    wu, wd = matrix(w_ref, at), matrix(w_ref, at + 1)
    a, slope = gelu_both(nn(n, wu))
    a = a.astype(bf16)
    dw_ref[:, to + 1] = packed(tn(a, gb), shards)
    du = (slope * nt(gb, wd)).astype(bf16)
    dw_ref[:, to] = packed(tn(n, du), shards)
    return a, wd, nt(du, wu)


def enc_ffn_bwd_first_kernel(h_ref, small_ref, w_ref, cot_ref, gm_ref, gmem_ref, dn_ref, dw_ref, gb_s):
    rows, length, width = cot_ref.shape
    late = gm_ref.shape[1]
    n = normed(h_ref[...], small_ref[GAIN_ROW + 1 : GAIN_ROW + 2])
    for r in range(rows):
        gmem_ref[r, : length - late] = cot_ref[r, : length - late].astype(f32)
        gmem_ref[r, length - late :] = cot_ref[r, length - late :].astype(f32) + gm_ref[r]
        gb_s[r * length : (r + 1) * length] = gmem_ref[r].astype(bf16)
    gb = gb_s[...]
    for i in range(dw_ref.shape[1] // 2):
        dn = ffn_step(n, gb, w_ref, dw_ref, 2 * i, 2 * i)[2]
        dn_ref[...] = dn if i == 0 else dn_ref[...] + dn


def enc_ffn_bwd_next_kernel(h_ref, small_ref, w_ref, gmem_ref, dn_ref, gh_ref, dw_ref, dn_s):
    rows, length, width = gmem_ref.shape
    gain = small_ref[GAIN_ROW + 1 : GAIN_ROW + 2]
    n = normed(h_ref[...], gain)
    gmem = gmem_ref[...].reshape(rows * length, width)
    gb = gmem.astype(bf16)
    count = dw_ref.shape[1]
    for i in range(count // 2):
        dn = ffn_step(n, gb, w_ref, dw_ref, w_ref.shape[1] - count + 2 * i, 2 * i)[2]
        dn_s[...] = (dn_ref[...] if i == 0 else dn_s[...]) + dn
    gh_ref[...] = gmem + norm_back(h_ref[...], gain, dn_s[...])


def enc_ffn_bwd_first(h, small, weights, cot, late_grad, after):
    grads = sds((weights.shape[0], weights.shape[1] // 2) + weights.shape[2:], bf16)
    args = (h, small, weights, cot, late_grad)
    outs = [sds(cot.shape, f32), sds(h.shape, f32), grads]
    return simple(enc_ffn_bwd_first_kernel, "enc_ffn_bwd", 10, args, outs, after, [pltpu.VMEM(h.shape, bf16)])


def enc_ffn_bwd_next(h, small, weights, gmem, dn, after):
    grads = sds((weights.shape[0], weights.shape[1] // 2) + weights.shape[2:], bf16)
    args = (h, small, weights, gmem, dn)
    outs = [sds(h.shape, f32), grads]
    return simple(enc_ffn_bwd_next_kernel, "enc_ffn_bwd", 10, args, outs, after, [pltpu.VMEM(h.shape, f32)])


def enc_attn_bwd_kernel(
    gh_ref, q_ref, k_ref, v_ref, segc_ref, segr_ref, w_ref, small_ref, hot_ref,
    dq_ref, dk_ref, dv_ref, dt_ref, strip_ref, acc_ref, do_s, *, r,
):
    length = q_ref.shape[1]
    blocks = length // TILE
    table = small_ref[TABLE_ROW : TABLE_ROW + HEADS, :BUCKETS].astype(bf16)
    fill_strip(strip_ref, table, hot_ref[...], -TILE)
    acc_ref[...] = jnp.zeros_like(acc_ref)
    gb = gh_ref[r * length : (r + 1) * length].astype(bf16)
    do_s[...] = nt(gb, matrix(w_ref, 3)).astype(bf16)
    lane = lax.broadcasted_iota(jnp.int32, (length, 2 * HEAD_DIM), 1)
    same = segc_ref[r] == segr_ref[r]
    for hp in range(HEADS // 2):
        ls = slice(hp * 2 * HEAD_DIM, (hp + 1) * 2 * HEAD_DIM)
        qp, kp, vp, dop = q_ref[r, :, ls], k_ref[r, :, ls], v_ref[r, :, ls], do_s[:, ls]
        dq = dk = dv = None
        for sub in range(2):
            h = hp * 2 + sub
            qm, km, dom = half(lane, qp, sub), half(lane, kp, sub), half(lane, dop, sub)
            s = nt(kp, qm)
            starts = [(blocks - 1 - b) * TILE for b in range(blocks)]
            bias = [strip_ref[h, :, c : c + length] for c in starts]
            p = soft_columns(jnp.where(same, s + jnp.concatenate(bias, axis=0), MASKED))
            dp = nt(vp, dom)
            ds = (p * (dp - jnp.sum(dp * p, axis=0, keepdims=True))).astype(bf16)
            new = (tn(ds, km), nn(ds, qm), nn(p.astype(bf16), dom))
            dq, dk, dv = new if dq is None else (dq + new[0], dk + new[1], dv + new[2])
            wide = ds.astype(f32)
            for b, c in enumerate(starts):
                acc_ref[h, :, c : c + length] += wide[b * TILE : (b + 1) * TILE]
        dq_ref[0, :, ls] = dq.astype(bf16)
        dk_ref[0, :, ls] = dk.astype(bf16)
        dv_ref[0, :, ls] = dv.astype(bf16)
    dt_ref[...] = strip_sums(acc_ref[...], hot_ref[...])


def enc_attn_bwd(r, grad_hidden, q, k, v, segc, segr, weights, small, after):
    rows, length, width = q.shape
    strip = pltpu.VMEM((HEADS, TILE, 2 * length), f32)
    args = (grad_hidden, q, k, v, segc, segr, weights, small, offset_hot(length, True, True))
    outs = [sds((1, length, width), bf16)] * 3 + [sds((HEADS, BUCKETS), f32)]
    return simple(
        functools.partial(enc_attn_bwd_kernel, r=r), "enc_attn_bwd", 10, args, outs, after,
        [strip, strip, pltpu.VMEM((length, width), bf16)],
    )


def enc_weight_grads_kernel(x_ref, small_ref, mix_ref, gh_ref, td_ref, *refs):
    *parts, dw_ref = refs
    rows, length, width = x_ref.shape
    shards = dw_ref.shape[0]
    blk = width // shards
    gain = small_ref[GAIN_ROW : GAIN_ROW + 1]
    n = normed(x_ref[...].astype(f32).reshape(rows * length, width), gain)
    for w in range(3):
        total = None
        for r in range(rows):
            new = tn(n[r * length : (r + 1) * length], parts[4 * r + w][0])
            total = new if total is None else total + new
        dw_ref[:, w * blk : (w + 1) * blk] = packed(total, shards)
    dw_ref[:, 3 * blk : 4 * blk] = packed(tn(mix_ref[...], gh_ref[...].astype(bf16)), shards)
    table = sum(parts[4 * r + 3][...] for r in range(rows))
    for s in range(shards):
        dw_ref[s, 4 * blk :] = jnp.zeros((SMALL_ROWS, width), bf16)
        dw_ref[s, 4 * blk : 4 * blk + HEADS, :BUCKETS] = table.astype(bf16)
        dw_ref[s, 4 * blk : 4 * blk + HEADS, DEC_LANE : DEC_LANE + BUCKETS] = td_ref[...].astype(bf16)


def enc_weight_grads(x, small, mix, grad_hidden, dec_grad, parts, shards, after):
    width = x.shape[-1]
    grads = sds((shards, 4 * width // shards + SMALL_ROWS, width), bf16)
    args = (x, small, mix, grad_hidden, dec_grad) + tuple(a for row in parts for a in row)
    return simple(enc_weight_grads_kernel, "enc_weight_grads", 3, args, [grads], after)[0]


def enc_input_grad_kernel(x_ref, small_ref, gh_ref, w_ref, *refs):
    *parts, gi_ref = refs
    rows, length, width = x_ref.shape
    gain = small_ref[GAIN_ROW : GAIN_ROW + 1]
    for r in range(rows):
        dn = sum(nt(parts[4 * r + w][0], matrix(w_ref, w)) for w in range(3))
        gi_ref[r] = gh_ref[r * length : (r + 1) * length] + norm_back(x_ref[r].astype(f32), gain, dn)


def enc_input_grad(x, small, grad_hidden, weights, parts, after):
    args = (x, small, grad_hidden, weights, *(a for row in parts for a in row))
    return simple(enc_input_grad_kernel, "enc_input_grad", 4, args, [sds(x.shape, f32)], after)[0]


def embed_rows_kernel(me_ref, embed_ref, *refs):
    pieces, (found_ref, ids_ref) = refs[:-2], refs[-2:]
    shards, tokens, _ = found_ref.shape
    own = embed_ref.shape[0]
    me = me_ref[0]
    count = len(pieces) // 2
    row = pieces[0].shape[1] - SMALL_ROWS + ID_ROW
    for core, part in ((me, pieces[:count]), (me ^ 1, pieces[count:])):
        for p, (ref, i) in enumerate(spread(part)):
            code = ref[i, row : row + 1, :].astype(f32).astype(jnp.int32)
            ids = code[:, :tokens] * 64 + code[:, tokens : 2 * tokens]
            s = shard_at(p, core, shards)
            ids_ref[s] = ids
            found_ref[s] = tn(one_hot(ids, own, me), embed_ref[...]).astype(bf16)


def sum_rows_kernel(a_ref, o_ref):
    total = a_ref[0].astype(f32)
    for s in range(1, a_ref.shape[0]):
        total = total + a_ref[s].astype(f32)
    o_ref[...] = total.astype(bf16)


def sum_rows(a, after):
    return simple(sum_rows_kernel, "sum_rows", 0.7, (a,), [sds(a.shape[1:], bf16)], after)[0]


def one_hot(ids, own, me):
    return (lax.broadcasted_iota(jnp.int32, (own, ids.shape[1]), 0) + me * own == ids).astype(f32).astype(bf16)


def embed_rows(me, embed, pieces, tokens, after):
    shards = sum(p.shape[0] for p in pieces)
    outs = [sds((shards, tokens, embed.shape[1]), bf16), sds((shards, 1, tokens), jnp.int32)]
    args = (embed, *pieces)
    return call(
        embed_rows_kernel, "embed_rows", 2, (me,) + args, [SCALAR] + [whole_spec(a) for a in args], outs,
        [whole_spec(o) for o in outs], after=after,
    )


def embed_grads_kernel(me_ref, ids_ref, *refs):
    pieces, out_ref = refs[:-1], refs[-1]
    shards = ids_ref.shape[0]
    me = me_ref[0]
    count = len(pieces) // 2
    total = jnp.zeros(out_ref.shape, f32)
    for core, part in ((me, pieces[:count]), (me ^ 1, pieces[count:])):
        for p, (ref, i) in enumerate(spread(part)):
            ids = ids_ref[shard_at(p, core, shards)]
            total = total + nn(one_hot(ids, out_ref.shape[0], me), ref[i])
    out_ref[...] = total.astype(bf16)


def embed_grads(me, ids, pieces, own, after):
    out = sds((own, pieces[0].shape[-1]), bf16)
    args = (ids, *pieces)
    return call(
        embed_grads_kernel, "embed_grads", 2, (me,) + args, [SCALAR] + [whole_spec(a) for a in args], [out],
        [whole_spec(out)], after=after,
    )[0]


def dec_masks(rows, steps, late, last_ref, key_major):
    tokens, keys = rows * steps, rows * late
    shape = (tokens, tokens)
    i = lax.broadcasted_iota(jnp.int32, shape, 1 if key_major else 0)
    j = lax.broadcasted_iota(jnp.int32, shape, 0 if key_major else 1)
    causal = (i // steps == j // steps) & (j <= i)
    shape = (keys, tokens) if key_major else (tokens, keys)
    i = lax.broadcasted_iota(jnp.int32, shape, 1 if key_major else 0)
    j = lax.broadcasted_iota(jnp.int32, shape, 0 if key_major else 1)
    return causal, (i // steps == j // late) & (last_ref[...] == 1)


def dec_table(small_ref):
    return small_ref[TABLE_ROW : TABLE_ROW + HEADS, DEC_LANE : DEC_LANE + BUCKETS].astype(bf16)


def dec_attn_fwd_kernel(
    emb_ref, enc_ref, last_ref, small_ref, w_ref, hot_ref,
    na_ref, qkv_ref, mixa_ref, hida_ref, nb_ref, cq_ref, ckv_ref, mixb_ref, hidb_ref, strip_ref, *, rows,
):
    tokens = emb_ref.shape[0]
    keys = enc_ref.shape[0]
    causal, allowed = dec_masks(rows, tokens // rows, keys // rows, last_ref, False)
    fill_strip(strip_ref, dec_table(small_ref), hot_ref[...], 1 - tokens)
    lane = lax.broadcasted_iota(jnp.int32, (tokens, 2 * HEAD_DIM), 1)

    def attend(q_at, k_at, v_at, bias_at, mask, mix_ref):
        for hp in range(HEADS // 2):
            ls = slice(hp * 2 * HEAD_DIM, (hp + 1) * 2 * HEAD_DIM)
            qp, kp, vp = q_at(ls), k_at(ls), v_at(ls)
            outs = []
            for sub in range(2):
                s = nt(half(lane, qp, sub), kp)
                if bias_at is not None:
                    s = s + bias_at(hp * 2 + sub)
                outs.append(nn(soft_rows(jnp.where(mask, s, MASKED)).astype(bf16), vp))
            mix_ref[:, ls] = jnp.where(lane < HEAD_DIM, outs[0], outs[1]).astype(bf16)

    emb = emb_ref[...].astype(f32)
    na_ref[...] = normed(emb, small_ref[GAIN_ROW + 2 : GAIN_ROW + 3])
    for w in range(3):
        qkv_ref[w] = nn(na_ref[...], matrix(w_ref, w)).astype(bf16)
    attend(
        lambda ls: qkv_ref[0, :, ls],
        lambda ls: qkv_ref[1, :, ls],
        lambda ls: qkv_ref[2, :, ls],
        lambda h: strip_ref[h, :, :tokens],
        causal,
        mixa_ref,
    )
    hida_ref[...] = emb + nn(mixa_ref[...], matrix(w_ref, 3))
    nb_ref[...] = normed(hida_ref[...], small_ref[GAIN_ROW + 3 : GAIN_ROW + 4])
    cq_ref[...] = nn(nb_ref[...], matrix(w_ref, 4)).astype(bf16)
    for w in range(2):
        ckv_ref[w] = nn(enc_ref[...], matrix(w_ref, 5 + w)).astype(bf16)
    attend(
        lambda ls: cq_ref[:, ls],
        lambda ls: ckv_ref[0, :, ls],
        lambda ls: ckv_ref[1, :, ls],
        None,
        allowed,
        mixb_ref,
    )
    hidb_ref[...] = hida_ref[...] + nn(mixb_ref[...], matrix(w_ref, 7))


def dec_attn_fwd(emb, enc_late, last, small, pieces, me, rows, after):
    tokens, width = emb.shape
    keys = enc_late.shape[0]
    hot = dec_hot(tokens, tokens // rows, False)
    one = sds((tokens, width), bf16)
    wide = sds((tokens, width), f32)
    full = sds((sum(p.shape[0] for p in pieces),) + pieces[0].shape[1:], bf16)
    outs = [one, sds((3, tokens, width), bf16), one, wide, one, one, sds((2, keys, width), bf16), one, wide, full]
    args = (emb, enc_late, last, small, hot, *pieces)

    def body(me_ref, emb_ref, enc_ref, last_ref, small_ref, hot_ref, *refs):
        parts, kept, w_ref, strip_ref = refs[: len(pieces)], refs[len(pieces) : -2], refs[-2], refs[-1]
        collect(w_ref, parts, me_ref[0])
        dec_attn_fwd_kernel(
            emb_ref, enc_ref, last_ref, small_ref, w_ref, hot_ref, *kept, strip_ref, rows=rows
        )

    return call(
        body, "dec_attn_fwd", 7, (me,) + args, [SCALAR] + [whole_spec(a) for a in args], outs,
        [whole_spec(o) for o in outs], [pltpu.VMEM((HEADS, tokens, 2 * tokens), f32)], after=after,
    )


def dec_hot(tokens, steps, reverse):
    codes = np.full(2 * tokens, -1, np.int32)
    own = bucket_codes(steps, False)
    codes[tokens - steps : tokens - steps + len(own)] = own
    if reverse:
        codes = codes[::-1]
    return jnp.asarray(codes[None, :] == np.arange(BUCKETS)[:, None], bf16)


def dec_ffn_kernel(me_ref, h_ref, small_ref, cot_ref, *refs):
    pieces, (out_ref, gh_ref, dw_ref, w_s, dn_s, o_s) = refs[:-6], refs[-6:]
    gain = small_ref[GAIN_ROW + 4 : GAIN_ROW + 5]
    collect(w_s, pieces, me_ref[0])
    n = normed(h_ref[...], gain)
    gb = cot_ref[...]
    for i in range(w_s.shape[1] // 2):
        a, wd, dn = ffn_step(n, gb, w_s, dw_ref, 2 * i, 2 * i)
        o_s[...] = (h_ref[...] if i == 0 else o_s[...]) + nn(a, wd)
        dn_s[...] = dn if i == 0 else dn_s[...] + dn
    out_ref[...] = o_s[...].astype(bf16)
    gh_ref[...] = gb.astype(f32) + norm_back(h_ref[...], gain, dn_s[...])


def dec_ffn(me, h, small, cot, pieces, after):
    grads = sds((sum(p.shape[0] for p in pieces),) + pieces[0].shape[1:], bf16)
    outs = [sds(h.shape, bf16), sds(h.shape, f32), grads]
    args = (me, h, small, cot, *pieces)
    return call(
        dec_ffn_kernel, "dec_ffn", 8, args, [SCALAR] + [whole_spec(a) for a in args[1:]],
        outs, [whole_spec(o) for o in outs],
        [pltpu.VMEM(grads.shape, bf16), pltpu.VMEM(h.shape, f32), pltpu.VMEM(h.shape, f32)], after=after,
    )


def attend_back(q_at, k_at, v_at, do, bias_at, mask, take_score, dq_s, dk_s, dv_s):
    for hp in range(HEADS // 2):
        ls = slice(hp * 2 * HEAD_DIM, (hp + 1) * 2 * HEAD_DIM)
        qp, kp, vp, dop = q_at(ls), k_at(ls), v_at(ls), do[:, ls]
        lane = lax.broadcasted_iota(jnp.int32, qp.shape, 1)
        lanek = lax.broadcasted_iota(jnp.int32, kp.shape, 1)
        dq = dk = dv = None
        for sub in range(2):
            qm, km, dom = half(lane, qp, sub), half(lanek, kp, sub), half(lane, dop, sub)
            s = nt(kp, qm)
            if bias_at is not None:
                s = s + bias_at(hp * 2 + sub)
            p = soft_columns(jnp.where(mask, s, MASKED))
            dp = nt(vp, dom)
            ds = (p * (dp - jnp.sum(dp * p, axis=0, keepdims=True))).astype(bf16)
            new = (tn(ds, km), nn(ds, qm), nn(p.astype(bf16), dom))
            dq, dk, dv = new if dq is None else (dq + new[0], dk + new[1], dv + new[2])
            if take_score is not None:
                take_score(hp * 2 + sub, ds)
        dq_s[:, ls] = dq.astype(bf16)
        dk_s[:, ls] = dk.astype(bf16)
        dv_s[:, ls] = dv.astype(bf16)


def dec_cross_bwd_kernel(
    gb_ref, enc_ref, last_ref, small_ref, w_ref, hida_ref, nb_ref, cq_ref, ckv_ref, mixb_ref,
    gm_ref, ga_ref, dw_ref, dq_s, dk_s, dv_s, *, rows,
):
    tokens = gb_ref.shape[0]
    keys = enc_ref.shape[0]
    shards = dw_ref.shape[0]
    _, allowed = dec_masks(rows, tokens // rows, keys // rows, last_ref, True)
    grad_b = gb_ref[...]
    branch = grad_b.astype(bf16)
    dw_ref[:, 3] = packed(tn(mixb_ref[...], branch), shards)
    do = nt(branch, matrix(w_ref, 7)).astype(bf16)
    attend_back(
        lambda ls: cq_ref[:, ls],
        lambda ls: ckv_ref[0, :, ls],
        lambda ls: ckv_ref[1, :, ls],
        do,
        None,
        allowed,
        None,
        dq_s,
        dk_s,
        dv_s,
    )
    gm_ref[...] = nt(dk_s[...], matrix(w_ref, 5)) + nt(dv_s[...], matrix(w_ref, 6))
    dw_ref[:, 0] = packed(tn(nb_ref[...], dq_s[...]), shards)
    dw_ref[:, 1] = packed(tn(enc_ref[...], dk_s[...]), shards)
    dw_ref[:, 2] = packed(tn(enc_ref[...], dv_s[...]), shards)
    gain = small_ref[GAIN_ROW + 3 : GAIN_ROW + 4]
    ga_ref[...] = grad_b + norm_back(hida_ref[...], gain, nt(dq_s[...], matrix(w_ref, 4)))


def dec_cross_bwd(grad_b, enc_late, last, small, weights, kept, rows, after):
    tokens, width = grad_b.shape
    keys = enc_late.shape[0]
    _, _, _, hida, nb, cq, ckv, mixb, _ = kept
    shards, _, blk, _ = weights.shape
    outs = [sds((keys, width), f32), sds((tokens, width), f32), sds((shards, 4, blk, width), bf16)]
    args = (grad_b, enc_late, last, small, weights, hida, nb, cq, ckv, mixb)
    return simple(
        functools.partial(dec_cross_bwd_kernel, rows=rows), "dec_cross_bwd", 6, args, outs, after,
        [pltpu.VMEM((tokens, width), bf16), pltpu.VMEM((keys, width), bf16), pltpu.VMEM((keys, width), bf16)],
    )


def dec_self_bwd_kernel(
    ga_ref, emb_ref, small_ref, w_ref, hot_ref, na_ref, qkv_ref, mixa_ref,
    gr_ref, dt_ref, dw_ref, strip_ref, acc_ref, dq_s, dk_s, dv_s, *, rows,
):
    tokens = emb_ref.shape[0]
    shards = dw_ref.shape[0]
    steps = tokens // rows
    i = lax.broadcasted_iota(jnp.int32, (tokens, tokens), 1)
    j = lax.broadcasted_iota(jnp.int32, (tokens, tokens), 0)
    causal = (i // steps == j // steps) & (j <= i)
    fill_strip(strip_ref, dec_table(small_ref), hot_ref[...], -tokens)
    grad_a = ga_ref[...]
    branch = grad_a.astype(bf16)
    dw_ref[:, 3] = packed(tn(mixa_ref[...], branch), shards)
    do = nt(branch, matrix(w_ref, 3)).astype(bf16)
    acc_ref[...] = jnp.zeros_like(acc_ref)

    def take_score(h, ds):
        acc_ref[h, :, :tokens] = ds.astype(f32)

    attend_back(
        lambda ls: qkv_ref[0, :, ls],
        lambda ls: qkv_ref[1, :, ls],
        lambda ls: qkv_ref[2, :, ls],
        do,
        lambda h: strip_ref[h, :, :tokens],
        causal,
        take_score,
        dq_s,
        dk_s,
        dv_s,
    )
    parts = (dq_s[...], dk_s[...], dv_s[...])
    dn = nt(parts[0], matrix(w_ref, 0)) + nt(parts[1], matrix(w_ref, 1)) + nt(parts[2], matrix(w_ref, 2))
    for w in range(3):
        dw_ref[:, w] = packed(tn(na_ref[...], parts[w]), shards)
    gain = small_ref[GAIN_ROW + 2 : GAIN_ROW + 3]
    gr_ref[0] = (grad_a + norm_back(emb_ref[...].astype(f32), gain, dn)).astype(bf16)
    dt_ref[...] = strip_sums(acc_ref[...], hot_ref[...])


def dec_self_bwd(grad_a, emb, small, weights, kept, rows, after):
    tokens, width = emb.shape
    shards, _, blk, _ = weights.shape
    na, qkv, mixa = kept[:3]
    hot = dec_hot(tokens, tokens // rows, True)
    outs = [sds((1, tokens, width), bf16), sds((HEADS, BUCKETS), f32), sds((shards, 4, blk, width), bf16)]
    args = (grad_a, emb, small, weights, hot, na, qkv, mixa)
    strip = pltpu.VMEM((HEADS, tokens, 2 * tokens), f32)
    return simple(
        functools.partial(dec_self_bwd_kernel, rows=rows), "dec_self_bwd", 4, args, outs, after,
        [strip, strip] + [pltpu.VMEM((tokens, width), bf16)] * 3,
    )


def exchange(value, shards, even_bit, odd_bit):
    pairs = [(i, i ^ (1 << (odd_bit if i & 1 else even_bit))) for i in range(shards)]
    return lax.ppermute(value, "fsdp", pairs)


def swap_cores(value, shards):
    return exchange(value, shards, 0, 0)


def round_of(value, j, shards):
    upper = shards.bit_length() - 2
    return exchange(value, shards, 1 + j, upper - j)


class Gather:
    def __init__(self, block, shards, apart=False):
        self.shards = shards
        self.upper = shards.bit_length() - 2
        self.held = block
        self.apart = apart and self.upper == 2
        if self.apart:
            self.one, self.two = round_of(block, 0, shards), round_of(block, 1, shards)
            self.swapped = [swap_cores(block, shards)]
        else:
            self.step = self.upper - 1
            self.flight = round_of(block, self.step, shards)

    def forward(self, after):
        if self.apart:
            passed = gate(self.one, after)
            self.far = round_of(passed, 1, self.shards)
            self.pieces = [self.held, self.two, passed, self.far]
            self.swapped += [swap_cores(p, self.shards) for p in self.pieces[1:3]]
            return passed
        self.held = join(self.held, self.flight, after)
        self.step -= 1
        self.flight = round_of(self.held, self.step, self.shards)
        if self.step == 0:
            self.pieces = [self.held, self.flight]
            self.swapped = [swap_cores(self.held, self.shards)]
        return self.held

    def done(self):
        return hasattr(self, "pieces")

    def finish(self, after=None):
        if after is not None:
            self.pieces[-1] = gate(self.pieces[-1], after)
        return self.pieces + self.swapped + [swap_cores(self.pieces[-1], self.shards)]


class Sum:
    def __init__(self, me, groups, over_dp=True, short=False):
        self.me, self.shards, self.short, self.line = me, groups[0].shape[0], short, None
        self.over_dp = over_dp
        self.groups = [(g, swap_cores(g, self.shards)) for g in groups]
        self.upper = self.shards.bit_length() - 2
        self.size = lax.axis_size("dp")
        self.step = -1

    def include(self, group):
        self.groups.append((group, swap_cores(group, self.shards)))

    def done(self):
        if not self.over_dp:
            return self.step >= self.upper
        return self.line is not None and self.line.done()

    def advance(self, after, hold=False):
        if self.done():
            return after[0]
        if 0 <= self.step < self.upper and self.flight is None:
            self.flight = round_of(self.send, self.step, self.shards)
        if self.step < 0:
            self.keep, send = add_first(self.me, self.groups, after)
        elif self.step < self.upper - 1:
            self.keep, send = add_halves(self.keep, self.flight, after)
        else:
            if self.step == self.upper - 1:
                self.keep = add(self.keep, self.flight, after)[0]
                if self.over_dp:
                    self.line = Line(self.keep, self.size, self.short, hold)
            else:
                self.keep = self.line.advance(after, hold)
            self.step += 1
            return self.keep
        self.step += 1
        self.send = send
        self.flight = None if hold else round_of(send, self.step, self.shards)
        return self.keep

    def release(self, after):
        passed = gate(self.send, after)
        self.flight = round_of(passed, self.step, self.shards)
        return passed


class Line:
    def __init__(self, value, size, short=False, hold=False):
        self.value, self.size = value, size
        self.short = short or size != 4
        self.step = 0
        self.shared = False
        self.flight = None
        if not hold:
            self.start()

    def start(self):
        if self.short:
            pairs = [(i, i ^ (1 << self.step)) for i in range(self.size)]
        else:
            pairs = ([(0, 1), (3, 2)], [(1, 2), (2, 1)], [(1, 0), (2, 3)])[self.step]
        self.flight = lax.ppermute(self.value, "dp", pairs)

    def rounds(self):
        return self.size.bit_length() - 1 if self.short else 3

    def done(self):
        return self.step >= self.rounds()

    def advance(self, after, hold=False):
        if self.done():
            return after[0]
        if self.flight is None:
            self.start()
        if self.shared and self.step == 0:
            self.value = add_inner(inner_flag(), self.value, self.flight, after)
        elif self.short or self.step < 2:
            self.value = add(self.value, self.flight, after)
        else:
            self.value = pick(inner_flag(), self.value, self.flight, after)
        self.step += 1
        self.flight = None
        if not self.done() and not hold:
            self.start()
        return self.value


def inner_flag():
    return ((lax.axis_index("dp") + 1) // 2 % 2).astype(jnp.int32).reshape(1)


def share(ending, opening, after):
    lines = (ending.line, opening.line)
    if any(x is None or x.short for x in lines) or lines[0].step != 2 or lines[1].step != 0:
        return after[0]
    value = pick(inner_flag(), lines[0].value, lines[1].value, after)
    flight = lax.ppermute(value, "dp", [(0, 1), (1, 0), (2, 3), (3, 2)])
    for x in lines:
        x.flight, x.shared = flight, True
    return value


def pick_kernel(inner_ref, a_ref, b_ref, o_ref):
    @pl.when(inner_ref[0] == 1)
    def _():
        o_ref[...] = a_ref[...]

    @pl.when(inner_ref[0] == 0)
    def _():
        o_ref[...] = b_ref[...]


def add_inner_kernel(inner_ref, a_ref, b_ref, o_ref):
    @pl.when(inner_ref[0] == 1)
    def _():
        add_kernel(a_ref, b_ref, o_ref)

    @pl.when(inner_ref[0] == 0)
    def _():
        o_ref[...] = a_ref[...]


def add_inner(inner, a, b, after):
    size = 1 + 6 * np.prod(a.shape) * a.dtype.itemsize / 2**20
    return call(
        add_inner_kernel, "add_inner", 0.7, (inner, a, b), [SCALAR, whole_spec(a), whole_spec(b)], [a], [whole_spec(a)],
        after=after, vmem=size,
    )[0]


def pick(inner, a, b, after):
    size = 1 + 6 * np.prod(a.shape) * a.dtype.itemsize / 2**20
    return call(
        pick_kernel, "pick", 0.7, (inner, a, b), [SCALAR, whole_spec(a), whole_spec(b)], [a], [whole_spec(a)],
        after=after, vmem=size,
    )[0]


def unpack_ffn_kernel(sum_ref, up_ref, down_ref, *, shards):
    blocks = sum_ref.shape[0] // 2
    blk = up_ref.shape[0]
    for b in range(blocks):
        up = sum_ref[2 * b].astype(f32)
        for c in range(shards):
            up_ref[:, (c * blocks + b) * blk : (c * blocks + b + 1) * blk] = up[:, c * blk : (c + 1) * blk]
        down_ref[b * blk : (b + 1) * blk] = sum_ref[2 * b + 1].astype(f32)


def unpack_ffn(a, shards, after=()):
    count, blk, width = a.shape
    outs = [sds((blk, count // 2 * width), f32), sds((count // 2 * blk, width), f32)]
    return simple(functools.partial(unpack_ffn_kernel, shards=shards), "unpack_ffn", 1.5, (a,), outs, after)


def on_device(
    enc_input,
    segments,
    targets,
    enc_cot,
    dec_cot,
    enc_gains,
    enc_attn,
    enc_table,
    enc_up,
    enc_down,
    embed,
    dec_gains,
    dec_self,
    dec_cross,
    dec_table,
    dec_up,
    dec_down,
):
    rows, length, width = enc_input.shape
    steps = targets.shape[1]
    tokens = rows * steps
    shards = lax.axis_size("fsdp")
    blk = enc_attn.shape[1]
    own = embed.shape[0]
    index = lax.axis_index("fsdp").astype(jnp.int32)
    me = index.reshape(1)
    late = min(length, SERIES_MOST)
    flat = lambda a: a.reshape(-1, width)
    segc, segr = segments[:, :, None], segments[:, None, :]

    first = pack_first(me, enc_attn, enc_gains, dec_gains, enc_table, dec_table, targets, shards)
    a = Gather(first, shards, apart=True)
    b_block = pack_ffn(enc_up, enc_down, shards, (first,))
    mark = a.forward((b_block, a.two) if a.apart else (b_block,))
    while not a.done():
        mark = a.forward((mark,))
    b = Gather(gate(b_block, (mark,)), shards)
    c_block = pack_attn(dec_self, dec_cross, (b.held,))
    a_pieces = a.finish()
    found, ids = embed_rows(me, embed, a_pieces, tokens, (c_block,))
    e = Sum(me, [found], over_dp=False)
    mark = ids
    while not b.done():
        mark = b.forward((mark,))
    c = Gather(gate(c_block, (mark,)), shards)
    hidden, q, k, v, mix, w_attn, small = enc_attn_fwd(me, enc_input, segc, segr, a_pieces, (c.held,))
    b_pieces = b.finish((hidden,))
    mark = b_pieces[1]
    while not c.done():
        mark = c.forward((mark,))
    d = Gather(pack_ffn(dec_up, dec_down, shards, (mark,)), shards)
    mark = e.advance((d.held,))
    mark = gate(small, (mark,), 4)
    enc_out, w_ffn = enc_ffn_fwd(me, hidden, small, b_pieces, (mark,))
    mark = enc_out
    while not d.done():
        mark = d.forward((mark,))
    c_pieces = c.finish((mark,))
    mark = c_pieces[1]
    while e.step < e.upper - 1:
        mark = e.advance((mark,))
    mark = gate(small, (mark,), 4)
    mark = e.advance((mark,))
    emb = e.keep
    enc_out = enc_out.reshape(rows, length, width)
    enc_late = flat(enc_out[:, length - late :])
    last = (segments == segments[:, -1:])[:, length - late :].astype(jnp.int32).reshape(1, -1)
    kept = dec_attn_fwd(emb, enc_late, last, small, c_pieces, me, rows, ())
    kept, w_dec = kept[:-1], kept[-1]
    d_pieces = d.finish((kept[-1],))
    mark = gate(small, (d_pieces[1],), 4)
    dec_out, grad_b, g_dffn = dec_ffn(me, kept[-1], small, flat(dec_cot), d_pieces, (mark,))

    def turn(mark, *sums):
        for r in sums:
            mark = r.advance((mark,))
        return mark

    r1 = Sum(me, [g_dffn])
    grad_late, grad_a, g_cross = dec_cross_bwd(grad_b, enc_late, last.reshape(-1, 1), small, w_dec, kept, rows, ())
    r2 = Sum(me, [g_cross])
    grad_rows, d_dtab, g_self = dec_self_bwd(grad_a, emb, small, w_dec, kept, rows, ())
    r2.include(g_self)
    mark = turn(grad_rows, r1)
    f = Gather(gate(grad_rows, (mark,)), shards)
    grad_memory, dn, g_half = enc_ffn_bwd_first(
        hidden, small, w_ffn, enc_cot, grad_late.reshape(rows, late, width), (f.held,)
    )
    r3 = Sum(me, [g_half])
    mark = r2.advance((turn(dn, r1),), hold=True)
    while not f.done():
        mark = f.forward((mark,))
    grad_hidden, g_ffn = enc_ffn_bwd_next(hidden, small, w_ffn, grad_memory, dn, (mark,))
    r3.include(g_ffn)
    mark = r2.release((turn(grad_hidden, r1),))
    f_pieces = f.finish((mark,))
    mark = gate(small, (f_pieces[1],), 8)
    mark = turn(mark, r3)
    g_embed = embed_grads(me, ids, f_pieces, own, (mark,))
    r5 = Line(g_embed, lax.axis_size("dp"))
    mark = g_embed
    parts = []
    for row in range(rows):
        parts.append(enc_attn_bwd(row, grad_hidden, q, k, v, segc, segr, w_attn, small, (mark,)))
        mark = parts[-1][3]
        if row == 0:
            mark = turn(mark, r1, r5, r2, r3)
    mark = r1.advance((mark,), hold=True)
    mark = r2.advance((mark,), hold=True)
    mark = share(r1, r2, (mark,))
    mark = turn(mark, r3, r5)
    g_attn = enc_weight_grads(enc_input, small, mix, grad_hidden, d_dtab, parts, shards, (mark,))
    r6 = Sum(me, [g_attn])
    mark = gate(small, (g_attn,), 8)
    mark = turn(mark, r6, r2)
    grad_input = enc_input_grad(enc_input, small, grad_hidden, w_attn, parts, (mark,))
    mark = turn(grad_input, r3, r6, r1, r5, r2, r6, r3, r6, r2, r6, r3, r6)
    for r in (r6, r1, r2, r3, r5):
        while not r.done():
            mark = r.advance((mark,))
    s_dup, s_ddown = unpack_ffn(r1.keep, shards)
    s_up, s_down = unpack_ffn(r3.keep, shards)
    s_attn = r6.keep.astype(f32)
    tabs = s_attn[4 * blk :]
    per = enc_table.shape[0]
    entries = lambda lane: lax.dynamic_slice(
        tabs[:HEADS, lane : lane + BUCKETS].reshape(-1), (index * per,), (per,)
    )
    s_attn = s_attn[: 4 * blk].reshape(4, blk, width)
    s_dec = r2.keep.astype(f32)

    def gain_grad(weights, sums, gain):
        axes = (0, 2) if weights.ndim == 3 else 1
        return jnp.sum(weights.astype(f32) * sums, axis=axes) / gain.astype(f32)

    return (
        enc_out,
        dec_out.reshape(rows, steps, width),
        grad_input,
        grad_memory,
        jnp.stack([gain_grad(enc_attn[:3], s_attn[:3], enc_gains[0]), gain_grad(enc_up, s_up, enc_gains[1])]),
        s_attn,
        entries(0),
        s_up,
        s_down,
        r5.value.astype(f32),
        jnp.stack(
            [
                gain_grad(dec_self[:3], s_dec[4:7], dec_gains[0]),
                gain_grad(dec_cross[0], s_dec[0], dec_gains[1]),
                gain_grad(dec_up, s_dup, dec_gains[2]),
            ]
        ),
        s_dec[4:],
        s_dec[:4],
        entries(DEC_LANE),
        s_dup,
        s_ddown,
    )


def solution(mesh):
    placed = (
        P(("fsdp", "dp"), None, None),
        P(("fsdp", "dp"), None),
        P(("fsdp", "dp"), None),
        P(("fsdp", "dp"), None, None),
        P(("fsdp", "dp"), None, None),
        P(None, "fsdp"),
        P(None, "fsdp", None),
        P("fsdp"),
        P("fsdp", None),
        P("fsdp", None),
        P("fsdp", None),
        P(None, "fsdp"),
        P(None, "fsdp", None),
        P(None, "fsdp", None),
        P("fsdp"),
        P("fsdp", None),
        P("fsdp", None),
    )
    return jax.shard_map(
        on_device,
        mesh=mesh,
        in_specs=placed,
        out_specs=(
            P(("fsdp", "dp"), None, None),
            P(("fsdp", "dp"), None, None),
            P(("fsdp", "dp"), None, None),
            P(("fsdp", "dp"), None, None),
            P(None, "fsdp"),
            P(None, "fsdp", None),
            P("fsdp"),
            P("fsdp", None),
            P("fsdp", None),
            P("fsdp", None),
            P(None, "fsdp"),
            P(None, "fsdp", None),
            P(None, "fsdp", None),
            P("fsdp"),
            P("fsdp", None),
            P("fsdp", None),
        ),
        check_vma=False,
    )
```
